256 devices in a mesh: ctx: 32 (over z_hi, y, core), tp: 8 (over z_lo, x).
Axes of the slice: x: 4, y: 4, z: 8 (z_hi: 4, z_lo: 2; z = z_hi * 2 + z_lo), core: 2. Of those that a mesh axis runs over, the one named last changes fastest.
Arguments:
- tokens: bfloat16 [10240, 6144], P('ctx', 'tp'), may hold values from -6 to 6
- norm_gain_vector: bfloat16 [6144], P('tp'), may hold values from 0.099609375 to 1.8984375
- keys: bfloat16 [10240, 3072], P('ctx', 'tp'), may hold values from -67 to 67
- values: bfloat16 [10240, 3072], P('ctx', 'tp'), may hold values from -6 to 6
- query_frozen_weight: bfloat16 [6144, 3072], P(None, 'tp'), may hold values from -0.078125 to 0.078125
- output_frozen_weight: bfloat16 [3072, 6144], P('tp'), may hold values from -2 to 2
- query_update_first: bfloat16 [32, 6144, 64], P('ctx'), may hold values from -0.078125 to 0.078125
- query_update_second: bfloat16 [32, 64, 3072], P('ctx', None, 'tp'), may hold values from -0.75 to 0.75
- output_update_first: bfloat16 [32, 3072, 64], P('ctx', 'tp'), may hold values from -0.109375 to 0.109375
- output_update_second: bfloat16 [32, 64, 6144], P('ctx'), may hold values from -6 to 6
- owners: int32 [4], replicated, may hold values from 0 to 31
- frame_block_number: int32 [160], replicated, may hold values from 0 to 39, never falling along the last dimension, each value on 1 to 8 neighbouring positions
Outputs:
- mixed: bfloat16 [10240, 6144], P('ctx', 'tp')
The draws below stay inside these ranges and needn't reach their ends.
Inputs may be any that keep to these rules, and one draw needn't show every extreme that they name: `frame_block_number`: never falls along the frames; every block holds 1 to 8 frames, one exactly 8.
All inputs are finite; a program needn't handle non-finite values.
Results may differ from the reference program's by a relative error of at most 0.02.
The reference program's roundings to bfloat16 on the way count: a program that leaves them out, or rounds other values in their place, can miss the bound.
Values may be sent and summed in bfloat16 or wider, within the bound.
No kernel may reach another device: no remote copies, remote signals or barrier semaphores. Data moves between devices by JAX's collectives and lax.ppermute only.
A program may use at most 128 MiB of HBM per device.

```python
import math
import jax
import jax.numpy as jnp
import numpy as np
from jax import lax

MODEL_WIDTH = 6144
HEADS = 24
HS = 128
LOWRANK_SIZE = 64
FTOK = 64
SEQ = 10240
QUERY_FEATURES = 3072
FRAMES = 160
N_CTX = 32


def draw_keys(key, part):
    key = jax.random.fold_in(key, 11)
    first_key, second_key = jax.random.split(key, 2)
    leading = jnp.clip(jax.random.normal(first_key, (SEQ // 2, QUERY_FEATURES), jnp.float32), -4.0, 4.0)
    partner = jnp.clip(jax.random.normal(second_key, (SEQ // 2, QUERY_FEATURES), jnp.float32), -4.0, 4.0)
    paired = jnp.stack([leading, leading + 0.3 * partner], axis=1)
    return paired.reshape(SEQ, QUERY_FEATURES).astype(jnp.bfloat16)


def with_ends(values, key, low, largest):
    longest = values.shape.index(max(values.shape))
    spots = []
    for shift in (0, 1):
        where = [jax.random.randint(jax.random.fold_in(key, axis), (), 0, length) for axis, length in enumerate(values.shape)]
        where[longest] = (where[longest] + shift) % values.shape[longest]
        spots.append(tuple(where))
    return values.at[spots[0]].set(low).at[spots[1]].set(largest)


def levels(own_key, shape, shards, smallest, top_value):
    level = 1.0
    for position, shards_of in shards:
        draws = jax.random.uniform(jax.random.fold_in(jax.random.fold_in(own_key, 6), position), (shards_of,), jnp.float32, smallest / len(shards), top_value / len(shards))
        level = level * jnp.repeat(jnp.exp(draws), shape[position] // shards_of).reshape((-1,) + (1,) * (len(shape) - 1 - position))
    return level


def length_profile(count, total, most, slope):
    portions = [(1 << 20) // math.isqrt(grade ** slope) + 1 for grade in range(2, count + 1)]
    rest, counts = total - most - (count - 1), [1] * (count - 1)
    while rest > 0:
        movable = [i for i in range(count - 1) if counts[i] < most]
        pool, budget = sum([portions[i] for i in movable]), rest
        for i in movable:
            addition = min(most - counts[i], max(1, budget * portions[i] // pool), rest)
            counts[i] = counts[i] + addition
            rest = rest - addition
    return np.array([most] + counts)


def ragged_sizes(key, count, total, limit, slope):
    if count == 2:
        one = jax.random.randint(key, (), max(1, total - limit), min(limit, total - 1) + 1)
        return jnp.stack([one, total - one])
    tallies = jnp.asarray(length_profile(count, total, limit, slope), jnp.int32)
    couples = (count - 1) // 2
    donor, receiver = tallies[1:1 + 2 * couples:2], tallies[2:2 + 2 * couples:2]
    slack = jnp.minimum(donor - 1, limit - receiver)
    shifted = jax.random.randint(jax.random.fold_in(key, 1), (couples,), 0, 1 << 20) % (slack + 1)
    tallies = tallies.at[1:1 + 2 * couples:2].set(donor - shifted).at[2:2 + 2 * couples:2].set(receiver + shifted)
    return tallies[jax.random.permutation(jax.random.fold_in(key, 2), count)]


def centred(rng, extent, width, reach, cuts=(), dtype=jnp.bfloat16):
    entries = width * jax.random.normal(rng, extent, jnp.float32)
    if cuts:
        entries = entries * levels(rng, extent, cuts, -0.22, 0.18)
    return jnp.clip(entries, -reach, reach).astype(dtype)


def setup_inputs(seed: int = 0) -> dict:
    key_of = jax.random.split(jax.random.key(seed), 13)
    tokens = centred(key_of[0], (SEQ, MODEL_WIDTH), 1.0, 6.0, ((0, 32), (1, 8)))
    norm_gain_vector = jnp.clip(1.0 + 0.18 * jax.random.normal(key_of[1], (MODEL_WIDTH,), jnp.float32), 0.099609375, 1.8984375).astype(jnp.bfloat16)
    keys = draw_keys(jax.random.fold_in(key_of[12], 71), 0)
    values = centred(key_of[3], (SEQ, QUERY_FEATURES), 1.0, 6.0, ((0, 32), (1, 8)))
    query_frozen_weight = centred(key_of[4], (MODEL_WIDTH, QUERY_FEATURES), MODEL_WIDTH ** -0.5, 0.078125, ((1, 8),))
    output_frozen_weight = centred(key_of[5], (QUERY_FEATURES, MODEL_WIDTH), 8 ** -0.5, 2.0, ((0, 8),))
    query_update_first = centred(key_of[6], (N_CTX, MODEL_WIDTH, LOWRANK_SIZE), MODEL_WIDTH ** -0.5, 0.078125, ((0, 32),))
    query_update_second = centred(key_of[7], (N_CTX, LOWRANK_SIZE, QUERY_FEATURES), LOWRANK_SIZE ** -0.5, 0.75, ((0, 32), (2, 8)))
    output_update_first = centred(key_of[8], (N_CTX, QUERY_FEATURES, LOWRANK_SIZE), QUERY_FEATURES ** -0.5, 0.109375, ((0, 32), (1, 8)))
    output_update_second = centred(key_of[9], (N_CTX, LOWRANK_SIZE, MODEL_WIDTH), 1 ** -0.5, 6.0, ((0, 32),))
    owners = with_ends(jax.random.randint(key_of[10], (4,), 0, N_CTX), jax.random.fold_in(key_of[10], 1), 0, N_CTX - 1).astype(jnp.int32)
    frame_block_number = jnp.searchsorted(jnp.cumsum(ragged_sizes(key_of[11], FRAMES // 4, FRAMES, 8, 1)), jnp.arange(FRAMES), side="right").astype(jnp.int32)
    return dict(tokens=tokens, norm_gain_vector=norm_gain_vector, keys=keys, values=values, query_frozen_weight=query_frozen_weight, output_frozen_weight=output_frozen_weight, query_update_first=query_update_first, query_update_second=query_update_second, output_update_first=output_update_first, output_update_second=output_update_second, owners=owners, frame_block_number=frame_block_number)


norm_eps = 1e-06
masked_score = -1e+30

def reference(tokens, norm_gain_vector, keys, values, query_frozen_weight, output_frozen_weight, query_update_first, query_update_second, output_update_first, output_update_second, owners, frame_block_number):
    features = tokens.astype(jnp.float32)
    mean_square = lax.optimization_barrier(jnp.mean(features * features, axis=-1, keepdims=True))
    normed = (features * lax.rsqrt(mean_square + norm_eps) * norm_gain_vector.astype(jnp.float32)).astype(jnp.bfloat16)
    query_down_factor = lax.dynamic_index_in_dim(query_update_first, owners[0], 0, keepdims=False)
    query_up_factor = lax.dynamic_index_in_dim(query_update_second, owners[1], 0, keepdims=False)
    output_down_factor = lax.dynamic_index_in_dim(output_update_first, owners[2], 0, keepdims=False)
    output_up_factor = lax.dynamic_index_in_dim(output_update_second, owners[3], 0, keepdims=False)
    query_merged = (query_frozen_weight.astype(jnp.float32) + jnp.dot(query_down_factor, query_up_factor, preferred_element_type=jnp.float32)).astype(jnp.bfloat16)
    out_merged = (output_frozen_weight.astype(jnp.float32) + jnp.dot(output_down_factor, output_up_factor, preferred_element_type=jnp.float32)).astype(jnp.bfloat16)
    queries = jnp.dot(normed, query_merged, preferred_element_type=jnp.float32).astype(jnp.bfloat16)
    token_block = jnp.repeat(frame_block_number, FTOK, total_repeat_length=SEQ)
    visible = token_block[None, :] <= token_block[:, None]

    def per_head(operands):
        head_queries, head_keys, head_values = operands
        scores = jnp.dot(head_queries, head_keys.T, preferred_element_type=jnp.float32) * HS ** (-0.5)
        scores = jnp.where(visible, scores, masked_score)
        top = lax.optimization_barrier(jnp.max(scores, axis=-1, keepdims=True))
        weights = jnp.where(visible, jnp.exp(scores - top), 0.0)
        total = lax.optimization_barrier(jnp.sum(weights, axis=-1, keepdims=True))
        summed = jnp.dot(weights.astype(jnp.bfloat16), head_values, preferred_element_type=jnp.float32)
        return summed / total

    def split_heads(matrix):
        return matrix.reshape(SEQ, HEADS, HS).transpose(1, 0, 2)
    attended = lax.map(per_head, (split_heads(queries), split_heads(keys), split_heads(values)))
    attended = attended.transpose(1, 0, 2).reshape(SEQ, QUERY_FEATURES).astype(jnp.bfloat16)
    return jnp.dot(attended, out_merged, preferred_element_type=jnp.float32).astype(jnp.bfloat16)
```

```python
import functools
import math

import jax
import jax.numpy as jnp
from jax import lax
from jax.experimental import pallas as pl
from jax.experimental.pallas import tpu as pltpu
from jax.sharding import Mesh
from jax.sharding import PartitionSpec as P

HS = 128
FTOK = 64
ROWS = 320
FRAMES_DEV = 5
WIDTH = 768
RANK = 64
HEADS_DEV = 3
QCOLS = HEADS_DEV * HS
CHUNK = 2 * ROWS
CHUNKS = 4
NEG = -1e30
EPS = 1e-6
AXES = ("zh", "y", "c", "zl", "x")
SIZES = {"zh": 4, "y": 4, "c": 2, "zl": 2, "x": 4}
CTX = ("zh", "y", "c")
TP = ("zl", "x")
EXP_SCALE = (HS ** (-0.5)) * math.log2(math.e)
BF = jnp.bfloat16
F32 = jnp.float32


def shift(v, axis, step):
    n = SIZES[axis]
    return lax.ppermute(v, axis, [(i, (i + step) % n) for i in range(n)])


def tp_shift(v, a, d):
    pairs = []
    for z in range(2):
        for x in range(4):
            pairs.append((z * 4 + x, (z ^ a) * 4 + (x + d) % 4))
    return lax.ppermute(v, TP, pairs)


def tp_source(a, d):
    return (lax.axis_index("zl") ^ a) * 4 + (lax.axis_index("x") - d) % 4


def vmem_call(body, out_shape, n_smem, n_vmem, scratch=(), flops=0, nbytes=0):
    return pl.pallas_call(
        body,
        out_shape=out_shape,
        in_specs=[pl.BlockSpec(memory_space=pltpu.SMEM)] * n_smem
        + [pl.BlockSpec(memory_space=pltpu.VMEM)] * n_vmem,
        scratch_shapes=list(scratch),
        cost_estimate=pl.CostEstimate(flops=flops, bytes_accessed=nbytes, transcendentals=0),
        compiler_params=pltpu.CompilerParams(vmem_limit_bytes=48 * 1024 * 1024),
    )


def tdot(a, b):
    return lax.dot_general(a, b, (((0,), (0,)), ((), ())), preferred_element_type=F32)


def query_kernel(order_ref, *refs):
    parts = refs[:8]
    lora = refs[8:16]
    w_ref, up_ref, out_ref = refs[16:]

    total = jnp.zeros((ROWS, 1), F32)
    for i in range(8):
        v = parts[i][...].astype(F32)
        total = total + jnp.sum(v * v, axis=1, keepdims=True)
    inv = lax.rsqrt(total * (1.0 / (8 * WIDTH)) + EPS)
    acc = jnp.zeros((ROWS, QCOLS), F32)
    up = up_ref[...]
    for i in range(8):
        rows = pl.ds(pl.multiple_of(order_ref[i] * WIDTH, WIDTH), WIDTH)
        piece = lora[i]
        gain = piece[RANK : RANK + 1, :].astype(F32)
        normed = (parts[i][...].astype(F32) * inv * gain).astype(BF)
        merged = (w_ref[rows, :].astype(F32) + tdot(piece[:RANK, :], up)).astype(BF)
        acc = acc + jnp.dot(normed, merged, preferred_element_type=F32)
    out_ref[...] = acc.astype(BF)


def attention_kernel(n, qframe_ref, kframe_ref, vis_ref, *refs):
    q_refs = refs[:n]
    kv_ref = refs[n]
    o_refs = refs[n + 1 : 2 * n + 1]
    m_ref, l_ref, acc_ref = refs[2 * n + 1 :]
    j = pl.program_id(0)

    @pl.when(j == 0)
    def _():
        m_ref[...] = jnp.full_like(m_ref, NEG)
        l_ref[...] = jnp.zeros_like(l_ref)
        acc_ref[...] = jnp.zeros_like(acc_ref)

    key_start = kframe_ref[j] * FTOK

    def heads(b, limit):
        for h in range(HEADS_DEV):
            cols = slice(h * HS, (h + 1) * HS)
            q = q_refs[b][:, cols]
            k = kv_ref[0, :, cols]
            v = kv_ref[0, :, QCOLS + h * HS : QCOLS + (h + 1) * HS]
            s = lax.dot_general(q, k, (((1,), (1,)), ((), ())), preferred_element_type=F32)
            if limit is not None:
                seen = lax.broadcasted_iota(jnp.int32, (ROWS, CHUNK), 1) < limit
                s = jnp.where(seen, s, NEG)
            slot = b * HEADS_DEV + h
            m_old = m_ref[slot][:, :1]
            m_new = jnp.maximum(m_old, jnp.max(s, axis=1, keepdims=True))
            p = jnp.exp2((s - m_new) * EXP_SCALE)
            if limit is not None:
                p = jnp.where(seen, p, 0.0)
            alpha = jnp.exp2((m_old - m_new) * EXP_SCALE)
            l_new = l_ref[slot][:, :1] * alpha + jnp.sum(p, axis=1, keepdims=True)
            m_ref[slot] = jnp.broadcast_to(m_new, (ROWS, HS))
            l_ref[slot] = jnp.broadcast_to(l_new, (ROWS, HS))
            acc_ref[slot] = acc_ref[slot] * alpha + jnp.dot(
                p.astype(BF), v, preferred_element_type=F32
            )

    for b in range(n):
        first = qframe_ref[b]
        ends = [vis_ref[first + f] - key_start for f in range(FRAMES_DEV)]
        full = ends[0] >= CHUNK
        some = ends[FRAMES_DEV - 1] > 0

        @pl.when(full)
        def _(b=b):
            heads(b, None)

        @pl.when(jnp.logical_and(some, jnp.logical_not(full)))
        def _(b=b, ends=ends):
            row = lax.broadcasted_iota(jnp.int32, (ROWS, 1), 0)
            limit = jnp.full((ROWS, 1), ends[0], jnp.int32)
            for f in range(1, FRAMES_DEV):
                limit = jnp.where(row >= f * FTOK, ends[f], limit)
            heads(b, limit)

    @pl.when(j == CHUNKS - 1)
    def _():
        lane = lax.broadcasted_iota(jnp.int32, (ROWS, HS), 1)
        for b in range(n):
            stats = jnp.zeros((ROWS, HS), F32)
            for h in range(HEADS_DEV):
                slot = b * HEADS_DEV + h
                m = m_ref[slot][:, :1]
                l = l_ref[slot][:, :1]
                has = l > 0.0
                safe = jnp.where(has, l, 1.0)
                o_refs[b][:, h * HS : (h + 1) * HS] = jnp.where(
                    has, acc_ref[slot] / safe, 0.0
                ).astype(BF)
                level = jnp.where(has, m * EXP_SCALE + jnp.log2(safe), NEG)
                high = level.astype(BF).astype(F32)
                mid = (level - high).astype(BF).astype(F32)
                low = level - high - mid
                stats = jnp.where(lane == 3 * h, high, stats)
                stats = jnp.where(lane == 3 * h + 1, mid, stats)
                stats = jnp.where(lane == 3 * h + 2, low, stats)
            o_refs[b][:, QCOLS:] = stats.astype(BF)


def attention(queries, qframes, kframes, vis_end, kv):
    n = len(queries)
    out = jax.ShapeDtypeStruct((ROWS, QCOLS + HS), BF)
    whole = pl.BlockSpec((ROWS, QCOLS), lambda j: (0, 0))
    smem = pl.BlockSpec(memory_space=pltpu.SMEM)
    return pl.pallas_call(
        functools.partial(attention_kernel, n),
        out_shape=[out] * n,
        grid=(CHUNKS,),
        in_specs=[smem] * 3
        + [whole] * n
        + [pl.BlockSpec((1, CHUNK, 2 * QCOLS), lambda j: (j, 0, 0))],
        out_specs=[pl.BlockSpec((ROWS, QCOLS + HS), lambda j: (0, 0))] * n,
        scratch_shapes=[pltpu.VMEM((n * HEADS_DEV, ROWS, HS), F32)] * 3,
        cost_estimate=pl.CostEstimate(
            flops=n * 4 * ROWS * QCOLS * CHUNK * CHUNKS * 2,
            bytes_accessed=CHUNKS * CHUNK * 2 * QCOLS * 2,
            transcendentals=n * HEADS_DEV * ROWS * CHUNK * CHUNKS,
        ),
        compiler_params=pltpu.CompilerParams(
            vmem_limit_bytes=48 * 1024 * 1024, dimension_semantics=("arbitrary",)
        ),
    )(jnp.stack(qframes), kframes, vis_end, *queries, kv)


def combine_kernel(*refs):
    parts, out_ref = refs[:4], refs[4]
    stats = [p[:, QCOLS:].astype(F32) for p in parts]
    for h in range(HEADS_DEV):
        levels = []
        for s in stats:
            levels.append(
                s[:, 3 * h : 3 * h + 1] + s[:, 3 * h + 1 : 3 * h + 2] + s[:, 3 * h + 2 : 3 * h + 3]
            )
        top = functools.reduce(jnp.maximum, levels)
        shares = [jnp.exp2(v - top) for v in levels]
        total = shares[0] + shares[1] + shares[2] + shares[3]
        cols = slice(h * HS, (h + 1) * HS)
        acc = jnp.zeros((ROWS, HS), F32)
        for p, w in zip(parts, shares):
            acc = acc + p[:, cols].astype(F32) * w
        out_ref[:, cols] = (acc / total).astype(BF)


def project_kernel(a_ref, w_ref, down_ref, up_ref, out_ref):
    down = down_ref[...]
    a = a_ref[...]
    for i in range(8):
        cols = slice(i * WIDTH, (i + 1) * WIDTH)
        merged = (w_ref[:, cols].astype(F32) + tdot(down, up_ref[i])).astype(BF)
        out_ref[:, cols] = jnp.dot(a, merged, preferred_element_type=F32).astype(BF)


def gather_tokens(tok):
    from_left = shift(tok, "x", 1)
    from_right = shift(tok, "x", -1)
    other = shift(tok, "zl", 1)
    other_left = shift(other, "x", 1)
    other_right = shift(other, "x", -1)
    half = ROWS // 2
    far = jnp.concatenate([shift(from_left[:half], "x", 1), shift(from_right[half:], "x", -1)])
    other_far = jnp.concatenate(
        [shift(other_left[:half], "x", 1), shift(other_right[half:], "x", -1)]
    )
    return [tok, from_left, far, from_right, other, other_left, other_far, other_right]


def spread_ctx(payload):
    payload = payload + shift(payload, "c", 1)
    half = payload.shape[0] // 2
    part = lax.dynamic_slice_in_dim(payload, lax.axis_index("c") * half, half, 0)
    for axis in ("y", "zh"):
        part = part + shift(part, axis, 1) + shift(part, axis, 2) + shift(part, axis, 3)
    other = shift(part, "c", 1)
    return jnp.where(
        lax.axis_index("c") == 0,
        jnp.concatenate([part, other]),
        jnp.concatenate([other, part]),
    )


def shards(
    tokens,
    norm_gain_vector,
    keys,
    values,
    query_frozen_weight,
    output_frozen_weight,
    query_update_first,
    query_update_second,
    output_update_first,
    output_update_second,
    owners,
    frame_block_number,
):
    zh, y, c = (lax.axis_index(a) for a in CTX)
    tp = lax.axis_index("zl") * 4 + lax.axis_index("x")
    rank = zh * 8 + y * 2 + c

    kv = lax.all_gather(jnp.concatenate([keys, values], axis=1), ("zh", "c"), axis=0, tiled=True)
    kv = kv.reshape(CHUNKS, CHUNK, 2 * QCOLS)

    down_q = lax.dynamic_slice_in_dim(query_update_first[0], tp * WIDTH, WIDTH, 0).T
    up_o = lax.dynamic_slice_in_dim(output_update_second[0], tp * WIDTH, WIDTH, 1)
    factors = [down_q, query_update_second[0], output_update_first[0].T, up_o]
    factors = [
        jnp.where(owners[i] == rank, f, jnp.zeros_like(f)) for i, f in enumerate(factors)
    ]
    spread = spread_ctx(jnp.concatenate(factors, axis=1))
    cuts = [0, WIDTH, WIDTH + QCOLS, WIDTH + 2 * QCOLS, 2 * WIDTH + 2 * QCOLS]
    down_q, up_q, down_o, up_o = [spread[:, a:b] for a, b in zip(cuts, cuts[1:])]

    gain = jnp.broadcast_to(norm_gain_vector[None, :], (16, WIDTH))
    small = jnp.concatenate([down_q, gain], axis=0)
    shifts = [(a, d) for a in range(2) for d in range(4)]
    lora = [small] + [tp_shift(small, a, d) for a, d in shifts[1:]]
    order = jnp.stack([tp_source(a, d) for a, d in shifts])

    up_all = lax.all_gather(up_o, TP, axis=0)

    blocks = gather_tokens(tokens)
    queries = vmem_call(
        query_kernel,
        jax.ShapeDtypeStruct((ROWS, QCOLS), BF),
        1,
        18,
        flops=2 * ROWS * 8 * WIDTH * QCOLS + 2 * 8 * WIDTH * RANK * QCOLS,
        nbytes=10**7,
    )(order, *blocks, *lora, query_frozen_weight, up_q)

    counts = jnp.sum(
        (frame_block_number[None, :] <= frame_block_number[:, None]).astype(jnp.int32), axis=1
    )
    vis_end = counts * FTOK
    kframes = (jnp.arange(CHUNKS, dtype=jnp.int32) * 8 + y * 2) * FRAMES_DEV

    def frames_of(step):
        return (zh * 8 + ((y - step) % 4) * 2 + c) * FRAMES_DEV

    q_left = shift(queries, "y", 1)
    q_right = shift(queries, "y", -1)
    q_far = shift(queries, "y", 2)
    (own,) = attention([queries], [frames_of(0)], kframes, vis_end, kv)
    left, right = attention([q_left, q_right], [frames_of(1), frames_of(-1)], kframes, vis_end, kv)
    back_left = shift(left, "y", -1)
    back_right = shift(right, "y", 1)
    (far,) = attention([q_far], [frames_of(2)], kframes, vis_end, kv)
    back_far = shift(far, "y", 2)

    attended = vmem_call(combine_kernel, jax.ShapeDtypeStruct((ROWS, QCOLS), BF), 0, 4, nbytes=10**6)(
        own, back_left, back_right, back_far
    )
    partial = vmem_call(
        project_kernel,
        jax.ShapeDtypeStruct((ROWS, 8 * WIDTH), BF),
        0,
        4,
        flops=2 * ROWS * 8 * WIDTH * QCOLS + 2 * 8 * WIDTH * RANK * QCOLS,
        nbytes=10**7,
    )(attended, output_frozen_weight, down_o, up_all)
    return lax.psum_scatter(partial, TP, scatter_dimension=1, tiled=True)


def solution(mesh):
    fine = Mesh(mesh.devices.reshape([SIZES[a] for a in AXES]), AXES)
    in_specs = (
        P(CTX, TP),
        P(TP),
        P(CTX, TP),
        P(CTX, TP),
        P(None, TP),
        P(TP, None),
        P(CTX, None, None),
        P(CTX, None, TP),
        P(CTX, TP, None),
        P(CTX, None, None),
        P(),
        P(),
    )
    return jax.shard_map(
        shards, mesh=fine, in_specs=in_specs, out_specs=P(CTX, TP), check_vma=False
    )
```

```python
import functools
import math

import jax
import jax.numpy as jnp
from jax import lax
from jax.experimental import pallas as pl
from jax.experimental.pallas import tpu as pltpu
from jax.sharding import Mesh
from jax.sharding import PartitionSpec as P

HS = 128
FTOK = 64
ROWS = 320
FRAMES_DEV = 5
WIDTH = 768
RANK = 64
HEADS_DEV = 3
QCOLS = HEADS_DEV * HS
CHUNK = 2 * ROWS
CHUNKS = 4
NEG = -1e30
EPS = 1e-6
AXES = ("zh", "y", "c", "zl", "x")
SIZES = {"zh": 4, "y": 4, "c": 2, "zl": 2, "x": 4}
CTX = ("zh", "y", "c")
TP = ("zl", "x")
EXP_SCALE = (HS ** (-0.5)) * math.log2(math.e)
BF = jnp.bfloat16
F32 = jnp.float32


def shift(v, axis, step):
    n = SIZES[axis]
    return lax.ppermute(v, axis, [(i, (i + step) % n) for i in range(n)])


def tp_shift(v, a, d):
    pairs = []
    for z in range(2):
        for x in range(4):
            pairs.append((z * 4 + x, (z ^ a) * 4 + (x + d) % 4))
    return lax.ppermute(v, TP, pairs)


def tp_source(a, d):
    return (lax.axis_index("zl") ^ a) * 4 + (lax.axis_index("x") - d) % 4


def vmem_call(body, out_shape, n_smem, n_vmem, scratch=(), flops=0, nbytes=0):
    return pl.pallas_call(
        body,
        out_shape=out_shape,
        in_specs=[pl.BlockSpec(memory_space=pltpu.SMEM)] * n_smem
        + [pl.BlockSpec(memory_space=pltpu.VMEM)] * n_vmem,
        scratch_shapes=list(scratch),
        cost_estimate=pl.CostEstimate(flops=flops, bytes_accessed=nbytes, transcendentals=0),
        compiler_params=pltpu.CompilerParams(vmem_limit_bytes=48 * 1024 * 1024),
    )


def tdot(a, b):
    return lax.dot_general(a, b, (((0,), (0,)), ((), ())), preferred_element_type=F32)


def gain_row(piece, lanes):
    return jnp.concatenate(
        [piece[r : r + 1, lanes : lanes + HS].astype(F32) for r in range(WIDTH // HS)], axis=1
    )


def norm_kernel(*refs):
    parts, lora, out_ref = refs[:8], refs[8], refs[9]
    total = jnp.zeros((ROWS, 1), F32)
    for i in range(8):
        v = parts[i][...].astype(F32)
        total = total + jnp.sum(v * v, axis=1, keepdims=True)
    inv = lax.rsqrt(total * (1.0 / (8 * WIDTH)) + EPS)
    for i in range(8):
        gain = gain_row(lora.at[i], WIDTH)
        out_ref[i] = (parts[i][...].astype(F32) * inv * gain).astype(BF)


def query_kernel(order_ref, normed_ref, mine_ref, other_ref, up_ref, up_other_ref, w_ref, out_ref):
    acc = jnp.zeros((ROWS, QCOLS), F32)
    up = jnp.concatenate([up_ref[...], up_other_ref[...]], axis=0)
    for i in range(8):
        rows = pl.ds(pl.multiple_of(order_ref[i] * WIDTH, WIDTH), WIDTH)
        down = jnp.concatenate([mine_ref[i, :, :WIDTH], other_ref[i, :, :WIDTH]], axis=0)
        merged = (w_ref[rows, :].astype(F32) + tdot(down, up)).astype(BF)
        acc = acc + jnp.dot(normed_ref[i], merged, preferred_element_type=F32)
    out_ref[...] = acc.astype(BF)


def attention_kernel(n, qframe_ref, kframe_ref, vis_ref, *refs):
    q_refs = refs[:n]
    kv_ref = refs[n]
    o_refs = refs[n + 1 :]
    lane = lax.broadcasted_iota(jnp.int32, (ROWS, HS), 1)
    row = lax.broadcasted_iota(jnp.int32, (ROWS, 1), 0)

    def heads(b, first, chunks):
        width = chunks * CHUNK
        last = kframe_ref[chunks - 1] * FTOK
        limit = jnp.full((ROWS, 1), vis_ref[first] - last, jnp.int32)
        for f in range(1, FRAMES_DEV):
            limit = jnp.where(row >= f * FTOK, vis_ref[first + f] - last, limit)
        seen = lax.broadcasted_iota(jnp.int32, (ROWS, CHUNK), 1) < limit

        def scores(h):
            cols = slice(h * HS, (h + 1) * HS)
            return lax.dot_general(
                q_refs[b][:, cols],
                kv_ref[:width, cols],
                (((1,), (1,)), ((), ())),
                preferred_element_type=F32,
            )

        s = scores(0)
        stats = jnp.zeros((ROWS, HS), F32)
        for h in range(HEADS_DEV):
            ahead = scores(h + 1) if h + 1 < HEADS_DEV else None
            tail = jnp.where(seen, s[:, width - CHUNK :], NEG)
            s = jnp.concatenate([s[:, : width - CHUNK], tail], axis=1) if chunks > 1 else tail
            top = jnp.max(s, axis=1, keepdims=True)
            p = jnp.exp2((s - top) * EXP_SCALE)
            lanes = p[:, :HS]
            for g in range(1, width // HS):
                lanes = lanes + p[:, g * HS : (g + 1) * HS]
            total = jnp.sum(lanes, axis=1, keepdims=True)
            acc = jnp.dot(
                p.astype(BF),
                kv_ref[:width, QCOLS + h * HS : QCOLS + (h + 1) * HS],
                preferred_element_type=F32,
            )
            has = top > 0.5 * NEG
            o_refs[b][:, h * HS : (h + 1) * HS] = jnp.where(has, acc / total, 0.0).astype(BF)
            level = jnp.where(has, top * EXP_SCALE + jnp.log2(total), NEG)
            high = level.astype(BF).astype(F32)
            mid = (level - high).astype(BF).astype(F32)
            low = level - high - mid
            stats = jnp.where(lane == 3 * h, high, stats)
            stats = jnp.where(lane == 3 * h + 1, mid, stats)
            stats = jnp.where(lane == 3 * h + 2, low, stats)
            s = ahead
        o_refs[b][:, QCOLS:] = stats.astype(BF)

    for b in range(n):
        first = qframe_ref[b]
        end = vis_ref[first + FRAMES_DEV - 1]
        some = jnp.int32(0)
        for j in range(CHUNKS):
            some = some + (kframe_ref[j] * FTOK < end).astype(jnp.int32)

        @pl.when(some == 0)
        def _(b=b):
            o_refs[b][:, :QCOLS] = jnp.zeros((ROWS, QCOLS), BF)
            blank = jnp.where((lane < 3 * HEADS_DEV) & (lane % 3 == 0), NEG, 0.0)
            o_refs[b][:, QCOLS:] = blank.astype(BF)

        for chunks in range(1, CHUNKS + 1):

            @pl.when(some == chunks)
            def _(b=b, first=first, chunks=chunks):
                heads(b, first, chunks)


def attention(queries, qframes, kframes, vis_end, kv):
    n = len(queries)
    return vmem_call(
        functools.partial(attention_kernel, n),
        [jax.ShapeDtypeStruct((ROWS, QCOLS + HS), BF)] * n,
        3,
        n + 1,
        flops=n * 8 * ROWS * QCOLS * CHUNK * CHUNKS,
        nbytes=CHUNKS * CHUNK * 2 * QCOLS * 2,
    )(jnp.stack(qframes), kframes, vis_end, *queries, kv)


def combine_kernel(*refs):
    parts, out_ref = refs[:4], refs[4]
    stats = [p[:, QCOLS:].astype(F32) for p in parts]
    for h in range(HEADS_DEV):
        levels = []
        for s in stats:
            levels.append(
                s[:, 3 * h : 3 * h + 1] + s[:, 3 * h + 1 : 3 * h + 2] + s[:, 3 * h + 2 : 3 * h + 3]
            )
        top = functools.reduce(jnp.maximum, levels)
        shares = [jnp.exp2(v - top) for v in levels]
        total = shares[0] + shares[1] + shares[2] + shares[3]
        cols = slice(h * HS, (h + 1) * HS)
        acc = jnp.zeros((ROWS, HS), F32)
        for p, w in zip(parts, shares):
            acc = acc + p[:, cols].astype(F32) * w
        out_ref[:, cols] = (acc / total).astype(BF)


def merge_out_kernel(order_ref, mine_ref, other_ref, down_ref, down_other_ref, w_ref, out_ref):
    down = jnp.concatenate([down_ref[...], down_other_ref[...]], axis=0)
    for i in range(8):
        cols = pl.ds(pl.multiple_of(order_ref[i] * WIDTH, WIDTH), WIDTH)
        up = jnp.concatenate([mine_ref[i], other_ref[i]], axis=0)
        out_ref[:, cols] = (w_ref[:, cols].astype(F32) + tdot(down, up)).astype(BF)


def project_kernel(a_ref, w_ref, out_ref):
    a = a_ref[...]
    for i in range(8):
        cols = slice(i * WIDTH, (i + 1) * WIDTH)
        out_ref[:, cols] = jnp.dot(a, w_ref[:, cols], preferred_element_type=F32).astype(BF)


def after(value, *others):
    return lax.optimization_barrier((value,) + others)[0]


def owned(factors, ids, owners, rank):
    masked = [
        jnp.where(owners[i] == rank, f, jnp.zeros_like(f)) for i, f in zip(ids, factors)
    ]
    return jnp.concatenate(masked, axis=1)


def spread(part, axis):
    return part + shift(part, axis, 1) + shift(part, axis, 2) + shift(part, axis, 3)


SHIFTS = [(a, d) for a in range(2) for d in range(4)]


def gather_tp(piece):
    return jnp.stack([piece] + [tp_shift(piece, a, d) for a, d in SHIFTS[1:]])


def shards(
    tokens,
    norm_gain_vector,
    keys,
    values,
    query_frozen_weight,
    output_frozen_weight,
    query_update_first,
    query_update_second,
    output_update_first,
    output_update_second,
    owners,
    frame_block_number,
):
    zh, y, c = (lax.axis_index(a) for a in CTX)
    tp = lax.axis_index("zl") * 4 + lax.axis_index("x")
    rank = zh * 8 + y * 2 + c

    kv = lax.all_gather(jnp.concatenate([keys, values], axis=1), ("zh", "c"), axis=0, tiled=True)

    half_rows = ROWS // 2
    left = shift(tokens, "x", 1)
    right = shift(tokens, "x", -1)
    other = shift(tokens, "zl", 1)

    down_q = lax.dynamic_slice_in_dim(query_update_first[0], tp * WIDTH, WIDTH, 0).T
    up_o = lax.dynamic_slice_in_dim(output_update_second[0], tp * WIDTH, WIDTH, 1)
    factors = owned(
        [down_q, query_update_second[0], up_o, output_update_first[0].T],
        [0, 1, 3, 2],
        owners,
        rank,
    )
    factors = factors + shift(factors, "c", 1)
    half = RANK // 2
    part = lax.dynamic_slice_in_dim(factors, c * half, half, 0)
    part_q, part_o = part[:, : WIDTH + QCOLS], part[:, WIDTH + QCOLS :]
    part_q = spread(part_q, "y")
    part_q = spread(after(part_q, left, right), "zh")

    far = [shift(left[:half_rows], "x", 1), shift(right[half_rows:], "x", -1)]
    other_left = shift(other, "x", 1)
    other_right = shift(other, "x", -1)

    gain = jnp.pad(norm_gain_vector.reshape(WIDTH // HS, HS), ((0, half - WIDTH // HS), (0, 0)))
    small = jnp.concatenate([part_q[:, :WIDTH], gain], axis=1)
    small = after(small, *far, other_left, other_right)
    mine_q = gather_tp(small)
    other_far = [
        shift(other_left[:half_rows], "x", 1),
        shift(other_right[half_rows:], "x", -1),
    ]
    up_q = part_q[:, WIDTH:]
    up_q_other = shift(up_q, "c", 1)
    other_q = shift(mine_q, "c", 1)

    part_o = spread(after(part_o, part_q), "y")
    part_o = spread(after(part_o, mine_q), "zh")
    mine_o = gather_tp(part_o[:, :WIDTH])
    down_o = part_o[:, WIDTH:]
    down_o_other = shift(down_o, "c", 1)
    other_o = shift(mine_o, "c", 1)

    order = jnp.stack([tp_source(a, d) for a, d in SHIFTS])
    blocks = [
        tokens,
        left,
        jnp.concatenate(far),
        right,
        other,
        other_left,
        jnp.concatenate(other_far),
        other_right,
    ]
    normed = vmem_call(
        norm_kernel, jax.ShapeDtypeStruct((8, ROWS, WIDTH), BF), 0, 9, nbytes=10**7
    )(*blocks, mine_q)
    queries = vmem_call(
        query_kernel,
        jax.ShapeDtypeStruct((ROWS, QCOLS), BF),
        1,
        6,
        flops=2 * ROWS * 8 * WIDTH * QCOLS + 2 * 8 * WIDTH * RANK * QCOLS,
        nbytes=10**7,
    )(order, normed, mine_q, other_q, up_q, up_q_other, query_frozen_weight)
    out_merged = vmem_call(
        merge_out_kernel,
        jax.ShapeDtypeStruct((QCOLS, 8 * WIDTH), BF),
        1,
        5,
        flops=2 * 8 * WIDTH * RANK * QCOLS,
        nbytes=10**7,
    )(order, mine_o, other_o, down_o, down_o_other, output_frozen_weight)

    counts = jnp.sum(
        (frame_block_number[None, :] <= frame_block_number[:, None]).astype(jnp.int32), axis=1
    )
    vis_end = counts * FTOK
    kframes = (jnp.arange(CHUNKS, dtype=jnp.int32) * 8 + y * 2) * FRAMES_DEV

    def frames_of(step):
        return (zh * 8 + ((y - step) % 4) * 2 + c) * FRAMES_DEV

    q_left = shift(queries, "y", 1)
    q_right = shift(queries, "y", -1)
    q_far = shift(queries, "y", 2)
    (own,) = attention([queries], [frames_of(0)], kframes, vis_end, kv)
    left, right = attention([q_left, q_right], [frames_of(1), frames_of(-1)], kframes, vis_end, kv)
    back_left = shift(left, "y", -1)
    back_right = shift(right, "y", 1)
    (far,) = attention([q_far], [frames_of(2)], kframes, vis_end, kv)
    back_far = shift(far, "y", 2)

    attended = vmem_call(combine_kernel, jax.ShapeDtypeStruct((ROWS, QCOLS), BF), 0, 4, nbytes=10**6)(
        own, back_left, back_right, back_far
    )
    partial = vmem_call(
        project_kernel,
        jax.ShapeDtypeStruct((ROWS, 8 * WIDTH), BF),
        0,
        2,
        flops=2 * ROWS * 8 * WIDTH * QCOLS,
        nbytes=10**7,
    )(attended, out_merged)
    return lax.psum_scatter(partial, TP, scatter_dimension=1, tiled=True)


def solution(mesh):
    fine = Mesh(mesh.devices.reshape([SIZES[a] for a in AXES]), AXES)
    in_specs = (
        P(CTX, TP),
        P(TP),
        P(CTX, TP),
        P(CTX, TP),
        P(None, TP),
        P(TP, None),
        P(CTX, None, None),
        P(CTX, None, TP),
        P(CTX, TP, None),
        P(CTX, None, None),
        P(),
        P(),
    )
    return jax.shard_map(
        shards, mesh=fine, in_specs=in_specs, out_specs=P(CTX, TP), check_vma=False
    )
```

```python
import functools
import math

import jax
import jax.numpy as jnp
from jax import lax
from jax.experimental import pallas as pl
from jax.experimental.pallas import tpu as pltpu
from jax.sharding import Mesh
from jax.sharding import PartitionSpec as P

HS = 128
FTOK = 64
ROWS = 320
FRAMES_DEV = 5
WIDTH = 768
RANK = 64
HEADS_DEV = 3
QCOLS = HEADS_DEV * HS
CHUNK = 2 * ROWS
CHUNKS = 4
NEG = -1e30
EPS = 1e-6
AXES = ("zh", "y", "c", "zl", "x")
SIZES = {"zh": 4, "y": 4, "c": 2, "zl": 2, "x": 4}
CTX = ("zh", "y", "c")
TP = ("zl", "x")
EXP_SCALE = (HS ** (-0.5)) * math.log2(math.e)
BF = jnp.bfloat16
F32 = jnp.float32


def shift(v, axis, step):
    n = SIZES[axis]
    return lax.ppermute(v, axis, [(i, (i + step) % n) for i in range(n)])


def tp_source(a, d):
    return (lax.axis_index("zl") ^ a) * 4 + (lax.axis_index("x") - d) % 4


def vmem_call(body, out_shape, n_smem, n_vmem, scratch=(), flops=0, nbytes=0):
    return pl.pallas_call(
        body,
        out_shape=out_shape,
        in_specs=[pl.BlockSpec(memory_space=pltpu.SMEM)] * n_smem
        + [pl.BlockSpec(memory_space=pltpu.VMEM)] * n_vmem,
        scratch_shapes=list(scratch),
        cost_estimate=pl.CostEstimate(flops=flops, bytes_accessed=nbytes, transcendentals=0),
        compiler_params=pltpu.CompilerParams(vmem_limit_bytes=48 * 1024 * 1024),
    )


def tdot(a, b):
    return lax.dot_general(a, b, (((0,), (0,)), ((), ())), preferred_element_type=F32)


def gain_row(piece, lanes):
    return jnp.concatenate(
        [piece[r : r + 1, lanes : lanes + HS].astype(F32) for r in range(WIDTH // HS)], axis=1
    )


def norm_kernel(order_ref, *refs):
    parts, lora, out_ref = refs[:8], refs[8], refs[9]
    total = jnp.zeros((ROWS, 1), F32)
    for i in range(8):
        v = parts[i][...].astype(F32)
        total = total + jnp.sum(v * v, axis=1, keepdims=True)
    inv = lax.rsqrt(total * (1.0 / (8 * WIDTH)) + EPS)
    for i in range(8):
        gain = gain_row(lora.at[order_ref[i]], WIDTH)
        out_ref[i] = (parts[i][...].astype(F32) * inv * gain).astype(BF)


def query_kernel(order_ref, normed_ref, mine_ref, other_ref, up_ref, up_other_ref, w_ref, out_ref):
    acc = jnp.zeros((ROWS, QCOLS), F32)
    up = jnp.concatenate([up_ref[...], up_other_ref[...]], axis=0)
    for i in range(8):
        rows = pl.ds(pl.multiple_of(order_ref[i] * WIDTH, WIDTH), WIDTH)
        at = order_ref[i]
        down = jnp.concatenate([mine_ref[at, :, :WIDTH], other_ref[at, :, :WIDTH]], axis=0)
        merged = (w_ref[rows, :].astype(F32) + tdot(down, up)).astype(BF)
        acc = acc + jnp.dot(normed_ref[i], merged, preferred_element_type=F32)
    out_ref[...] = acc.astype(BF)


def attention_kernel(n, qframe_ref, kframe_ref, vis_ref, *refs):
    q_refs = refs[:n]
    kv_ref = refs[n]
    o_refs = refs[n + 1 :]
    lane = lax.broadcasted_iota(jnp.int32, (ROWS, HS), 1)
    row = lax.broadcasted_iota(jnp.int32, (ROWS, 1), 0)

    def heads(b, first, chunks):
        width = chunks * CHUNK
        last = kframe_ref[chunks - 1] * FTOK
        limit = jnp.full((ROWS, 1), vis_ref[first] - last, jnp.int32)
        for f in range(1, FRAMES_DEV):
            limit = jnp.where(row >= f * FTOK, vis_ref[first + f] - last, limit)
        seen = lax.broadcasted_iota(jnp.int32, (ROWS, CHUNK), 1) < limit

        def scores(h):
            cols = slice(h * HS, (h + 1) * HS)
            return lax.dot_general(
                q_refs[b][:, cols],
                kv_ref[:width, cols],
                (((1,), (1,)), ((), ())),
                preferred_element_type=F32,
            )

        s = scores(0)
        stats = jnp.zeros((ROWS, HS), F32)
        for h in range(HEADS_DEV):
            ahead = scores(h + 1) if h + 1 < HEADS_DEV else None
            tail = jnp.where(seen, s[:, width - CHUNK :], NEG)
            s = jnp.concatenate([s[:, : width - CHUNK], tail], axis=1) if chunks > 1 else tail
            top = jnp.max(s, axis=1, keepdims=True)
            p = jnp.exp2((s - top) * EXP_SCALE)
            lanes = p[:, :HS]
            for g in range(1, width // HS):
                lanes = lanes + p[:, g * HS : (g + 1) * HS]
            total = jnp.sum(lanes, axis=1, keepdims=True)
            acc = jnp.dot(
                p.astype(BF),
                kv_ref[:width, QCOLS + h * HS : QCOLS + (h + 1) * HS],
                preferred_element_type=F32,
            )
            has = top > 0.5 * NEG
            o_refs[b][:, h * HS : (h + 1) * HS] = jnp.where(has, acc / total, 0.0).astype(BF)
            level = jnp.where(has, top * EXP_SCALE + jnp.log2(total), NEG)
            high = level.astype(BF).astype(F32)
            mid = (level - high).astype(BF).astype(F32)
            low = level - high - mid
            stats = jnp.where(lane == 3 * h, high, stats)
            stats = jnp.where(lane == 3 * h + 1, mid, stats)
            stats = jnp.where(lane == 3 * h + 2, low, stats)
            s = ahead
        o_refs[b][:, QCOLS:] = stats.astype(BF)

    for b in range(n):
        first = qframe_ref[b]
        end = vis_ref[first + FRAMES_DEV - 1]
        some = jnp.int32(0)
        for j in range(CHUNKS):
            some = some + (kframe_ref[j] * FTOK < end).astype(jnp.int32)

        @pl.when(some == 0)
        def _(b=b):
            o_refs[b][:, :QCOLS] = jnp.zeros((ROWS, QCOLS), BF)
            blank = jnp.where((lane < 3 * HEADS_DEV) & (lane % 3 == 0), NEG, 0.0)
            o_refs[b][:, QCOLS:] = blank.astype(BF)

        for chunks in range(1, CHUNKS + 1):

            @pl.when(some == chunks)
            def _(b=b, first=first, chunks=chunks):
                heads(b, first, chunks)


def attention(queries, qframes, kframes, vis_end, kv):
    n = len(queries)
    return vmem_call(
        functools.partial(attention_kernel, n),
        [jax.ShapeDtypeStruct((ROWS, QCOLS + HS), BF)] * n,
        3,
        n + 1,
        flops=n * 8 * ROWS * QCOLS * CHUNK * CHUNKS,
        nbytes=CHUNKS * CHUNK * 2 * QCOLS * 2,
    )(jnp.stack(qframes), kframes, vis_end, *queries, kv)


def combine_kernel(*refs):
    parts, out_ref = refs[:4], refs[4]
    stats = [p[:, QCOLS:].astype(F32) for p in parts]
    for h in range(HEADS_DEV):
        levels = []
        for s in stats:
            levels.append(
                s[:, 3 * h : 3 * h + 1] + s[:, 3 * h + 1 : 3 * h + 2] + s[:, 3 * h + 2 : 3 * h + 3]
            )
        top = functools.reduce(jnp.maximum, levels)
        shares = [jnp.exp2(v - top) for v in levels]
        total = shares[0] + shares[1] + shares[2] + shares[3]
        cols = slice(h * HS, (h + 1) * HS)
        acc = jnp.zeros((ROWS, HS), F32)
        for p, w in zip(parts, shares):
            acc = acc + p[:, cols].astype(F32) * w
        out_ref[:, cols] = (acc / total).astype(BF)


def merge_out_kernel(mine_ref, other_ref, down_ref, down_other_ref, w_ref, out_ref):
    down = jnp.concatenate([down_ref[...], down_other_ref[...]], axis=0)
    for i in range(8):
        cols = slice(i * WIDTH, (i + 1) * WIDTH)
        up = jnp.concatenate([mine_ref[i], other_ref[i]], axis=0)
        out_ref[:, cols] = (w_ref[:, cols].astype(F32) + tdot(down, up)).astype(BF)


def project_kernel(a_ref, w_ref, out_ref):
    a = a_ref[...]
    for i in range(8):
        cols = slice(i * WIDTH, (i + 1) * WIDTH)
        out_ref[:, cols] = jnp.dot(a, w_ref[:, cols], preferred_element_type=F32).astype(BF)


def after(value, *others):
    return lax.optimization_barrier((value,) + others)[0]


def prep_kernel(scal_ref, down_q_ref, up_q_ref, down_o_ref, up_o_ref, out_ref):
    def keep(i, v):
        return jnp.where(scal_ref[1 + i] == scal_ref[0], v.astype(F32), 0.0).astype(BF)

    out_ref[:, :WIDTH] = keep(0, down_q_ref[0].astype(F32).T)
    out_ref[:, WIDTH : WIDTH + QCOLS] = keep(1, up_q_ref[0])
    out_ref[:, WIDTH + QCOLS : 2 * WIDTH + QCOLS] = keep(3, up_o_ref[0])
    out_ref[:, 2 * WIDTH + QCOLS :] = keep(2, down_o_ref[0].astype(F32).T)


def prepare(rank, tp, owners, down_q, up_q, down_o, up_o):
    scal = jnp.concatenate([jnp.stack([rank, tp])[:1], owners, tp[None]]).astype(jnp.int32)
    return pl.pallas_call(
        prep_kernel,
        out_shape=jax.ShapeDtypeStruct((RANK, 2 * WIDTH + 2 * QCOLS), BF),
        grid_spec=pltpu.PrefetchScalarGridSpec(
            num_scalar_prefetch=1,
            grid=(1,),
            in_specs=[
                pl.BlockSpec((1, WIDTH, RANK), lambda i, sc: (0, sc[5], 0)),
                pl.BlockSpec((1, RANK, QCOLS), lambda i, sc: (0, 0, 0)),
                pl.BlockSpec((1, QCOLS, RANK), lambda i, sc: (0, 0, 0)),
                pl.BlockSpec((1, RANK, WIDTH), lambda i, sc: (0, 0, sc[5])),
            ],
            out_specs=pl.BlockSpec((RANK, 2 * WIDTH + 2 * QCOLS), lambda i, sc: (0, 0)),
        ),
        cost_estimate=pl.CostEstimate(flops=0, bytes_accessed=10**6, transcendentals=0),
        compiler_params=pltpu.CompilerParams(vmem_limit_bytes=16 * 1024 * 1024),
    )(scal, down_q, up_q, down_o, up_o)


def copies(piece, axis, n):
    everywhere = jnp.broadcast_to(piece[None], (n,) + piece.shape)
    return lax.all_to_all(everywhere, axis, 0, 0)


def spread(part, axis):
    got = copies(part, axis, SIZES[axis])
    return got[0] + got[1] + got[2] + got[3]


SHIFTS = [(a, d) for a in range(2) for d in range(4)]


def shards(
    tokens,
    norm_gain_vector,
    keys,
    values,
    query_frozen_weight,
    output_frozen_weight,
    query_update_first,
    query_update_second,
    output_update_first,
    output_update_second,
    owners,
    frame_block_number,
):
    zh, y, c = (lax.axis_index(a) for a in CTX)
    tp = lax.axis_index("zl") * 4 + lax.axis_index("x")
    rank = zh * 8 + y * 2 + c

    left = shift(tokens, "x", 1)
    right = shift(tokens, "x", -1)
    other = shift(tokens, "zl", 1)

    factors = prepare(
        rank,
        tp,
        owners,
        query_update_first,
        query_update_second,
        output_update_first,
        output_update_second,
    )
    factors = factors + shift(factors, "c", 1)
    half = RANK // 2
    part = lax.dynamic_slice_in_dim(factors, c * half, half, 0)
    part_q, part_o = part[:, : WIDTH + QCOLS], part[:, WIDTH + QCOLS :]
    part_q = spread(part_q, "zh")

    kv = jnp.concatenate([keys, values], axis=1)
    kv = lax.all_gather(after(kv, other, part_q), ("zh", "c"), axis=0, tiled=True)

    other_left = shift(other, "x", 1)
    other_right = shift(other, "x", -1)
    part_q = spread(after(part_q, left, right), "y")

    gain = jnp.pad(norm_gain_vector.reshape(WIDTH // HS, HS), ((0, half - WIDTH // HS), (0, 0)))
    small = jnp.concatenate([part_q[:, :WIDTH], gain], axis=1)
    mine_q = copies(small, TP, 8)
    up_q = part_q[:, WIDTH:]
    up_q_other = shift(up_q, "c", 1)
    other_q = shift(mine_q, "c", 1)

    half_rows = ROWS // 2
    far_left = shift(jnp.concatenate([left[:half_rows], other_left[:half_rows]]), "x", 1)
    far_right = shift(jnp.concatenate([right[half_rows:], other_right[half_rows:]]), "x", -1)

    part_o = spread(after(part_o, other_left, other_right, mine_q), "zh")
    part_o = spread(part_o, "y")
    order = jnp.stack([tp_source(a, d) for a, d in SHIFTS])
    blocks = [
        tokens,
        left,
        jnp.concatenate([far_left[:half_rows], far_right[:half_rows]]),
        right,
        other,
        other_left,
        jnp.concatenate([far_left[half_rows:], far_right[half_rows:]]),
        other_right,
    ]
    normed = vmem_call(
        norm_kernel, jax.ShapeDtypeStruct((8, ROWS, WIDTH), BF), 1, 9, nbytes=10**7
    )(order, *blocks, mine_q)
    queries = vmem_call(
        query_kernel,
        jax.ShapeDtypeStruct((ROWS, QCOLS), BF),
        1,
        6,
        flops=2 * ROWS * 8 * WIDTH * QCOLS + 2 * 8 * WIDTH * RANK * QCOLS,
        nbytes=10**7,
    )(order, normed, mine_q, other_q, up_q, up_q_other, query_frozen_weight)
    mine_o = copies(after(part_o[:, :WIDTH], queries), TP, 8)
    down_o = part_o[:, WIDTH:]
    down_o_other = shift(down_o, "c", 1)
    other_o = shift(mine_o, "c", 1)
    out_merged = vmem_call(
        merge_out_kernel,
        jax.ShapeDtypeStruct((QCOLS, 8 * WIDTH), BF),
        0,
        5,
        flops=2 * 8 * WIDTH * RANK * QCOLS,
        nbytes=10**7,
    )(mine_o, other_o, down_o, down_o_other, output_frozen_weight)

    counts = jnp.sum(
        (frame_block_number[None, :] <= frame_block_number[:, None]).astype(jnp.int32), axis=1
    )
    vis_end = counts * FTOK
    kframes = (jnp.arange(CHUNKS, dtype=jnp.int32) * 8 + y * 2) * FRAMES_DEV

    def frames_of(step):
        return (zh * 8 + ((y - step) % 4) * 2 + c) * FRAMES_DEV

    q_left = shift(queries, "y", 1)
    q_right = shift(queries, "y", -1)
    q_far = shift(queries, "y", 2)
    (own,) = attention([queries], [frames_of(0)], kframes, vis_end, kv)
    left, right = attention([q_left, q_right], [frames_of(1), frames_of(-1)], kframes, vis_end, kv)
    back_left = shift(left, "y", -1)
    back_right = shift(right, "y", 1)
    (far,) = attention([q_far], [frames_of(2)], kframes, vis_end, kv)
    back_far = shift(far, "y", 2)

    attended = vmem_call(combine_kernel, jax.ShapeDtypeStruct((ROWS, QCOLS), BF), 0, 4, nbytes=10**6)(
        own, back_left, back_right, back_far
    )
    partial = vmem_call(
        project_kernel,
        jax.ShapeDtypeStruct((ROWS, 8 * WIDTH), BF),
        0,
        2,
        flops=2 * ROWS * 8 * WIDTH * QCOLS,
        nbytes=10**7,
    )(attended, out_merged)
    return lax.psum_scatter(partial, TP, scatter_dimension=1, tiled=True)


def solution(mesh):
    fine = Mesh(mesh.devices.reshape([SIZES[a] for a in AXES]), AXES)
    in_specs = (
        P(CTX, TP),
        P(TP),
        P(CTX, TP),
        P(CTX, TP),
        P(None, TP),
        P(TP, None),
        P(CTX, None, None),
        P(CTX, None, TP),
        P(CTX, TP, None),
        P(CTX, None, None),
        P(),
        P(),
    )
    return jax.shard_map(
        shards, mesh=fine, in_specs=in_specs, out_specs=P(CTX, TP), check_vma=False
    )
```

```python
import functools
import math

import jax
import jax.numpy as jnp
from jax import lax
from jax.experimental import pallas as pl
from jax.experimental.pallas import tpu as pltpu
from jax.sharding import Mesh
from jax.sharding import PartitionSpec as P

HS = 128
FTOK = 64
ROWS = 320
FRAMES_DEV = 5
WIDTH = 768
RANK = 64
HEADS_DEV = 3
QCOLS = HEADS_DEV * HS
CHUNK = 2 * ROWS
CHUNKS = 4
NEG = -1e30
PIECE = 96
EPS = 1e-6
AXES = ("zh", "y", "c", "zl", "x")
SIZES = {"zh": 4, "y": 4, "c": 2, "zl": 2, "x": 4}
CTX = ("zh", "y", "c")
TP = ("zl", "x")
EXP_SCALE = (HS ** (-0.5)) * math.log2(math.e)
BF = jnp.bfloat16
F32 = jnp.float32


def shift(v, axis, step):
    n = SIZES[axis]
    return lax.ppermute(v, axis, [(i, (i + step) % n) for i in range(n)])


def tp_source(a, d):
    return (lax.axis_index("zl") ^ a) * 4 + (lax.axis_index("x") - d) % 4


def vmem_call(body, out_shape, n_smem, n_vmem, scratch=(), flops=0, nbytes=0, mib=16, n_any=0):
    return pl.pallas_call(
        body,
        out_shape=out_shape,
        in_specs=[pl.BlockSpec(memory_space=pltpu.SMEM)] * n_smem
        + [pl.BlockSpec(memory_space=pltpu.VMEM)] * n_vmem
        + [pl.BlockSpec(memory_space=pl.ANY)] * n_any,
        scratch_shapes=list(scratch),
        cost_estimate=pl.CostEstimate(flops=flops, bytes_accessed=nbytes, transcendentals=0),
        compiler_params=pltpu.CompilerParams(vmem_limit_bytes=mib * 1024 * 1024),
    )


def tdot(a, b):
    return lax.dot_general(a, b, (((0,), (0,)), ((), ())), preferred_element_type=F32)


def gain_row(piece, lanes):
    return jnp.concatenate(
        [piece[r : r + 1, lanes : lanes + HS].astype(F32) for r in range(WIDTH // HS)], axis=1
    )


def query_kernel(order_ref, *refs):
    parts = refs[:8]
    mine_ref, other_ref, up_ref, up_other_ref, w_ref, out_ref, held, sems = refs[8:]

    def fetch(i):
        rows = pl.ds(pl.multiple_of(order_ref[i] * WIDTH, WIDTH), WIDTH)
        return pltpu.make_async_copy(w_ref.at[rows, :], held.at[i], sems.at[i])

    for i in range(8):
        fetch(i).start()
    total = jnp.zeros((ROWS, HS), F32)
    for i in range(8):
        v = parts[i][...].astype(F32)
        v = v * v
        for g in range(WIDTH // HS):
            total = total + v[:, g * HS : (g + 1) * HS]
    total = jnp.sum(total, axis=1, keepdims=True)
    inv = lax.rsqrt(total * (1.0 / (8 * WIDTH)) + EPS)
    acc = jnp.zeros((ROWS, QCOLS), F32)
    up = jnp.concatenate([up_ref[...], up_other_ref[...]], axis=0)
    for i in range(8):
        at = order_ref[i]
        gain = gain_row(mine_ref.at[at], WIDTH)
        normed = (parts[i][...].astype(F32) * inv * gain).astype(BF)
        down = jnp.concatenate([mine_ref[at, :, :WIDTH], other_ref[at, :, :WIDTH]], axis=0)
        fetch(i).wait()
        merged = (held[i].astype(F32) + tdot(down, up)).astype(BF)
        acc = acc + jnp.dot(normed, merged, preferred_element_type=F32)
    out_ref[...] = acc.astype(BF)


def attention_kernel(n, qframe_ref, kframe_ref, vis_ref, *refs):
    q_refs = refs[:n]
    kv_ref = refs[n]
    o_refs = refs[n + 1 :]
    lane = lax.broadcasted_iota(jnp.int32, (ROWS, HS), 1)
    row = lax.broadcasted_iota(jnp.int32, (ROWS, 1), 0)

    def heads(b, first, chunks):
        width = chunks * CHUNK
        last = kframe_ref[chunks - 1] * FTOK
        limit = jnp.full((ROWS, 1), vis_ref[first] - last, jnp.int32)
        for f in range(1, FRAMES_DEV):
            limit = jnp.where(row >= f * FTOK, vis_ref[first + f] - last, limit)
        seen = lax.broadcasted_iota(jnp.int32, (ROWS, CHUNK), 1) < limit

        def scores(h):
            cols = slice(h * HS, (h + 1) * HS)
            return lax.dot_general(
                q_refs[b][:, cols],
                kv_ref[:width, cols],
                (((1,), (1,)), ((), ())),
                preferred_element_type=F32,
            )

        s = scores(0)
        stats = jnp.zeros((ROWS, HS), F32)
        for h in range(HEADS_DEV):
            ahead = scores(h + 1) if h + 1 < HEADS_DEV else None
            tail = jnp.where(seen, s[:, width - CHUNK :], NEG)
            s = jnp.concatenate([s[:, : width - CHUNK], tail], axis=1) if chunks > 1 else tail
            top = jnp.max(s, axis=1, keepdims=True)
            p = jnp.exp2((s - top) * EXP_SCALE)
            lanes = p[:, :HS]
            for g in range(1, width // HS):
                lanes = lanes + p[:, g * HS : (g + 1) * HS]
            total = jnp.sum(lanes, axis=1, keepdims=True)
            acc = jnp.dot(
                p.astype(BF),
                kv_ref[:width, QCOLS + h * HS : QCOLS + (h + 1) * HS],
                preferred_element_type=F32,
            )
            has = top > 0.5 * NEG
            o_refs[b][:, h * HS : (h + 1) * HS] = jnp.where(has, acc / total, 0.0).astype(BF)
            level = jnp.where(has, top * EXP_SCALE + jnp.log2(total), NEG)
            high = level.astype(BF).astype(F32)
            mid = (level - high).astype(BF).astype(F32)
            low = level - high - mid
            stats = jnp.where(lane == 3 * h, high, stats)
            stats = jnp.where(lane == 3 * h + 1, mid, stats)
            stats = jnp.where(lane == 3 * h + 2, low, stats)
            s = ahead
        o_refs[b][:, QCOLS:] = stats.astype(BF)

    for b in range(n):
        first = qframe_ref[b]
        end = vis_ref[first + FRAMES_DEV - 1]
        some = jnp.int32(0)
        for j in range(CHUNKS):
            some = some + (kframe_ref[j] * FTOK < end).astype(jnp.int32)

        @pl.when(some == 0)
        def _(b=b):
            o_refs[b][:, :QCOLS] = jnp.zeros((ROWS, QCOLS), BF)
            blank = jnp.where((lane < 3 * HEADS_DEV) & (lane % 3 == 0), NEG, 0.0)
            o_refs[b][:, QCOLS:] = blank.astype(BF)

        for chunks in range(1, CHUNKS + 1):

            @pl.when(some == chunks)
            def _(b=b, first=first, chunks=chunks):
                heads(b, first, chunks)


def attention(queries, qframes, kframes, vis_end, kv):
    n = len(queries)
    return vmem_call(
        functools.partial(attention_kernel, n),
        [jax.ShapeDtypeStruct((ROWS, QCOLS + HS), BF)] * n,
        3,
        n + 1,
        flops=n * 8 * ROWS * QCOLS * CHUNK * CHUNKS,
        nbytes=CHUNKS * CHUNK * 2 * QCOLS * 2,
        mib=32,
    )(jnp.stack(qframes), kframes, vis_end, *queries, kv)


def combine_kernel(*refs):
    parts, out_ref = refs[:4], refs[4]
    stats = [p[:, QCOLS:].astype(F32) for p in parts]
    for h in range(HEADS_DEV):
        levels = []
        for s in stats:
            levels.append(
                s[:, 3 * h : 3 * h + 1] + s[:, 3 * h + 1 : 3 * h + 2] + s[:, 3 * h + 2 : 3 * h + 3]
            )
        top = functools.reduce(jnp.maximum, levels)
        shares = [jnp.exp2(v - top) for v in levels]
        total = shares[0] + shares[1] + shares[2] + shares[3]
        cols = slice(h * HS, (h + 1) * HS)
        acc = jnp.zeros((ROWS, HS), F32)
        for p, w in zip(parts, shares):
            acc = acc + p[:, cols].astype(F32) * w
        out_ref[:, cols] = (acc / total).astype(BF)


def merge_out_kernel(order_ref, w_ref, mine_ref, other_ref, up_ref, up_other_ref, out_ref):
    at = order_ref[pl.program_id(0)]
    up = jnp.concatenate([up_ref[...], up_other_ref[...]], axis=0)
    down = jnp.concatenate([mine_ref[at], other_ref[at]], axis=0)
    out_ref[...] = (w_ref[...].astype(F32) + tdot(down, up)).astype(BF)


def merge_out(order, w, mine, other, up, up_other):
    def whole(shape):
        return pl.BlockSpec(shape, lambda i: (0,) * len(shape))

    return pl.pallas_call(
        merge_out_kernel,
        out_shape=jax.ShapeDtypeStruct((8 * QCOLS, WIDTH), BF),
        grid=(8,),
        in_specs=[
            pl.BlockSpec(memory_space=pltpu.SMEM),
            pl.BlockSpec((QCOLS, WIDTH), lambda i: (i, 0)),
            whole(mine.shape),
            whole(other.shape),
            whole(up.shape),
            whole(up_other.shape),
        ],
        out_specs=pl.BlockSpec((QCOLS, WIDTH), lambda i: (i, 0)),
        cost_estimate=pl.CostEstimate(
            flops=2 * 8 * WIDTH * RANK * QCOLS, bytes_accessed=10**7, transcendentals=0
        ),
        compiler_params=pltpu.CompilerParams(vmem_limit_bytes=16 * 1024 * 1024),
    )(order, w, mine, other, up, up_other)


def project_kernel(order_ref, a_ref, w_ref, out_ref):
    acc = jnp.zeros((ROWS, WIDTH), F32)
    for i in range(8):
        acc = acc + jnp.dot(
            a_ref[order_ref[i]],
            w_ref[i * QCOLS : (i + 1) * QCOLS, :],
            preferred_element_type=F32,
        )
    out_ref[...] = acc.astype(BF)


def after(value, *others):
    return lax.optimization_barrier((value,) + others)[0]


def prep_kernel(scal_ref, down_q_ref, up_q_ref, down_o_ref, up_o_ref, q_ref, o_ref):
    def keep(i, v):
        return jnp.where(scal_ref[1 + i] == scal_ref[0], v.astype(F32), 0.0).astype(BF)

    half = RANK // 2
    q_parts = [keep(0, down_q_ref[...]), keep(1, up_q_ref[...])]
    o_parts = [keep(2, down_o_ref[...]), keep(3, up_o_ref[...])]
    for out_ref, parts in ((q_ref, q_parts), (o_ref, o_parts)):
        start = 0
        for v in parts:
            width = v.shape[1]
            for y in range(4):
                for c in range(2):
                    out_ref[2 * y + c, :, start : start + width] = v[c * half : (c + 1) * half]
            start += width


def prepare(rank, tp, owners, down_q, up_q, down_o, up_o):
    scal = jnp.concatenate([rank[None], owners, tp[None]]).astype(jnp.int32)
    out = jax.ShapeDtypeStruct((8, RANK // 2, WIDTH + QCOLS), BF)
    return pl.pallas_call(
        prep_kernel,
        out_shape=[out, out],
        grid_spec=pltpu.PrefetchScalarGridSpec(
            num_scalar_prefetch=1,
            grid=(1,),
            in_specs=[
                pl.BlockSpec((RANK, WIDTH), lambda i, sc: (0, sc[5])),
                pl.BlockSpec((RANK, QCOLS), lambda i, sc: (0, 0)),
                pl.BlockSpec((RANK, QCOLS), lambda i, sc: (0, 0)),
                pl.BlockSpec((RANK, WIDTH), lambda i, sc: (0, sc[5])),
            ],
            out_specs=[pl.BlockSpec(out.shape, lambda i, sc: (0, 0, 0))] * 2,
        ),
        cost_estimate=pl.CostEstimate(flops=0, bytes_accessed=10**6, transcendentals=0),
        compiler_params=pltpu.CompilerParams(vmem_limit_bytes=16 * 1024 * 1024),
    )(scal, down_q, up_q, down_o, up_o)


def copies(piece, axis, n):
    everywhere = jnp.broadcast_to(piece[None], (n,) + piece.shape)
    return lax.all_to_all(everywhere, axis, 0, 0)


def spread_ctx(pieces):
    got = jnp.sum(lax.all_to_all(pieces, ("y", "c"), 0, 0), axis=0)
    return jnp.sum(copies(got, "zh", 4), axis=0)


def column_piece(weight, rank, tp):
    piece = lax.dynamic_slice(
        weight, ((rank % 4) * PIECE, (tp ^ (rank // 4)) * WIDTH), (PIECE, WIDTH)
    )
    return piece


def to_columns(piece):
    pairs = []
    for r in range(32):
        for t in range(8):
            pairs.append((r * 8 + t, r * 8 + (t ^ (r // 4))))
    return lax.ppermute(piece, AXES, pairs)


SHIFTS = [(a, d) for a in range(2) for d in range(4)]


def shards(
    tokens,
    norm_gain_vector,
    keys,
    values,
    query_frozen_weight,
    output_frozen_weight,
    query_update_first,
    query_update_second,
    output_update_first,
    output_update_second,
    owners,
    frame_block_number,
):
    zh, y, c = (lax.axis_index(a) for a in CTX)
    tp = lax.axis_index("zl") * 4 + lax.axis_index("x")
    rank = zh * 8 + y * 2 + c

    left = shift(tokens, "x", 1)
    right = shift(tokens, "x", -1)
    other = shift(tokens, "zl", 1)

    half = RANK // 2
    pieces_q, pieces_o = prepare(
        rank,
        tp,
        owners,
        query_update_first[0].T,
        query_update_second[0],
        output_update_first[0].T,
        output_update_second[0],
    )
    part_q = spread_ctx(after(pieces_q, left, right))

    kv = jnp.concatenate([keys, values], axis=1)
    kv = lax.all_gather(after(kv, other, part_q), ("zh", "c"), axis=0, tiled=True)

    other_left = shift(other, "x", 1)
    other_right = shift(other, "x", -1)

    gain = jnp.pad(norm_gain_vector.reshape(WIDTH // HS, HS), ((0, half - WIDTH // HS), (0, 0)))
    mine_q = copies(jnp.concatenate([part_q[:, :WIDTH], gain], axis=1), TP, 8)
    up_q = part_q[:, WIDTH:]
    up_q_other = shift(up_q, "c", 1)
    other_q = shift(mine_q, "c", 1)

    half_rows = ROWS // 2
    far_left = shift(jnp.concatenate([left[:half_rows], other_left[:half_rows]]), "x", 1)
    far_right = shift(jnp.concatenate([right[half_rows:], other_right[half_rows:]]), "x", -1)

    order = jnp.stack([tp_source(a, d) for a, d in SHIFTS])
    blocks = [
        tokens,
        left,
        jnp.concatenate([far_left[:half_rows], far_right[:half_rows]]),
        right,
        other,
        other_left,
        jnp.concatenate([far_left[half_rows:], far_right[half_rows:]]),
        other_right,
    ]
    queries = pl.pallas_call(
        query_kernel,
        out_shape=jax.ShapeDtypeStruct((ROWS, QCOLS), BF),
        in_specs=[pl.BlockSpec(memory_space=pltpu.SMEM)]
        + [pl.BlockSpec(memory_space=pltpu.VMEM)] * 12
        + [pl.BlockSpec(memory_space=pl.ANY)],
        out_specs=pl.BlockSpec(memory_space=pltpu.VMEM),
        scratch_shapes=[pltpu.VMEM((8, WIDTH, QCOLS), BF), pltpu.SemaphoreType.DMA((8,))],
        cost_estimate=pl.CostEstimate(
            flops=2 * ROWS * 8 * WIDTH * QCOLS + 2 * 8 * WIDTH * RANK * QCOLS,
            bytes_accessed=10**7,
            transcendentals=0,
        ),
        compiler_params=pltpu.CompilerParams(vmem_limit_bytes=24 * 1024 * 1024),
    )(order, *blocks, mine_q, other_q, up_q, up_q_other, query_frozen_weight)

    columns = column_piece(output_frozen_weight, rank, tp)
    columns = to_columns(after(columns, far_left, far_right))
    columns = lax.all_gather(columns, CTX, axis=0, tiled=True)
    order_out = jnp.stack([tp ^ i for i in range(8)])

    part_o = spread_ctx(after(pieces_o, queries))
    mine_o = copies(part_o[:, :QCOLS], TP, 8)
    up_o = part_o[:, QCOLS:]
    up_o_other = shift(up_o, "c", 1)
    other_o = shift(mine_o, "c", 1)
    out_merged = merge_out(order_out, columns, mine_o, other_o, up_o, up_o_other)

    counts = jnp.sum(
        (frame_block_number[None, :] <= frame_block_number[:, None]).astype(jnp.int32), axis=1
    )
    vis_end = counts * FTOK
    kframes = (jnp.arange(CHUNKS, dtype=jnp.int32) * 8 + y * 2) * FRAMES_DEV

    def frames_of(step):
        return (zh * 8 + ((y - step) % 4) * 2 + c) * FRAMES_DEV

    q_left = shift(queries, "y", 1)
    q_right = shift(queries, "y", -1)
    q_far = shift(queries, "y", 2)
    (own,) = attention([queries], [frames_of(0)], kframes, vis_end, kv)
    left, right = attention([q_left, q_right], [frames_of(1), frames_of(-1)], kframes, vis_end, kv)
    back_left = shift(left, "y", -1)
    back_right = shift(right, "y", 1)
    (far,) = attention([q_far], [frames_of(2)], kframes, vis_end, kv)
    back_far = shift(far, "y", 2)

    attended = vmem_call(combine_kernel, jax.ShapeDtypeStruct((ROWS, QCOLS), BF), 0, 4, nbytes=10**6)(
        own, back_left, back_right, back_far
    )
    attended = copies(attended, TP, 8)
    return vmem_call(
        project_kernel,
        jax.ShapeDtypeStruct((ROWS, WIDTH), BF),
        1,
        2,
        flops=2 * ROWS * 8 * WIDTH * QCOLS,
        nbytes=10**7,
    )(order_out, attended, out_merged)


def solution(mesh):
    fine = Mesh(mesh.devices.reshape([SIZES[a] for a in AXES]), AXES)
    in_specs = (
        P(CTX, TP),
        P(TP),
        P(CTX, TP),
        P(CTX, TP),
        P(None, TP),
        P(TP, None),
        P(CTX, None, None),
        P(CTX, None, TP),
        P(CTX, TP, None),
        P(CTX, None, None),
        P(),
        P(),
    )
    return jax.shard_map(
        shards, mesh=fine, in_specs=in_specs, out_specs=P(CTX, TP), check_vma=False
    )
```

```python
import functools
import math

import jax
import jax.numpy as jnp
from jax import lax
from jax.experimental import pallas as pl
from jax.experimental.pallas import tpu as pltpu
from jax.sharding import Mesh
from jax.sharding import PartitionSpec as P

HS = 128
FTOK = 64
ROWS = 320
FRAMES_DEV = 5
WIDTH = 768
RANK = 64
HEADS_DEV = 3
QCOLS = HEADS_DEV * HS
CHUNK = 2 * ROWS
CHUNKS = 4
NEG = -1e30
PIECE = 96
EPS = 1e-6
AXES = ("zh", "y", "c", "zl", "x")
SIZES = {"zh": 4, "y": 4, "c": 2, "zl": 2, "x": 4}
CTX = ("zh", "y", "c")
TP = ("zl", "x")
EXP_SCALE = (HS ** (-0.5)) * math.log2(math.e)
BF = jnp.bfloat16
F32 = jnp.float32


def shift(v, axis, step):
    n = SIZES[axis]
    return lax.ppermute(v, axis, [(i, (i + step) % n) for i in range(n)])


def tp_source(a, d):
    return (lax.axis_index("zl") ^ a) * 4 + (lax.axis_index("x") - d) % 4


def vmem_call(body, out_shape, n_smem, n_vmem, scratch=(), flops=0, nbytes=0, mib=16, n_any=0):
    return pl.pallas_call(
        body,
        out_shape=out_shape,
        in_specs=[pl.BlockSpec(memory_space=pltpu.SMEM)] * n_smem
        + [pl.BlockSpec(memory_space=pltpu.VMEM)] * n_vmem
        + [pl.BlockSpec(memory_space=pl.ANY)] * n_any,
        scratch_shapes=list(scratch),
        cost_estimate=pl.CostEstimate(flops=flops, bytes_accessed=nbytes, transcendentals=0),
        compiler_params=pltpu.CompilerParams(vmem_limit_bytes=mib * 1024 * 1024),
    )


def tdot(a, b):
    return lax.dot_general(a, b, (((0,), (0,)), ((), ())), preferred_element_type=F32)


def gain_row(piece, lanes):
    return jnp.concatenate(
        [piece[r : r + 1, lanes : lanes + HS].astype(F32) for r in range(WIDTH // HS)], axis=1
    )


def query_kernel(order_ref, *refs):
    parts = refs[:8]
    mine_ref, other_ref, up_ref, up_other_ref, w_ref, out_ref, held, sems = refs[8:]

    def fetch(i):
        rows = pl.ds(pl.multiple_of(order_ref[i] * WIDTH, WIDTH), WIDTH)
        return pltpu.make_async_copy(w_ref.at[rows, :], held.at[i], sems.at[i])

    for i in range(8):
        fetch(i).start()
    total = jnp.zeros((ROWS, HS), F32)
    for i in range(8):
        v = parts[i][...].astype(F32)
        v = v * v
        for g in range(WIDTH // HS):
            total = total + v[:, g * HS : (g + 1) * HS]
    total = jnp.sum(total, axis=1, keepdims=True)
    inv = lax.rsqrt(total * (1.0 / (8 * WIDTH)) + EPS)
    acc = jnp.zeros((ROWS, QCOLS), F32)
    up = jnp.concatenate([up_ref[:, :QCOLS], up_other_ref[:, :QCOLS]], axis=0)
    for i in range(8):
        at = order_ref[i]
        gain = gain_row(mine_ref.at[at], WIDTH + QCOLS)
        normed = (parts[i][...].astype(F32) * inv * gain).astype(BF)
        down = jnp.concatenate([mine_ref[at, :, :WIDTH], other_ref[at, :, :WIDTH]], axis=0)
        fetch(i).wait()
        merged = (held[i].astype(F32) + tdot(down, up)).astype(BF)
        acc = acc + jnp.dot(normed, merged, preferred_element_type=F32)
    out_ref[...] = acc.astype(BF)


def attention_kernel(n, qframe_ref, kframe_ref, vis_ref, *refs):
    q_refs = refs[:n]
    kv_ref = refs[n]
    o_refs = refs[n + 1 :]
    lane = lax.broadcasted_iota(jnp.int32, (ROWS, HS), 1)
    row = lax.broadcasted_iota(jnp.int32, (ROWS, 1), 0)

    def heads(b, first, chunks):
        width = chunks * CHUNK
        last = kframe_ref[chunks - 1] * FTOK
        limit = jnp.full((ROWS, 1), vis_ref[first] - last, jnp.int32)
        for f in range(1, FRAMES_DEV):
            limit = jnp.where(row >= f * FTOK, vis_ref[first + f] - last, limit)
        seen = lax.broadcasted_iota(jnp.int32, (ROWS, CHUNK), 1) < limit

        def scores(h):
            cols = slice(h * HS, (h + 1) * HS)
            return lax.dot_general(
                q_refs[b][:, cols],
                kv_ref[:width, cols],
                (((1,), (1,)), ((), ())),
                preferred_element_type=F32,
            )

        s = scores(0)
        stats = jnp.zeros((ROWS, HS), F32)
        for h in range(HEADS_DEV):
            ahead = scores(h + 1) if h + 1 < HEADS_DEV else None
            tail = jnp.where(seen, s[:, width - CHUNK :], NEG)
            s = jnp.concatenate([s[:, : width - CHUNK], tail], axis=1) if chunks > 1 else tail
            top = jnp.max(s, axis=1, keepdims=True)
            p = jnp.exp2((s - top) * EXP_SCALE)
            lanes = p[:, :HS]
            for g in range(1, width // HS):
                lanes = lanes + p[:, g * HS : (g + 1) * HS]
            total = jnp.sum(lanes, axis=1, keepdims=True)
            acc = jnp.dot(
                p.astype(BF),
                kv_ref[:width, QCOLS + h * HS : QCOLS + (h + 1) * HS],
                preferred_element_type=F32,
            )
            has = top > 0.5 * NEG
            o_refs[b][:, h * HS : (h + 1) * HS] = jnp.where(has, acc / total, 0.0).astype(BF)
            level = jnp.where(has, top * EXP_SCALE + jnp.log2(total), NEG)
            high = level.astype(BF).astype(F32)
            mid = (level - high).astype(BF).astype(F32)
            low = level - high - mid
            stats = jnp.where(lane == 3 * h, high, stats)
            stats = jnp.where(lane == 3 * h + 1, mid, stats)
            stats = jnp.where(lane == 3 * h + 2, low, stats)
            s = ahead
        o_refs[b][:, QCOLS:] = stats.astype(BF)

    for b in range(n):
        first = qframe_ref[b]
        end = vis_ref[first + FRAMES_DEV - 1]
        some = jnp.int32(0)
        for j in range(CHUNKS):
            some = some + (kframe_ref[j] * FTOK < end).astype(jnp.int32)

        @pl.when(some == 0)
        def _(b=b):
            o_refs[b][:, :QCOLS] = jnp.zeros((ROWS, QCOLS), BF)
            blank = jnp.where((lane < 3 * HEADS_DEV) & (lane % 3 == 0), NEG, 0.0)
            o_refs[b][:, QCOLS:] = blank.astype(BF)

        for chunks in range(1, CHUNKS + 1):

            @pl.when(some == chunks)
            def _(b=b, first=first, chunks=chunks):
                heads(b, first, chunks)


def attention(queries, qframes, kframes, vis_end, kv):
    n = len(queries)
    return vmem_call(
        functools.partial(attention_kernel, n),
        [jax.ShapeDtypeStruct((ROWS, QCOLS + HS), BF)] * n,
        3,
        n + 1,
        flops=n * 8 * ROWS * QCOLS * CHUNK * CHUNKS,
        nbytes=CHUNKS * CHUNK * 2 * QCOLS * 2,
        mib=32,
    )(jnp.stack(qframes), kframes, vis_end, *queries, kv)


def combine_kernel(*refs):
    parts, out_ref = refs[:4], refs[4]
    stats = [p[:, QCOLS:].astype(F32) for p in parts]
    for h in range(HEADS_DEV):
        levels = []
        for s in stats:
            levels.append(
                s[:, 3 * h : 3 * h + 1] + s[:, 3 * h + 1 : 3 * h + 2] + s[:, 3 * h + 2 : 3 * h + 3]
            )
        top = functools.reduce(jnp.maximum, levels)
        shares = [jnp.exp2(v - top) for v in levels]
        total = shares[0] + shares[1] + shares[2] + shares[3]
        cols = slice(h * HS, (h + 1) * HS)
        acc = jnp.zeros((ROWS, HS), F32)
        for p, w in zip(parts, shares):
            acc = acc + p[:, cols].astype(F32) * w
        out_ref[:, cols] = (acc / total).astype(BF)


def merge_out_kernel(order_ref, w_ref, mine_ref, other_ref, up_ref, up_other_ref, out_ref):
    at = order_ref[pl.program_id(0)]
    up = jnp.concatenate([up_ref[:, QCOLS:], up_other_ref[:, QCOLS:]], axis=0)
    cols = slice(WIDTH, WIDTH + QCOLS)
    down = jnp.concatenate([mine_ref[at, :, cols], other_ref[at, :, cols]], axis=0)
    out_ref[...] = (w_ref[...].astype(F32) + tdot(down, up)).astype(BF)


def merge_out(order, w, mine, other, up, up_other):
    def whole(shape):
        return pl.BlockSpec(shape, lambda i: (0,) * len(shape))

    return pl.pallas_call(
        merge_out_kernel,
        out_shape=jax.ShapeDtypeStruct((8 * QCOLS, WIDTH), BF),
        grid=(8,),
        in_specs=[
            pl.BlockSpec(memory_space=pltpu.SMEM),
            pl.BlockSpec((QCOLS, WIDTH), lambda i: (i, 0)),
            whole(mine.shape),
            whole(other.shape),
            whole(up.shape),
            whole(up_other.shape),
        ],
        out_specs=pl.BlockSpec((QCOLS, WIDTH), lambda i: (i, 0)),
        cost_estimate=pl.CostEstimate(
            flops=2 * 8 * WIDTH * RANK * QCOLS, bytes_accessed=10**7, transcendentals=0
        ),
        compiler_params=pltpu.CompilerParams(vmem_limit_bytes=16 * 1024 * 1024),
    )(order, w, mine, other, up, up_other)


def project_kernel(order_ref, a_ref, w_ref, out_ref):
    acc = jnp.zeros((ROWS, WIDTH), F32)
    for i in range(8):
        acc = acc + jnp.dot(
            a_ref[order_ref[i]],
            w_ref[i * QCOLS : (i + 1) * QCOLS, :],
            preferred_element_type=F32,
        )
    out_ref[...] = acc.astype(BF)


def after(value, *others):
    return lax.optimization_barrier((value,) + others)[0]


def prep_kernel(scal_ref, down_q_ref, down_o_ref, up_q_ref, up_o_ref, out_ref):
    start = 0
    for i, ref in ((0, down_q_ref), (2, down_o_ref), (1, up_q_ref), (3, up_o_ref)):
        width = ref.shape[1]
        mine = scal_ref[1 + i] == scal_ref[0]
        out_ref[:, start : start + width] = jnp.where(mine, ref[...].astype(F32), 0.0).astype(BF)
        start += width


def prepare(rank, tp, owners, down_q, down_o, up_q, up_o):
    scal = jnp.concatenate([rank[None], owners, tp[None]]).astype(jnp.int32)
    width = 2 * (WIDTH + QCOLS)
    return pl.pallas_call(
        prep_kernel,
        out_shape=jax.ShapeDtypeStruct((RANK, width), BF),
        grid_spec=pltpu.PrefetchScalarGridSpec(
            num_scalar_prefetch=1,
            grid=(1,),
            in_specs=[
                pl.BlockSpec((RANK, WIDTH), lambda i, sc: (0, sc[5])),
                pl.BlockSpec((RANK, QCOLS), lambda i, sc: (0, 0)),
                pl.BlockSpec((RANK, QCOLS), lambda i, sc: (0, 0)),
                pl.BlockSpec((RANK, WIDTH), lambda i, sc: (0, sc[5])),
            ],
            out_specs=pl.BlockSpec((RANK, width), lambda i, sc: (0, 0)),
        ),
        cost_estimate=pl.CostEstimate(flops=0, bytes_accessed=10**6, transcendentals=0),
        compiler_params=pltpu.CompilerParams(vmem_limit_bytes=16 * 1024 * 1024),
    )(scal, down_q, down_o, up_q, up_o)


def copies(piece, axis, n):
    everywhere = jnp.broadcast_to(piece[None], (n,) + piece.shape)
    return lax.all_to_all(everywhere, axis, 0, 0)


def spread(part, axis):
    got = copies(part, axis, SIZES[axis])
    return got[0] + got[1] + got[2] + got[3]


def column_piece(weight, rank, tp):
    piece = lax.dynamic_slice(
        weight, ((rank % 4) * PIECE, (tp ^ (rank // 4)) * WIDTH), (PIECE, WIDTH)
    )
    return piece


def to_columns(piece):
    pairs = []
    for r in range(32):
        for t in range(8):
            pairs.append((r * 8 + t, r * 8 + (t ^ (r // 4))))
    return lax.ppermute(piece, AXES, pairs)


SHIFTS = [(a, d) for a in range(2) for d in range(4)]


def shards(
    tokens,
    norm_gain_vector,
    keys,
    values,
    query_frozen_weight,
    output_frozen_weight,
    query_update_first,
    query_update_second,
    output_update_first,
    output_update_second,
    owners,
    frame_block_number,
):
    zh, y, c = (lax.axis_index(a) for a in CTX)
    tp = lax.axis_index("zl") * 4 + lax.axis_index("x")
    rank = zh * 8 + y * 2 + c

    left = shift(tokens, "x", 1)
    right = shift(tokens, "x", -1)
    other = shift(tokens, "zl", 1)

    half = RANK // 2
    factors = prepare(
        rank,
        tp,
        owners,
        query_update_first[0].T,
        output_update_first[0].T,
        query_update_second[0],
        output_update_second[0],
    )
    factors = factors + shift(factors, "c", 1)
    part = lax.dynamic_slice_in_dim(factors, c * half, half, 0)
    part = spread(after(part, left, right, other), "zh")

    kv = jnp.concatenate([keys, values], axis=1)
    kv = lax.all_gather(after(kv, other, part), ("zh", "c"), axis=0, tiled=True)

    other_left = shift(other, "x", 1)
    other_right = shift(other, "x", -1)
    part = spread(after(part, other_left, other_right), "y")

    half_rows = ROWS // 2
    far_left = shift(jnp.concatenate([left[:half_rows], other_left[:half_rows]]), "x", 1)
    far_right = shift(jnp.concatenate([right[half_rows:], other_right[half_rows:]]), "x", -1)

    gain = jnp.pad(norm_gain_vector.reshape(WIDTH // HS, HS), ((0, half - WIDTH // HS), (0, 0)))
    down = jnp.concatenate([part[:, : WIDTH + QCOLS], gain], axis=1)
    mine = copies(after(down, far_left, far_right), TP, 8)
    ups = part[:, WIDTH + QCOLS :]
    ups_other = shift(ups, "c", 1)
    theirs = shift(mine, "c", 1)

    order = jnp.stack([tp_source(a, d) for a, d in SHIFTS])
    blocks = [
        tokens,
        left,
        jnp.concatenate([far_left[:half_rows], far_right[:half_rows]]),
        right,
        other,
        other_left,
        jnp.concatenate([far_left[half_rows:], far_right[half_rows:]]),
        other_right,
    ]
    queries = pl.pallas_call(
        query_kernel,
        out_shape=jax.ShapeDtypeStruct((ROWS, QCOLS), BF),
        in_specs=[pl.BlockSpec(memory_space=pltpu.SMEM)]
        + [pl.BlockSpec(memory_space=pltpu.VMEM)] * 12
        + [pl.BlockSpec(memory_space=pl.ANY)],
        out_specs=pl.BlockSpec(memory_space=pltpu.VMEM),
        scratch_shapes=[pltpu.VMEM((8, WIDTH, QCOLS), BF), pltpu.SemaphoreType.DMA((8,))],
        cost_estimate=pl.CostEstimate(
            flops=2 * ROWS * 8 * WIDTH * QCOLS + 2 * 8 * WIDTH * RANK * QCOLS,
            bytes_accessed=10**7,
            transcendentals=0,
        ),
        compiler_params=pltpu.CompilerParams(vmem_limit_bytes=24 * 1024 * 1024),
    )(order, *blocks, mine, theirs, ups, ups_other, query_frozen_weight)

    columns = column_piece(output_frozen_weight, rank, tp)
    columns = to_columns(after(columns, mine))
    columns = lax.all_gather(columns, CTX, axis=0, tiled=True)
    order_out = jnp.stack([tp ^ i for i in range(8)])

    out_merged = merge_out(order_out, columns, mine, theirs, ups, ups_other)

    counts = jnp.sum(
        (frame_block_number[None, :] <= frame_block_number[:, None]).astype(jnp.int32), axis=1
    )
    vis_end = counts * FTOK
    kframes = (jnp.arange(CHUNKS, dtype=jnp.int32) * 8 + y * 2) * FRAMES_DEV

    def frames_of(step):
        return (zh * 8 + ((y - step) % 4) * 2 + c) * FRAMES_DEV

    q_left = shift(queries, "y", 1)
    q_right = shift(queries, "y", -1)
    q_far = shift(queries, "y", 2)
    (own,) = attention([queries], [frames_of(0)], kframes, vis_end, kv)
    left, right = attention([q_left, q_right], [frames_of(1), frames_of(-1)], kframes, vis_end, kv)
    back_left = shift(left, "y", -1)
    back_right = shift(right, "y", 1)
    (far,) = attention([q_far], [frames_of(2)], kframes, vis_end, kv)
    back_far = shift(far, "y", 2)

    attended = vmem_call(combine_kernel, jax.ShapeDtypeStruct((ROWS, QCOLS), BF), 0, 4, nbytes=10**6)(
        own, back_left, back_right, back_far
    )
    attended = copies(attended, TP, 8)
    return vmem_call(
        project_kernel,
        jax.ShapeDtypeStruct((ROWS, WIDTH), BF),
        1,
        2,
        flops=2 * ROWS * 8 * WIDTH * QCOLS,
        nbytes=10**7,
    )(order_out, attended, out_merged)


def solution(mesh):
    fine = Mesh(mesh.devices.reshape([SIZES[a] for a in AXES]), AXES)
    in_specs = (
        P(CTX, TP),
        P(TP),
        P(CTX, TP),
        P(CTX, TP),
        P(None, TP),
        P(TP, None),
        P(CTX, None, None),
        P(CTX, None, TP),
        P(CTX, TP, None),
        P(CTX, None, None),
        P(),
        P(),
    )
    return jax.shard_map(
        shards, mesh=fine, in_specs=in_specs, out_specs=P(CTX, TP), check_vma=False
    )
```

```python
import functools
import math

import jax
import jax.numpy as jnp
from jax import lax
from jax.experimental import pallas as pl
from jax.experimental.pallas import tpu as pltpu
from jax.sharding import Mesh
from jax.sharding import PartitionSpec as P

HS = 128
FTOK = 64
ROWS = 320
FRAMES_DEV = 5
WIDTH = 768
RANK = 64
HEADS_DEV = 3
QCOLS = HEADS_DEV * HS
CHUNK = 2 * ROWS
CHUNKS = 4
NEG = -1e30
PIECE = 96
EPS = 1e-6
AXES = ("zh", "y", "c", "zl", "x")
SIZES = {"zh": 4, "y": 4, "c": 2, "zl": 2, "x": 4}
CTX = ("zh", "y", "c")
TP = ("zl", "x")
EXP_SCALE = (HS ** (-0.5)) * math.log2(math.e)
BF = jnp.bfloat16
F32 = jnp.float32


def shift(v, axis, step):
    n = SIZES[axis]
    return lax.ppermute(v, axis, [(i, (i + step) % n) for i in range(n)])


def tp_source(a, d):
    return (lax.axis_index("zl") ^ a) * 4 + (lax.axis_index("x") - d) % 4


def vmem_call(body, out_shape, n_smem, n_vmem, scratch=(), flops=0, nbytes=0, mib=16, n_any=0):
    return pl.pallas_call(
        body,
        out_shape=out_shape,
        in_specs=[pl.BlockSpec(memory_space=pltpu.SMEM)] * n_smem
        + [pl.BlockSpec(memory_space=pltpu.VMEM)] * n_vmem
        + [pl.BlockSpec(memory_space=pl.ANY)] * n_any,
        scratch_shapes=list(scratch),
        cost_estimate=pl.CostEstimate(flops=flops, bytes_accessed=nbytes, transcendentals=0),
        compiler_params=pltpu.CompilerParams(vmem_limit_bytes=mib * 1024 * 1024),
    )


def tdot(a, b):
    return lax.dot_general(a, b, (((0,), (0,)), ((), ())), preferred_element_type=F32)


def gain_row(piece, lanes):
    return jnp.concatenate(
        [piece[r : r + 1, lanes : lanes + HS].astype(F32) for r in range(WIDTH // HS)], axis=1
    )


def query_kernel(order_ref, *refs):
    parts = refs[:8]
    mine_ref, other_ref, up_ref, up_other_ref, w_ref, out_ref, held, sems = refs[8:]
    half = ROWS // 2

    def block(i):
        if i in (2, 6):
            rows = slice(0, half) if i == 2 else slice(half, ROWS)
            return jnp.concatenate([parts[2][rows, :], parts[6][rows, :]], axis=0)
        return parts[i][...]

    def fetch(i):
        rows = pl.ds(pl.multiple_of(order_ref[i] * WIDTH, WIDTH), WIDTH)
        return pltpu.make_async_copy(w_ref.at[rows, :], held.at[i], sems.at[i])

    for i in range(8):
        fetch(i).start()
    total = jnp.zeros((ROWS, HS), F32)
    for i in range(8):
        v = block(i).astype(F32)
        v = v * v
        for g in range(WIDTH // HS):
            total = total + v[:, g * HS : (g + 1) * HS]
    total = jnp.sum(total, axis=1, keepdims=True)
    inv = lax.rsqrt(total * (1.0 / (8 * WIDTH)) + EPS)
    acc = jnp.zeros((ROWS, QCOLS), F32)
    up = jnp.concatenate([up_ref[:, :QCOLS], up_other_ref[:, :QCOLS]], axis=0)
    for i in range(8):
        at = order_ref[i]
        gain = gain_row(mine_ref.at[at], WIDTH + QCOLS)
        normed = (block(i).astype(F32) * inv * gain).astype(BF)
        down = jnp.concatenate([mine_ref[at, :, :WIDTH], other_ref[at, :, :WIDTH]], axis=0)
        fetch(i).wait()
        merged = (held[i].astype(F32) + tdot(down, up)).astype(BF)
        acc = acc + jnp.dot(normed, merged, preferred_element_type=F32)
    out_ref[...] = acc.astype(BF)


def attention_kernel(n, qframe_ref, kframe_ref, vis_ref, *refs):
    q_refs = refs[:n]
    kv_ref = refs[n]
    o_refs = refs[n + 1 :]
    lane = lax.broadcasted_iota(jnp.int32, (ROWS, HS), 1)
    row = lax.broadcasted_iota(jnp.int32, (ROWS, 1), 0)

    def heads(b, first, chunks):
        width = chunks * CHUNK
        last = kframe_ref[chunks - 1] * FTOK
        limit = jnp.full((ROWS, 1), vis_ref[first] - last, jnp.int32)
        for f in range(1, FRAMES_DEV):
            limit = jnp.where(row >= f * FTOK, vis_ref[first + f] - last, limit)
        seen = lax.broadcasted_iota(jnp.int32, (ROWS, CHUNK), 1) < limit

        def scores(h):
            cols = slice(h * HS, (h + 1) * HS)
            return lax.dot_general(
                q_refs[b][:, cols],
                kv_ref[:width, cols],
                (((1,), (1,)), ((), ())),
                preferred_element_type=F32,
            )

        s = scores(0)
        stats = jnp.zeros((ROWS, HS), F32)
        for h in range(HEADS_DEV):
            ahead = scores(h + 1) if h + 1 < HEADS_DEV else None
            tail = jnp.where(seen, s[:, width - CHUNK :], NEG)
            s = jnp.concatenate([s[:, : width - CHUNK], tail], axis=1) if chunks > 1 else tail
            top = jnp.max(s, axis=1, keepdims=True)
            p = jnp.exp2((s - top) * EXP_SCALE)
            lanes = p[:, :HS]
            for g in range(1, width // HS):
                lanes = lanes + p[:, g * HS : (g + 1) * HS]
            total = jnp.sum(lanes, axis=1, keepdims=True)
            acc = jnp.dot(
                p.astype(BF),
                kv_ref[:width, QCOLS + h * HS : QCOLS + (h + 1) * HS],
                preferred_element_type=F32,
            )
            has = top > 0.5 * NEG
            o_refs[b][:, h * HS : (h + 1) * HS] = jnp.where(has, acc / total, 0.0).astype(BF)
            level = jnp.where(has, top * EXP_SCALE + jnp.log2(total), NEG)
            high = level.astype(BF).astype(F32)
            mid = (level - high).astype(BF).astype(F32)
            low = level - high - mid
            stats = jnp.where(lane == 3 * h, high, stats)
            stats = jnp.where(lane == 3 * h + 1, mid, stats)
            stats = jnp.where(lane == 3 * h + 2, low, stats)
            s = ahead
        o_refs[b][:, QCOLS:] = stats.astype(BF)

    for b in range(n):
        first = qframe_ref[b]
        end = vis_ref[first + FRAMES_DEV - 1]
        some = jnp.int32(0)
        for j in range(CHUNKS):
            some = some + (kframe_ref[j] * FTOK < end).astype(jnp.int32)

        @pl.when(some == 0)
        def _(b=b):
            o_refs[b][:, :QCOLS] = jnp.zeros((ROWS, QCOLS), BF)
            blank = jnp.where((lane < 3 * HEADS_DEV) & (lane % 3 == 0), NEG, 0.0)
            o_refs[b][:, QCOLS:] = blank.astype(BF)

        for chunks in range(1, CHUNKS + 1):

            @pl.when(some == chunks)
            def _(b=b, first=first, chunks=chunks):
                heads(b, first, chunks)


def attention(queries, qframes, kframes, vis_end, kv):
    n = len(queries)
    return vmem_call(
        functools.partial(attention_kernel, n),
        [jax.ShapeDtypeStruct((ROWS, QCOLS + HS), BF)] * n,
        3,
        n + 1,
        flops=n * 8 * ROWS * QCOLS * CHUNK * CHUNKS,
        nbytes=CHUNKS * CHUNK * 2 * QCOLS * 2,
        mib=32,
    )(jnp.stack(qframes), kframes, vis_end, *queries, kv)


def combine_kernel(*refs):
    parts, out_ref = refs[:4], refs[4]
    stats = [p[:, QCOLS:].astype(F32) for p in parts]
    for h in range(HEADS_DEV):
        levels = []
        for s in stats:
            levels.append(
                s[:, 3 * h : 3 * h + 1] + s[:, 3 * h + 1 : 3 * h + 2] + s[:, 3 * h + 2 : 3 * h + 3]
            )
        top = functools.reduce(jnp.maximum, levels)
        shares = [jnp.exp2(v - top) for v in levels]
        total = shares[0] + shares[1] + shares[2] + shares[3]
        cols = slice(h * HS, (h + 1) * HS)
        acc = jnp.zeros((ROWS, HS), F32)
        for p, w in zip(parts, shares):
            acc = acc + p[:, cols].astype(F32) * w
        out_ref[:, cols] = (acc / total).astype(BF)


def merge_out_kernel(order_ref, w_ref, mine_ref, other_ref, up_ref, up_other_ref, out_ref):
    at = order_ref[pl.program_id(0)]
    up = jnp.concatenate([up_ref[:, QCOLS:], up_other_ref[:, QCOLS:]], axis=0)
    cols = slice(WIDTH, WIDTH + QCOLS)
    down = jnp.concatenate([mine_ref[at, :, cols], other_ref[at, :, cols]], axis=0)
    out_ref[...] = (w_ref[...].astype(F32) + tdot(down, up)).astype(BF)


def merge_out(order, w, mine, other, up, up_other):
    def whole(shape):
        return pl.BlockSpec(shape, lambda i: (0,) * len(shape))

    return pl.pallas_call(
        merge_out_kernel,
        out_shape=jax.ShapeDtypeStruct((8 * QCOLS, WIDTH), BF),
        grid=(8,),
        in_specs=[
            pl.BlockSpec(memory_space=pltpu.SMEM),
            pl.BlockSpec((QCOLS, WIDTH), lambda i: (i, 0)),
            whole(mine.shape),
            whole(other.shape),
            whole(up.shape),
            whole(up_other.shape),
        ],
        out_specs=pl.BlockSpec((QCOLS, WIDTH), lambda i: (i, 0)),
        cost_estimate=pl.CostEstimate(
            flops=2 * 8 * WIDTH * RANK * QCOLS, bytes_accessed=10**7, transcendentals=0
        ),
        compiler_params=pltpu.CompilerParams(vmem_limit_bytes=16 * 1024 * 1024),
    )(order, w, mine, other, up, up_other)


def project_kernel(order_ref, a_ref, w_ref, out_ref):
    acc = jnp.zeros((ROWS, WIDTH), F32)
    for i in range(8):
        acc = acc + jnp.dot(
            a_ref[order_ref[i]],
            w_ref[i * QCOLS : (i + 1) * QCOLS, :],
            preferred_element_type=F32,
        )
    out_ref[...] = acc.astype(BF)


def after(value, *others):
    return lax.optimization_barrier((value,) + others)[0]


def prep_kernel(scal_ref, down_q_ref, down_o_ref, up_q_ref, up_o_ref, out_ref):
    start = 0
    for i, ref in ((0, down_q_ref), (2, down_o_ref), (1, up_q_ref), (3, up_o_ref)):
        width = ref.shape[1]
        mine = scal_ref[1 + i] == scal_ref[0]
        out_ref[:, start : start + width] = jnp.where(mine, ref[...].astype(F32), 0.0).astype(BF)
        start += width


def prepare(rank, tp, owners, down_q, down_o, up_q, up_o):
    scal = jnp.concatenate([rank[None], owners, tp[None]]).astype(jnp.int32)
    width = 2 * (WIDTH + QCOLS)
    return pl.pallas_call(
        prep_kernel,
        out_shape=jax.ShapeDtypeStruct((RANK, width), BF),
        grid_spec=pltpu.PrefetchScalarGridSpec(
            num_scalar_prefetch=1,
            grid=(1,),
            in_specs=[
                pl.BlockSpec((RANK, WIDTH), lambda i, sc: (0, sc[5])),
                pl.BlockSpec((RANK, QCOLS), lambda i, sc: (0, 0)),
                pl.BlockSpec((RANK, QCOLS), lambda i, sc: (0, 0)),
                pl.BlockSpec((RANK, WIDTH), lambda i, sc: (0, sc[5])),
            ],
            out_specs=pl.BlockSpec((RANK, width), lambda i, sc: (0, 0)),
        ),
        cost_estimate=pl.CostEstimate(flops=0, bytes_accessed=10**6, transcendentals=0),
        compiler_params=pltpu.CompilerParams(vmem_limit_bytes=16 * 1024 * 1024),
    )(scal, down_q, down_o, up_q, up_o)


def copies(piece, axis, n):
    everywhere = jnp.broadcast_to(piece[None], (n,) + piece.shape)
    return lax.all_to_all(everywhere, axis, 0, 0)


def spread(part, axis):
    got = copies(part, axis, SIZES[axis])
    return got[0] + got[1] + got[2] + got[3]


def column_piece(weight, rank, tp):
    piece = lax.dynamic_slice(
        weight, ((rank % 4) * PIECE, (tp ^ (rank // 4)) * WIDTH), (PIECE, WIDTH)
    )
    return piece


def to_columns(piece):
    pairs = []
    for r in range(32):
        for t in range(8):
            pairs.append((r * 8 + t, r * 8 + (t ^ (r // 4))))
    return lax.ppermute(piece, AXES, pairs)


SHIFTS = [(a, d) for a in range(2) for d in range(4)]


def shards(
    tokens,
    norm_gain_vector,
    keys,
    values,
    query_frozen_weight,
    output_frozen_weight,
    query_update_first,
    query_update_second,
    output_update_first,
    output_update_second,
    owners,
    frame_block_number,
):
    zh, y, c = (lax.axis_index(a) for a in CTX)
    tp = lax.axis_index("zl") * 4 + lax.axis_index("x")
    rank = zh * 8 + y * 2 + c

    left = shift(tokens, "x", 1)
    right = shift(tokens, "x", -1)
    other = shift(tokens, "zl", 1)

    half = RANK // 2
    factors = prepare(
        rank,
        tp,
        owners,
        query_update_first[0].T,
        output_update_first[0].T,
        query_update_second[0],
        output_update_second[0],
    )
    factors = factors + shift(factors, "c", 1)
    part = lax.dynamic_slice_in_dim(factors, c * half, half, 0)
    part = spread(part, "zh")

    kv = jnp.concatenate([keys, values], axis=1)
    kv = lax.all_gather(after(kv, other), ("zh", "c"), axis=0, tiled=True)

    half_rows = ROWS // 2
    other_left = shift(other, "x", 1)
    other_right = shift(other, "x", -1)
    far_left = shift(jnp.concatenate([left[:half_rows], other_left[:half_rows]]), "x", 1)
    far_right = shift(jnp.concatenate([right[half_rows:], other_right[half_rows:]]), "x", -1)
    part = spread(after(part, far_left, far_right), "y")

    gain = jnp.pad(norm_gain_vector.reshape(WIDTH // HS, HS), ((0, half - WIDTH // HS), (0, 0)))
    down = jnp.concatenate([part[:, : WIDTH + QCOLS], gain], axis=1)
    mine = copies(down, TP, 8)
    ups = part[:, WIDTH + QCOLS :]
    ups_other = shift(ups, "c", 1)
    theirs = shift(mine, "c", 1)

    order = jnp.stack([tp_source(a, d) for a, d in SHIFTS])
    blocks = [tokens, left, far_left, right, other, other_left, far_right, other_right]
    queries = pl.pallas_call(
        query_kernel,
        out_shape=jax.ShapeDtypeStruct((ROWS, QCOLS), BF),
        in_specs=[pl.BlockSpec(memory_space=pltpu.SMEM)]
        + [pl.BlockSpec(memory_space=pltpu.VMEM)] * 12
        + [pl.BlockSpec(memory_space=pltpu.HBM)],
        out_specs=pl.BlockSpec(memory_space=pltpu.VMEM),
        scratch_shapes=[pltpu.VMEM((8, WIDTH, QCOLS), BF), pltpu.SemaphoreType.DMA((8,))],
        cost_estimate=pl.CostEstimate(
            flops=2 * ROWS * 8 * WIDTH * QCOLS + 2 * 8 * WIDTH * RANK * QCOLS,
            bytes_accessed=10**7,
            transcendentals=0,
        ),
        compiler_params=pltpu.CompilerParams(vmem_limit_bytes=24 * 1024 * 1024),
    )(order, *blocks, mine, theirs, ups, ups_other, query_frozen_weight)

    columns = column_piece(output_frozen_weight, rank, tp)
    columns = to_columns(after(columns, far_left, far_right))
    columns = lax.all_gather(columns, CTX, axis=0, tiled=True)
    order_out = jnp.stack([tp ^ i for i in range(8)])

    out_merged = merge_out(order_out, columns, mine, theirs, ups, ups_other)

    counts = jnp.sum(
        (frame_block_number[None, :] <= frame_block_number[:, None]).astype(jnp.int32), axis=1
    )
    vis_end = counts * FTOK
    kframes = (jnp.arange(CHUNKS, dtype=jnp.int32) * 8 + y * 2) * FRAMES_DEV

    def frames_of(step):
        return (zh * 8 + ((y - step) % 4) * 2 + c) * FRAMES_DEV

    q_left = shift(queries, "y", 1)
    q_right = shift(queries, "y", -1)
    q_far = shift(queries, "y", 2)
    (left,) = attention([q_left], [frames_of(1)], kframes, vis_end, kv)
    back_left = shift(left, "y", -1)
    (right,) = attention([q_right], [frames_of(-1)], kframes, vis_end, kv)
    back_right = shift(right, "y", 1)
    (far,) = attention([q_far], [frames_of(2)], kframes, vis_end, kv)
    back_far = shift(far, "y", 2)
    (own,) = attention([queries], [frames_of(0)], kframes, vis_end, kv)

    attended = vmem_call(combine_kernel, jax.ShapeDtypeStruct((ROWS, QCOLS), BF), 0, 4, nbytes=10**6)(
        own, back_left, back_right, back_far
    )
    attended = copies(attended, TP, 8)
    return vmem_call(
        project_kernel,
        jax.ShapeDtypeStruct((ROWS, WIDTH), BF),
        1,
        2,
        flops=2 * ROWS * 8 * WIDTH * QCOLS,
        nbytes=10**7,
    )(order_out, attended, out_merged)


def solution(mesh):
    fine = Mesh(mesh.devices.reshape([SIZES[a] for a in AXES]), AXES)
    in_specs = (
        P(CTX, TP),
        P(TP),
        P(CTX, TP),
        P(CTX, TP),
        P(None, TP),
        P(TP, None),
        P(CTX, None, None),
        P(CTX, None, TP),
        P(CTX, TP, None),
        P(CTX, None, None),
        P(),
        P(),
    )
    return jax.shard_map(
        shards, mesh=fine, in_specs=in_specs, out_specs=P(CTX, TP), check_vma=False
    )
```

```python
import functools
import math

import jax
import jax.numpy as jnp
from jax import lax
from jax.experimental import pallas as pl
from jax.experimental.pallas import tpu as pltpu
from jax.sharding import Mesh
from jax.sharding import PartitionSpec as P

HS = 128
FTOK = 64
ROWS = 320
FRAMES_DEV = 5
WIDTH = 768
RANK = 64
HEADS_DEV = 3
QCOLS = HEADS_DEV * HS
CHUNK = 2 * ROWS
CHUNKS = 4
NEG = -1e30
PIECE = 96
EPS = 1e-6
AXES = ("zh", "y", "c", "zl", "x")
SIZES = {"zh": 4, "y": 4, "c": 2, "zl": 2, "x": 4}
CTX = ("zh", "y", "c")
TP = ("zl", "x")
EXP_SCALE = (HS ** (-0.5)) * math.log2(math.e)
BF = jnp.bfloat16
F32 = jnp.float32


def shift(v, axis, step):
    n = SIZES[axis]
    return lax.ppermute(v, axis, [(i, (i + step) % n) for i in range(n)])


def tp_source(a, d):
    return (lax.axis_index("zl") ^ a) * 4 + (lax.axis_index("x") - d) % 4


def vmem_call(body, out_shape, n_smem, n_vmem, scratch=(), flops=0, nbytes=0, mib=16, n_any=0):
    return pl.pallas_call(
        body,
        out_shape=out_shape,
        in_specs=[pl.BlockSpec(memory_space=pltpu.SMEM)] * n_smem
        + [pl.BlockSpec(memory_space=pltpu.VMEM)] * n_vmem
        + [pl.BlockSpec(memory_space=pl.ANY)] * n_any,
        scratch_shapes=list(scratch),
        cost_estimate=pl.CostEstimate(flops=flops, bytes_accessed=nbytes, transcendentals=0),
        compiler_params=pltpu.CompilerParams(vmem_limit_bytes=mib * 1024 * 1024),
    )


def tdot(a, b):
    return lax.dot_general(a, b, (((0,), (0,)), ((), ())), preferred_element_type=F32)


def gain_row(piece, lanes):
    return jnp.concatenate(
        [piece[r : r + 1, lanes : lanes + HS].astype(F32) for r in range(WIDTH // HS)], axis=1
    )


def query_kernel(order_ref, *refs):
    parts = refs[:8]
    mine_ref, other_ref, up_ref, up_other_ref, w_ref, out_ref, tok, held, tok_sems, sems = refs[8:]
    half = ROWS // 2

    token_copies = []
    for i in range(8):
        if i in (2, 6):
            rows = slice(0, half) if i == 2 else slice(half, ROWS)
            for k, side in enumerate((2, 6)):
                token_copies.append(
                    pltpu.make_async_copy(
                        parts[side].at[rows, :],
                        tok.at[i, k * half : (k + 1) * half, :],
                        tok_sems.at[i + 8 * k],
                    )
                )
        else:
            token_copies.append(pltpu.make_async_copy(parts[i], tok.at[i], tok_sems.at[i]))
    for copy in token_copies:
        copy.start()
    weight_copies = []
    for i in range(8):
        rows = pl.ds(pl.multiple_of(order_ref[i] * WIDTH, WIDTH), WIDTH)
        weight_copies.append(pltpu.make_async_copy(w_ref.at[rows, :], held.at[i], sems.at[i]))
        weight_copies[i].start()
    for copy in token_copies:
        copy.wait()

    total = jnp.zeros((ROWS, HS), F32)
    for i in range(8):
        v = tok[i].astype(F32)
        v = v * v
        for g in range(WIDTH // HS):
            total = total + v[:, g * HS : (g + 1) * HS]
    total = jnp.sum(total, axis=1, keepdims=True)
    inv = lax.rsqrt(total * (1.0 / (8 * WIDTH)) + EPS)
    acc = jnp.zeros((ROWS, QCOLS), F32)
    up = jnp.concatenate([up_ref[:, :QCOLS], up_other_ref[:, :QCOLS]], axis=0)
    for i in range(8):
        at = order_ref[i]
        gain = gain_row(mine_ref.at[at], WIDTH + QCOLS)
        normed = (tok[i].astype(F32) * inv * gain).astype(BF)
        down = jnp.concatenate([mine_ref[at, :, :WIDTH], other_ref[at, :, :WIDTH]], axis=0)
        weight_copies[i].wait()
        merged = (held[i].astype(F32) + tdot(down, up)).astype(BF)
        acc = acc + jnp.dot(normed, merged, preferred_element_type=F32)
    out_ref[...] = acc.astype(BF)


def attention_kernel(n, qframe_ref, kframe_ref, vis_ref, *refs):
    q_refs = refs[:n]
    kv_ref = refs[n]
    o_refs = refs[n + 1 :]
    lane = lax.broadcasted_iota(jnp.int32, (ROWS, HS), 1)
    row = lax.broadcasted_iota(jnp.int32, (ROWS, 1), 0)

    def heads(b, first, chunks):
        width = chunks * CHUNK
        last = kframe_ref[chunks - 1] * FTOK
        limit = jnp.full((ROWS, 1), vis_ref[first] - last, jnp.int32)
        for f in range(1, FRAMES_DEV):
            limit = jnp.where(row >= f * FTOK, vis_ref[first + f] - last, limit)
        seen = lax.broadcasted_iota(jnp.int32, (ROWS, CHUNK), 1) < limit

        def scores(h):
            cols = slice(h * HS, (h + 1) * HS)
            return lax.dot_general(
                q_refs[b][:, cols],
                kv_ref[:width, cols],
                (((1,), (1,)), ((), ())),
                preferred_element_type=F32,
            )

        s = scores(0)
        stats = jnp.zeros((ROWS, HS), F32)
        for h in range(HEADS_DEV):
            ahead = scores(h + 1) if h + 1 < HEADS_DEV else None
            tail = jnp.where(seen, s[:, width - CHUNK :], NEG)
            s = jnp.concatenate([s[:, : width - CHUNK], tail], axis=1) if chunks > 1 else tail
            top = jnp.max(s, axis=1, keepdims=True)
            p = jnp.exp2((s - top) * EXP_SCALE)
            lanes = p[:, :HS]
            for g in range(1, width // HS):
                lanes = lanes + p[:, g * HS : (g + 1) * HS]
            total = jnp.sum(lanes, axis=1, keepdims=True)
            acc = jnp.dot(
                p.astype(BF),
                kv_ref[:width, QCOLS + h * HS : QCOLS + (h + 1) * HS],
                preferred_element_type=F32,
            )
            has = top > 0.5 * NEG
            o_refs[b][:, h * HS : (h + 1) * HS] = jnp.where(has, acc / total, 0.0).astype(BF)
            level = jnp.where(has, top * EXP_SCALE + jnp.log2(total), NEG)
            high = level.astype(BF).astype(F32)
            mid = (level - high).astype(BF).astype(F32)
            low = level - high - mid
            stats = jnp.where(lane == 3 * h, high, stats)
            stats = jnp.where(lane == 3 * h + 1, mid, stats)
            stats = jnp.where(lane == 3 * h + 2, low, stats)
            s = ahead
        o_refs[b][:, QCOLS:] = stats.astype(BF)

    for b in range(n):
        first = qframe_ref[b]
        end = vis_ref[first + FRAMES_DEV - 1]
        some = jnp.int32(0)
        for j in range(CHUNKS):
            some = some + (kframe_ref[j] * FTOK < end).astype(jnp.int32)

        @pl.when(some == 0)
        def _(b=b):
            o_refs[b][:, :QCOLS] = jnp.zeros((ROWS, QCOLS), BF)
            blank = jnp.where((lane < 3 * HEADS_DEV) & (lane % 3 == 0), NEG, 0.0)
            o_refs[b][:, QCOLS:] = blank.astype(BF)

        for chunks in range(1, CHUNKS + 1):

            @pl.when(some == chunks)
            def _(b=b, first=first, chunks=chunks):
                heads(b, first, chunks)


def attention(queries, qframes, kframes, vis_end, kv):
    n = len(queries)
    return vmem_call(
        functools.partial(attention_kernel, n),
        [jax.ShapeDtypeStruct((ROWS, QCOLS + HS), BF)] * n,
        3,
        n + 1,
        flops=n * 8 * ROWS * QCOLS * CHUNK * CHUNKS,
        nbytes=CHUNKS * CHUNK * 2 * QCOLS * 2,
        mib=32,
    )(jnp.stack(qframes), kframes, vis_end, *queries, kv)


def combine_kernel(*refs):
    parts, out_ref = refs[:4], refs[4]
    stats = [p[:, QCOLS:].astype(F32) for p in parts]
    for h in range(HEADS_DEV):
        levels = []
        for s in stats:
            levels.append(
                s[:, 3 * h : 3 * h + 1] + s[:, 3 * h + 1 : 3 * h + 2] + s[:, 3 * h + 2 : 3 * h + 3]
            )
        top = functools.reduce(jnp.maximum, levels)
        shares = [jnp.exp2(v - top) for v in levels]
        total = shares[0] + shares[1] + shares[2] + shares[3]
        cols = slice(h * HS, (h + 1) * HS)
        acc = jnp.zeros((ROWS, HS), F32)
        for p, w in zip(parts, shares):
            acc = acc + p[:, cols].astype(F32) * w
        out_ref[:, cols] = (acc / total).astype(BF)


def merge_out_kernel(order_ref, w_ref, mine_ref, other_ref, up_ref, up_other_ref, out_ref):
    at = order_ref[pl.program_id(0)]
    up = jnp.concatenate([up_ref[:, QCOLS:], up_other_ref[:, QCOLS:]], axis=0)
    cols = slice(WIDTH, WIDTH + QCOLS)
    down = jnp.concatenate([mine_ref[at, :, cols], other_ref[at, :, cols]], axis=0)
    out_ref[...] = (w_ref[...].astype(F32) + tdot(down, up)).astype(BF)


def merge_out(order, w, mine, other, up, up_other):
    def whole(shape):
        return pl.BlockSpec(shape, lambda i: (0,) * len(shape))

    return pl.pallas_call(
        merge_out_kernel,
        out_shape=jax.ShapeDtypeStruct((8 * QCOLS, WIDTH), BF),
        grid=(8,),
        in_specs=[
            pl.BlockSpec(memory_space=pltpu.SMEM),
            pl.BlockSpec((QCOLS, WIDTH), lambda i: (i, 0)),
            whole(mine.shape),
            whole(other.shape),
            whole(up.shape),
            whole(up_other.shape),
        ],
        out_specs=pl.BlockSpec((QCOLS, WIDTH), lambda i: (i, 0)),
        cost_estimate=pl.CostEstimate(
            flops=2 * 8 * WIDTH * RANK * QCOLS, bytes_accessed=10**7, transcendentals=0
        ),
        compiler_params=pltpu.CompilerParams(vmem_limit_bytes=16 * 1024 * 1024),
    )(order, w, mine, other, up, up_other)


def project_kernel(order_ref, a_ref, w_ref, out_ref):
    acc = jnp.zeros((ROWS, WIDTH), F32)
    for i in range(8):
        acc = acc + jnp.dot(
            a_ref[order_ref[i]],
            w_ref[i * QCOLS : (i + 1) * QCOLS, :],
            preferred_element_type=F32,
        )
    out_ref[...] = acc.astype(BF)


def cover_kernel(in_ref, out_ref):
    out_ref[...] = in_ref[...]


def cover(seed):
    return pl.pallas_call(
        cover_kernel,
        out_shape=jax.ShapeDtypeStruct(seed.shape, seed.dtype),
        cost_estimate=pl.CostEstimate(flops=3 * 10**10, bytes_accessed=10**8, transcendentals=0),
    )(seed)


def together(*values):
    return lax.optimization_barrier(values)


def after(value, *others):
    return lax.optimization_barrier((value,) + others)[0]


def prep_kernel(scal_ref, down_q_ref, down_o_ref, up_q_ref, up_o_ref, out_ref):
    start = 0
    for i, ref in ((0, down_q_ref), (2, down_o_ref), (1, up_q_ref), (3, up_o_ref)):
        width = ref.shape[1]
        mine = scal_ref[1 + i] == scal_ref[0]
        out_ref[:, start : start + width] = jnp.where(mine, ref[...].astype(F32), 0.0).astype(BF)
        start += width


def prepare(rank, tp, owners, down_q, down_o, up_q, up_o):
    scal = jnp.concatenate([rank[None], owners, tp[None]]).astype(jnp.int32)
    width = 2 * (WIDTH + QCOLS)
    return pl.pallas_call(
        prep_kernel,
        out_shape=jax.ShapeDtypeStruct((RANK, width), BF),
        grid_spec=pltpu.PrefetchScalarGridSpec(
            num_scalar_prefetch=1,
            grid=(1,),
            in_specs=[
                pl.BlockSpec((RANK, WIDTH), lambda i, sc: (0, sc[5])),
                pl.BlockSpec((RANK, QCOLS), lambda i, sc: (0, 0)),
                pl.BlockSpec((RANK, QCOLS), lambda i, sc: (0, 0)),
                pl.BlockSpec((RANK, WIDTH), lambda i, sc: (0, sc[5])),
            ],
            out_specs=pl.BlockSpec((RANK, width), lambda i, sc: (0, 0)),
        ),
        cost_estimate=pl.CostEstimate(flops=3 * 10**10, bytes_accessed=10**8, transcendentals=0),
        compiler_params=pltpu.CompilerParams(vmem_limit_bytes=16 * 1024 * 1024),
    )(scal, down_q, down_o, up_q, up_o)


def copies(piece, axis, n):
    everywhere = jnp.broadcast_to(piece[None], (n,) + piece.shape)
    return lax.all_to_all(everywhere, axis, 0, 0)


def spread(part, axis):
    got = copies(part, axis, SIZES[axis])
    return got[0] + got[1] + got[2] + got[3]


def column_piece(weight, rank, tp):
    piece = lax.dynamic_slice(
        weight, ((rank % 4) * PIECE, (tp ^ (rank // 4)) * WIDTH), (PIECE, WIDTH)
    )
    return piece


def to_columns(piece):
    pairs = []
    for r in range(32):
        for t in range(8):
            pairs.append((r * 8 + t, r * 8 + (t ^ (r // 4))))
    return lax.ppermute(piece, AXES, pairs)


SHIFTS = [(a, d) for a in range(2) for d in range(4)]


def shards(
    tokens,
    norm_gain_vector,
    keys,
    values,
    query_frozen_weight,
    output_frozen_weight,
    query_update_first,
    query_update_second,
    output_update_first,
    output_update_second,
    owners,
    frame_block_number,
):
    zh, y, c = (lax.axis_index(a) for a in CTX)
    tp = lax.axis_index("zl") * 4 + lax.axis_index("x")
    rank = zh * 8 + y * 2 + c

    half = RANK // 2
    half_rows = ROWS // 2
    left = shift(tokens, "x", 1)
    right = shift(tokens, "x", -1)
    other = shift(tokens, "zl", 1)
    factors = prepare(
        rank,
        tp,
        owners,
        query_update_first[0].T,
        output_update_first[0].T,
        query_update_second[0],
        output_update_second[0],
    )
    factors = factors + shift(factors, "c", 1)
    part = lax.dynamic_slice_in_dim(factors, c * half, half, 0)
    seed = jnp.zeros((8, HS), F32)
    kv = jnp.concatenate([keys, values], axis=1)
    left, right, other, part, seed, kv = together(left, right, other, part, seed, kv)

    kv = lax.all_gather(kv, ("zh", "c"), axis=0, tiled=True)
    other_left = shift(other, "x", 1)
    other_right = shift(other, "x", -1)
    part = spread(part, "zh")
    seed = cover(seed)
    other_left, other_right, part, seed = together(other_left, other_right, part, seed)

    far_left = shift(jnp.concatenate([left[:half_rows], other_left[:half_rows]]), "x", 1)
    far_right = shift(jnp.concatenate([right[half_rows:], other_right[half_rows:]]), "x", -1)
    columns = column_piece(output_frozen_weight, rank, tp)
    columns = to_columns(after(columns, other_left))
    part = spread(part, "y")
    seed = cover(seed)
    far_left, far_right, columns, part, seed = together(far_left, far_right, columns, part, seed)

    gain = jnp.pad(norm_gain_vector.reshape(WIDTH // HS, HS), ((0, half - WIDTH // HS), (0, 0)))
    down = jnp.concatenate([part[:, : WIDTH + QCOLS], gain], axis=1)
    mine = copies(down, TP, 8)
    ups = part[:, WIDTH + QCOLS :]
    ups_other = shift(ups, "c", 1)
    theirs = shift(mine, "c", 1)

    order = jnp.stack([tp_source(a, d) for a, d in SHIFTS])
    blocks = [tokens, left, far_left, right, other, other_left, far_right, other_right]
    queries = pl.pallas_call(
        query_kernel,
        out_shape=jax.ShapeDtypeStruct((ROWS, QCOLS), BF),
        in_specs=[pl.BlockSpec(memory_space=pltpu.SMEM)]
        + [pl.BlockSpec(memory_space=pl.ANY)] * 8
        + [pl.BlockSpec(memory_space=pltpu.VMEM)] * 4
        + [pl.BlockSpec(memory_space=pl.ANY)],
        out_specs=pl.BlockSpec(memory_space=pltpu.VMEM),
        scratch_shapes=[
            pltpu.VMEM((8, ROWS, WIDTH), BF),
            pltpu.VMEM((8, WIDTH, QCOLS), BF),
            pltpu.SemaphoreType.DMA((16,)),
            pltpu.SemaphoreType.DMA((8,)),
        ],
        cost_estimate=pl.CostEstimate(
            flops=2 * ROWS * 8 * WIDTH * QCOLS + 2 * 8 * WIDTH * RANK * QCOLS,
            bytes_accessed=10**7,
            transcendentals=0,
        ),
        compiler_params=pltpu.CompilerParams(vmem_limit_bytes=60 * 1024 * 1024),
    )(order, *blocks, mine, theirs, ups, ups_other, query_frozen_weight)

    columns = lax.all_gather(columns, CTX, axis=0, tiled=True)
    order_out = jnp.stack([tp ^ i for i in range(8)])

    out_merged = merge_out(order_out, columns, mine, theirs, ups, ups_other)

    counts = jnp.sum(
        (frame_block_number[None, :] <= frame_block_number[:, None]).astype(jnp.int32), axis=1
    )
    vis_end = counts * FTOK
    kframes = (jnp.arange(CHUNKS, dtype=jnp.int32) * 8 + y * 2) * FRAMES_DEV

    def frames_of(step):
        return (zh * 8 + ((y - step) % 4) * 2 + c) * FRAMES_DEV

    q_left = shift(queries, "y", 1)
    q_right = shift(queries, "y", -1)
    q_far = shift(queries, "y", 2)
    (own,) = attention([queries], [frames_of(0)], kframes, vis_end, kv)
    q_left = after(q_left, own)
    (left,) = attention([q_left], [frames_of(1)], kframes, vis_end, kv)
    back_left = shift(left, "y", -1)
    (right,) = attention([q_right], [frames_of(-1)], kframes, vis_end, kv)
    back_right = shift(right, "y", 1)
    (far,) = attention([q_far], [frames_of(2)], kframes, vis_end, kv)
    back_far = shift(far, "y", 2)
    attended = vmem_call(combine_kernel, jax.ShapeDtypeStruct((ROWS, QCOLS), BF), 0, 4, nbytes=10**6)(
        own, back_left, back_right, back_far
    )
    attended = copies(attended, TP, 8)
    return vmem_call(
        project_kernel,
        jax.ShapeDtypeStruct((ROWS, WIDTH), BF),
        1,
        2,
        flops=2 * ROWS * 8 * WIDTH * QCOLS,
        nbytes=10**7,
    )(order_out, attended, out_merged)


def solution(mesh):
    fine = Mesh(mesh.devices.reshape([SIZES[a] for a in AXES]), AXES)
    in_specs = (
        P(CTX, TP),
        P(TP),
        P(CTX, TP),
        P(CTX, TP),
        P(None, TP),
        P(TP, None),
        P(CTX, None, None),
        P(CTX, None, TP),
        P(CTX, TP, None),
        P(CTX, None, None),
        P(),
        P(),
    )
    return jax.shard_map(
        shards, mesh=fine, in_specs=in_specs, out_specs=P(CTX, TP), check_vma=False
    )
```

```python
import functools
import math

import jax
import jax.numpy as jnp
from jax import lax
from jax.experimental import pallas as pl
from jax.experimental.pallas import tpu as pltpu
from jax.sharding import Mesh
from jax.sharding import PartitionSpec as P

HS = 128
FTOK = 64
ROWS = 320
FRAMES_DEV = 5
WIDTH = 768
RANK = 64
HEADS_DEV = 3
QCOLS = HEADS_DEV * HS
CHUNK = 2 * ROWS
CHUNKS = 4
NEG = -1e30
PIECE = 96
EPS = 1e-6
AXES = ("zh", "y", "c", "zl", "x")
SIZES = {"zh": 4, "y": 4, "c": 2, "zl": 2, "x": 4}
CTX = ("zh", "y", "c")
TP = ("zl", "x")
EXP_SCALE = (HS ** (-0.5)) * math.log2(math.e)
BF = jnp.bfloat16
F32 = jnp.float32


def shift(v, axis, step):
    n = SIZES[axis]
    return lax.ppermute(v, axis, [(i, (i + step) % n) for i in range(n)])


def tp_source(a, d):
    return (lax.axis_index("zl") ^ a) * 4 + (lax.axis_index("x") - d) % 4


def vmem_call(body, out_shape, n_smem, n_vmem, scratch=(), flops=0, nbytes=0, mib=16, n_any=0):
    return pl.pallas_call(
        body,
        out_shape=out_shape,
        in_specs=[pl.BlockSpec(memory_space=pltpu.SMEM)] * n_smem
        + [pl.BlockSpec(memory_space=pltpu.VMEM)] * n_vmem
        + [pl.BlockSpec(memory_space=pl.ANY)] * n_any,
        scratch_shapes=list(scratch),
        cost_estimate=pl.CostEstimate(flops=flops, bytes_accessed=nbytes, transcendentals=0),
        compiler_params=pltpu.CompilerParams(vmem_limit_bytes=mib * 1024 * 1024),
    )


def tdot(a, b):
    return lax.dot_general(a, b, (((0,), (0,)), ((), ())), preferred_element_type=F32)


def norm_kernel(order_ref, gain_ref, *refs):
    parts, out_ref = refs[:8], refs[8]
    half = ROWS // 2

    def block(i):
        if i in (2, 6):
            rows = slice(0, half) if i == 2 else slice(half, ROWS)
            return jnp.concatenate([parts[2][rows, :], parts[6][rows, :]], axis=0)
        return parts[i][...]

    total = jnp.zeros((ROWS, HS), F32)
    for i in range(8):
        v = block(i).astype(F32)
        v = v * v
        for g in range(WIDTH // HS):
            total = total + v[:, g * HS : (g + 1) * HS]
    total = jnp.sum(total, axis=1, keepdims=True)
    inv = lax.rsqrt(total * (1.0 / (8 * WIDTH)) + EPS)
    for i in range(8):
        at = order_ref[i]
        gain = jnp.concatenate(
            [gain_ref[at, r : r + 1, :].astype(F32) for r in range(WIDTH // HS)], axis=1
        )
        out_ref[i] = (block(i).astype(F32) * inv * gain).astype(BF)


def query_kernel(
    order_ref, mine_ref, other_ref, up_ref, up_other_ref, x_ref, w_ref, out_ref, xs, ws, x_sems, w_sems
):
    copies_in = []
    for i in range(8):
        rows = pl.ds(pl.multiple_of(order_ref[i] * WIDTH, WIDTH), WIDTH)
        copies_in.append(
            (
                pltpu.make_async_copy(w_ref.at[rows, :], ws.at[i], w_sems.at[i]),
                pltpu.make_async_copy(x_ref.at[i], xs.at[i], x_sems.at[i]),
            )
        )
        for copy in copies_in[i]:
            copy.start()
    acc = jnp.zeros((ROWS, QCOLS), F32)
    up = jnp.concatenate([up_ref[:, :QCOLS], up_other_ref[:, :QCOLS]], axis=0)
    for i in range(8):
        at = order_ref[i]
        down = jnp.concatenate([mine_ref[at, :, :WIDTH], other_ref[at, :, :WIDTH]], axis=0)
        copies_in[i][0].wait()
        merged = (ws[i].astype(F32) + tdot(down, up)).astype(BF)
        copies_in[i][1].wait()
        acc = acc + jnp.dot(xs[i], merged, preferred_element_type=F32)
    out_ref[...] = acc.astype(BF)


def attention_kernel(n, qframe_ref, kframe_ref, vis_ref, *refs):
    q_refs = refs[:n]
    kv_ref = refs[n]
    o_refs = refs[n + 1 :]
    lane = lax.broadcasted_iota(jnp.int32, (ROWS, HS), 1)
    row = lax.broadcasted_iota(jnp.int32, (ROWS, 1), 0)

    def heads(b, first, chunks):
        width = chunks * CHUNK
        last = kframe_ref[chunks - 1] * FTOK
        limit = jnp.full((ROWS, 1), vis_ref[first] - last, jnp.int32)
        for f in range(1, FRAMES_DEV):
            limit = jnp.where(row >= f * FTOK, vis_ref[first + f] - last, limit)
        seen = lax.broadcasted_iota(jnp.int32, (ROWS, CHUNK), 1) < limit

        def scores(h):
            cols = slice(h * HS, (h + 1) * HS)
            return lax.dot_general(
                q_refs[b][:, cols],
                kv_ref[:width, cols],
                (((1,), (1,)), ((), ())),
                preferred_element_type=F32,
            )

        s = scores(0)
        stats = jnp.zeros((ROWS, HS), F32)
        for h in range(HEADS_DEV):
            ahead = scores(h + 1) if h + 1 < HEADS_DEV else None
            tail = jnp.where(seen, s[:, width - CHUNK :], NEG)
            s = jnp.concatenate([s[:, : width - CHUNK], tail], axis=1) if chunks > 1 else tail
            top = jnp.max(s, axis=1, keepdims=True)
            p = jnp.exp2((s - top) * EXP_SCALE)
            lanes = p[:, :HS]
            for g in range(1, width // HS):
                lanes = lanes + p[:, g * HS : (g + 1) * HS]
            total = jnp.sum(lanes, axis=1, keepdims=True)
            acc = jnp.dot(
                p.astype(BF),
                kv_ref[:width, QCOLS + h * HS : QCOLS + (h + 1) * HS],
                preferred_element_type=F32,
            )
            has = top > 0.5 * NEG
            o_refs[b][:, h * HS : (h + 1) * HS] = jnp.where(has, acc / total, 0.0).astype(BF)
            level = jnp.where(has, top * EXP_SCALE + jnp.log2(total), NEG)
            high = level.astype(BF).astype(F32)
            mid = (level - high).astype(BF).astype(F32)
            low = level - high - mid
            stats = jnp.where(lane == 3 * h, high, stats)
            stats = jnp.where(lane == 3 * h + 1, mid, stats)
            stats = jnp.where(lane == 3 * h + 2, low, stats)
            s = ahead
        o_refs[b][:, QCOLS:] = stats.astype(BF)

    for b in range(n):
        first = qframe_ref[b]
        end = vis_ref[first + FRAMES_DEV - 1]
        some = jnp.int32(0)
        for j in range(CHUNKS):
            some = some + (kframe_ref[j] * FTOK < end).astype(jnp.int32)

        @pl.when(some == 0)
        def _(b=b):
            o_refs[b][:, :QCOLS] = jnp.zeros((ROWS, QCOLS), BF)
            blank = jnp.where((lane < 3 * HEADS_DEV) & (lane % 3 == 0), NEG, 0.0)
            o_refs[b][:, QCOLS:] = blank.astype(BF)

        for chunks in range(1, CHUNKS + 1):

            @pl.when(some == chunks)
            def _(b=b, first=first, chunks=chunks):
                heads(b, first, chunks)


def attention(queries, qframes, kframes, vis_end, kv):
    n = len(queries)
    return vmem_call(
        functools.partial(attention_kernel, n),
        [jax.ShapeDtypeStruct((ROWS, QCOLS + HS), BF)] * n,
        3,
        n + 1,
        flops=n * 8 * ROWS * QCOLS * CHUNK * CHUNKS,
        nbytes=CHUNKS * CHUNK * 2 * QCOLS * 2,
        mib=32,
    )(jnp.stack(qframes), kframes, vis_end, *queries, kv)


def combine_kernel(*refs):
    parts, out_ref = refs[:4], refs[4]
    stats = [p[:, QCOLS:].astype(F32) for p in parts]
    for h in range(HEADS_DEV):
        levels = []
        for s in stats:
            levels.append(
                s[:, 3 * h : 3 * h + 1] + s[:, 3 * h + 1 : 3 * h + 2] + s[:, 3 * h + 2 : 3 * h + 3]
            )
        top = functools.reduce(jnp.maximum, levels)
        shares = [jnp.exp2(v - top) for v in levels]
        total = shares[0] + shares[1] + shares[2] + shares[3]
        cols = slice(h * HS, (h + 1) * HS)
        acc = jnp.zeros((ROWS, HS), F32)
        for p, w in zip(parts, shares):
            acc = acc + p[:, cols].astype(F32) * w
        out_ref[:, cols] = (acc / total).astype(BF)


def merge_out_kernel(order_ref, w_ref, mine_ref, other_ref, up_ref, up_other_ref, out_ref):
    at = order_ref[pl.program_id(0)]
    up = jnp.concatenate([up_ref[:, QCOLS:], up_other_ref[:, QCOLS:]], axis=0)
    cols = slice(WIDTH, WIDTH + QCOLS)
    down = jnp.concatenate([mine_ref[at, :, cols], other_ref[at, :, cols]], axis=0)
    out_ref[...] = (w_ref[...].astype(F32) + tdot(down, up)).astype(BF)


def merge_out(order, w, mine, other, up, up_other):
    def whole(shape):
        return pl.BlockSpec(shape, lambda i: (0,) * len(shape))

    return pl.pallas_call(
        merge_out_kernel,
        out_shape=jax.ShapeDtypeStruct((8 * QCOLS, WIDTH), BF),
        grid=(8,),
        in_specs=[
            pl.BlockSpec(memory_space=pltpu.SMEM),
            pl.BlockSpec((QCOLS, WIDTH), lambda i: (i, 0)),
            whole(mine.shape),
            whole(other.shape),
            whole(up.shape),
            whole(up_other.shape),
        ],
        out_specs=pl.BlockSpec((QCOLS, WIDTH), lambda i: (i, 0)),
        cost_estimate=pl.CostEstimate(
            flops=2 * 8 * WIDTH * RANK * QCOLS, bytes_accessed=10**7, transcendentals=0
        ),
        compiler_params=pltpu.CompilerParams(vmem_limit_bytes=16 * 1024 * 1024),
    )(order, w, mine, other, up, up_other)


def project_kernel(order_ref, *refs):
    parts, w_ref, out_ref, xs, ws, x_sems, w_sems = refs[:8], *refs[8:]
    half = ROWS // 2
    waits = []
    for i in range(8):
        rows = pl.ds(pl.multiple_of(order_ref[i] * QCOLS, QCOLS), QCOLS)
        mine = [pltpu.make_async_copy(w_ref.at[rows, :], ws.at[i], w_sems.at[i])]
        if i in (2, 6):
            src = slice(0, half) if i == 2 else slice(half, ROWS)
            for k, side in enumerate((2, 6)):
                dst = xs.at[i, k * half : (k + 1) * half, :]
                mine.append(
                    pltpu.make_async_copy(parts[side].at[src, :], dst, x_sems.at[i + 8 * k])
                )
        else:
            mine.append(pltpu.make_async_copy(parts[i], xs.at[i], x_sems.at[i]))
        for copy in mine:
            copy.start()
        waits.append(mine)
    acc = jnp.zeros((ROWS, WIDTH), F32)
    for i in range(8):
        for copy in waits[i]:
            copy.wait()
        acc = acc + jnp.dot(xs[i], ws[i], preferred_element_type=F32)
    out_ref[...] = acc.astype(BF)


def fetch_call(body, out_shape, n_vmem, n_any, x_shape, w_shape, flops):
    return pl.pallas_call(
        body,
        out_shape=out_shape,
        in_specs=[pl.BlockSpec(memory_space=pltpu.SMEM)]
        + [pl.BlockSpec(memory_space=pltpu.VMEM)] * n_vmem
        + [pl.BlockSpec(memory_space=pl.ANY)] * n_any,
        out_specs=pl.BlockSpec(memory_space=pltpu.VMEM),
        scratch_shapes=[
            pltpu.VMEM(x_shape, BF),
            pltpu.VMEM(w_shape, BF),
            pltpu.SemaphoreType.DMA((16,)),
            pltpu.SemaphoreType.DMA((8,)),
        ],
        cost_estimate=pl.CostEstimate(flops=flops, bytes_accessed=10**7, transcendentals=0),
        compiler_params=pltpu.CompilerParams(vmem_limit_bytes=60 * 1024 * 1024),
    )


def cover_kernel(in_ref, out_ref):
    out_ref[...] = in_ref[...]


def cover(seed):
    return pl.pallas_call(
        cover_kernel,
        out_shape=jax.ShapeDtypeStruct(seed.shape, seed.dtype),
        cost_estimate=pl.CostEstimate(flops=3 * 10**10, bytes_accessed=10**8, transcendentals=0),
    )(seed)


def together(*values):
    return lax.optimization_barrier(values)


def after(value, *others):
    return lax.optimization_barrier((value,) + others)[0]


def prep_kernel(scal_ref, down_q_ref, down_o_ref, up_q_ref, up_o_ref, out_ref):
    start = 0
    for i, ref in ((0, down_q_ref), (2, down_o_ref), (1, up_q_ref), (3, up_o_ref)):
        width = ref.shape[1]
        mine = scal_ref[1 + i] == scal_ref[0]
        out_ref[:, start : start + width] = jnp.where(mine, ref[...].astype(F32), 0.0).astype(BF)
        start += width


def prepare(rank, tp, owners, down_q, down_o, up_q, up_o):
    scal = jnp.concatenate([rank[None], owners, tp[None]]).astype(jnp.int32)
    width = 2 * (WIDTH + QCOLS)
    return pl.pallas_call(
        prep_kernel,
        out_shape=jax.ShapeDtypeStruct((RANK, width), BF),
        grid_spec=pltpu.PrefetchScalarGridSpec(
            num_scalar_prefetch=1,
            grid=(1,),
            in_specs=[
                pl.BlockSpec((RANK, WIDTH), lambda i, sc: (0, sc[5])),
                pl.BlockSpec((RANK, QCOLS), lambda i, sc: (0, 0)),
                pl.BlockSpec((RANK, QCOLS), lambda i, sc: (0, 0)),
                pl.BlockSpec((RANK, WIDTH), lambda i, sc: (0, sc[5])),
            ],
            out_specs=pl.BlockSpec((RANK, width), lambda i, sc: (0, 0)),
        ),
        cost_estimate=pl.CostEstimate(flops=3 * 10**10, bytes_accessed=10**8, transcendentals=0),
        compiler_params=pltpu.CompilerParams(vmem_limit_bytes=16 * 1024 * 1024),
    )(scal, down_q, down_o, up_q, up_o)


def copies(piece, axis, n):
    everywhere = jnp.broadcast_to(piece[None], (n,) + piece.shape)
    return lax.all_to_all(everywhere, axis, 0, 0)


def spread(part, axis):
    got = copies(part, axis, SIZES[axis])
    return got[0] + got[1] + got[2] + got[3]


def column_piece(weight, rank, tp):
    piece = lax.dynamic_slice(
        weight, ((rank % 4) * PIECE, (tp ^ (rank // 4)) * WIDTH), (PIECE, WIDTH)
    )
    return piece


def to_columns(piece):
    pairs = []
    for r in range(32):
        for t in range(8):
            pairs.append((r * 8 + t, r * 8 + (t ^ (r // 4))))
    return lax.ppermute(piece, AXES, pairs)


SHIFTS = [(a, d) for a in range(2) for d in range(4)]


def shards(
    tokens,
    norm_gain_vector,
    keys,
    values,
    query_frozen_weight,
    output_frozen_weight,
    query_update_first,
    query_update_second,
    output_update_first,
    output_update_second,
    owners,
    frame_block_number,
):
    zh, y, c = (lax.axis_index(a) for a in CTX)
    tp = lax.axis_index("zl") * 4 + lax.axis_index("x")
    rank = zh * 8 + y * 2 + c

    half = RANK // 2
    half_rows = ROWS // 2
    left = shift(tokens, "x", 1)
    right = shift(tokens, "x", -1)
    other = shift(tokens, "zl", 1)
    factors = prepare(
        rank,
        tp,
        owners,
        query_update_first[0].T,
        output_update_first[0].T,
        query_update_second[0],
        output_update_second[0],
    )
    gain = jnp.pad(norm_gain_vector.reshape(WIDTH // HS, HS), ((0, 16 - WIDTH // HS), (0, 0)))
    gain = copies(gain, TP, 8)
    seed = jnp.zeros((8, HS), F32)
    kv = jnp.concatenate([keys, values], axis=1)
    columns = to_columns(column_piece(output_frozen_weight, rank, tp))
    left, right, other, factors, seed, kv, gain, columns = together(
        left, right, other, factors, seed, kv, gain, columns
    )

    kv = lax.all_gather(kv, ("zh", "c"), axis=0, tiled=True)
    other_left = shift(other, "x", 1)
    other_right = shift(other, "x", -1)
    factors = factors + shift(factors, "c", 1)
    part = lax.dynamic_slice_in_dim(factors, c * half, half, 0)
    part = spread(part, "zh")
    seed = cover(seed)
    other_left, other_right, part, seed, columns = together(
        other_left, other_right, part, seed, columns
    )
    columns = lax.all_gather(columns, CTX, axis=0, tiled=True)

    far_left = shift(jnp.concatenate([left[:half_rows], other_left[:half_rows]]), "x", 1)
    far_right = shift(jnp.concatenate([right[half_rows:], other_right[half_rows:]]), "x", -1)
    part = spread(part, "y")
    seed = cover(seed)
    far_left, far_right, part, seed = together(far_left, far_right, part, seed)

    order = jnp.stack([tp_source(a, d) for a, d in SHIFTS])
    mine = copies(part[:, : WIDTH + QCOLS], TP, 8)
    ups = part[:, WIDTH + QCOLS :]
    ups_other = shift(ups, "c", 1)
    normed = vmem_call(
        norm_kernel,
        jax.ShapeDtypeStruct((8, ROWS, WIDTH), BF),
        1,
        9,
        flops=10**10,
        nbytes=4 * 10**7,
        mib=24,
    )(order, gain, tokens, left, far_left, right, other, other_left, far_right, other_right)
    mine, normed = together(mine, normed)
    theirs = shift(mine, "c", 1)
    queries = fetch_call(
        query_kernel,
        jax.ShapeDtypeStruct((ROWS, QCOLS), BF),
        4,
        2,
        (8, ROWS, WIDTH),
        (8, WIDTH, QCOLS),
        2 * ROWS * 8 * WIDTH * QCOLS + 2 * 8 * WIDTH * RANK * QCOLS,
    )(order, mine, theirs, ups, ups_other, normed, query_frozen_weight)

    order_out = jnp.stack([tp ^ i for i in range(8)])
    out_merged = merge_out(order_out, columns, mine, theirs, ups, ups_other)

    counts = jnp.sum(
        (frame_block_number[None, :] <= frame_block_number[:, None]).astype(jnp.int32), axis=1
    )
    vis_end = counts * FTOK
    kframes = (jnp.arange(CHUNKS, dtype=jnp.int32) * 8 + y * 2) * FRAMES_DEV

    def frames_of(step):
        return (zh * 8 + ((y - step) % 4) * 2 + c) * FRAMES_DEV

    q_left = shift(queries, "y", 1)
    q_right = shift(queries, "y", -1)
    q_far = shift(queries, "y", 2)
    (own,) = attention([queries], [frames_of(0)], kframes, vis_end, kv)
    q_left = after(q_left, own)
    (left,) = attention([q_left], [frames_of(1)], kframes, vis_end, kv)
    back_left = shift(left, "y", -1)
    (right,) = attention([q_right], [frames_of(-1)], kframes, vis_end, kv)
    back_right = shift(right, "y", 1)
    (far,) = attention([q_far], [frames_of(2)], kframes, vis_end, kv)
    back_far = shift(far, "y", 2)

    attended = vmem_call(combine_kernel, jax.ShapeDtypeStruct((ROWS, QCOLS), BF), 0, 4, nbytes=10**6)(
        own, back_left, back_right, back_far
    )
    left = shift(attended, "x", 1)
    right = shift(attended, "x", -1)
    other = shift(attended, "zl", 1)
    other_left = shift(other, "x", 1)
    other_right = shift(other, "x", -1)
    far_left = shift(jnp.concatenate([left[:half_rows], other_left[:half_rows]]), "x", 1)
    far_right = shift(jnp.concatenate([right[half_rows:], other_right[half_rows:]]), "x", -1)
    slots = jnp.stack([tp ^ tp_source(a, d) for a, d in SHIFTS])
    return fetch_call(
        project_kernel,
        jax.ShapeDtypeStruct((ROWS, WIDTH), BF),
        0,
        9,
        (8, ROWS, QCOLS),
        (8, QCOLS, WIDTH),
        2 * ROWS * 8 * WIDTH * QCOLS,
    )(slots, attended, left, far_left, right, other, other_left, far_right, other_right, out_merged)


def solution(mesh):
    fine = Mesh(mesh.devices.reshape([SIZES[a] for a in AXES]), AXES)
    in_specs = (
        P(CTX, TP),
        P(TP),
        P(CTX, TP),
        P(CTX, TP),
        P(None, TP),
        P(TP, None),
        P(CTX, None, None),
        P(CTX, None, TP),
        P(CTX, TP, None),
        P(CTX, None, None),
        P(),
        P(),
    )
    return jax.shard_map(
        shards, mesh=fine, in_specs=in_specs, out_specs=P(CTX, TP), check_vma=False
    )
```

```python
import functools
import math

import jax
import jax.numpy as jnp
from jax import lax
from jax.experimental import pallas as pl
from jax.experimental.pallas import tpu as pltpu
from jax.sharding import Mesh
from jax.sharding import PartitionSpec as P

HS = 128
FTOK = 64
ROWS = 320
FRAMES_DEV = 5
WIDTH = 768
RANK = 64
HEADS_DEV = 3
QCOLS = HEADS_DEV * HS
CHUNK = 2 * ROWS
CHUNKS = 4
NEG = -1e30
PIECE = 96
EPS = 1e-6
AXES = ("zh", "y", "c", "zl", "x")
SIZES = {"zh": 4, "y": 4, "c": 2, "zl": 2, "x": 4}
CTX = ("zh", "y", "c")
TP = ("zl", "x")
EXP_SCALE = (HS ** (-0.5)) * math.log2(math.e)
BF = jnp.bfloat16
F32 = jnp.float32


def shift(v, axis, step):
    n = SIZES[axis]
    return lax.ppermute(v, axis, [(i, (i + step) % n) for i in range(n)])


def tp_source(a, d):
    return (lax.axis_index("zl") ^ a) * 4 + (lax.axis_index("x") - d) % 4


def vmem_call(body, out_shape, n_smem, n_vmem, scratch=(), flops=0, nbytes=0, mib=16, n_any=0):
    return pl.pallas_call(
        body,
        out_shape=out_shape,
        in_specs=[pl.BlockSpec(memory_space=pltpu.SMEM)] * n_smem
        + [pl.BlockSpec(memory_space=pltpu.VMEM)] * n_vmem
        + [pl.BlockSpec(memory_space=pl.ANY)] * n_any,
        scratch_shapes=list(scratch),
        cost_estimate=pl.CostEstimate(flops=flops, bytes_accessed=nbytes, transcendentals=0),
        compiler_params=pltpu.CompilerParams(vmem_limit_bytes=mib * 1024 * 1024),
    )


def tdot(a, b):
    return lax.dot_general(a, b, (((0,), (0,)), ((), ())), preferred_element_type=F32)


def norm_kernel(order_ref, gain_ref, *refs):
    parts, out_ref = refs[:8], refs[8]
    half = ROWS // 2

    def block(i):
        if i in (2, 6):
            rows = slice(0, half) if i == 2 else slice(half, ROWS)
            return jnp.concatenate([parts[2][rows, :], parts[6][rows, :]], axis=0)
        return parts[i][...]

    total = jnp.zeros((ROWS, HS), F32)
    for i in range(8):
        v = block(i).astype(F32)
        v = v * v
        for g in range(WIDTH // HS):
            total = total + v[:, g * HS : (g + 1) * HS]
    total = jnp.sum(total, axis=1, keepdims=True)
    inv = lax.rsqrt(total * (1.0 / (8 * WIDTH)) + EPS)
    for i in range(8):
        at = order_ref[i]
        gain = jnp.concatenate(
            [gain_ref[at, r : r + 1, :].astype(F32) for r in range(WIDTH // HS)], axis=1
        )
        out_ref[i] = (block(i).astype(F32) * inv * gain).astype(BF)


def query_kernel(
    order_ref, mine_ref, other_ref, up_ref, up_other_ref, x_ref, w_ref, out_ref, xs, ws, x_sems, w_sems
):
    copies_in = []
    for i in range(8):
        rows = pl.ds(pl.multiple_of(order_ref[i] * WIDTH, WIDTH), WIDTH)
        copies_in.append(
            (
                pltpu.make_async_copy(w_ref.at[rows, :], ws.at[i], w_sems.at[i]),
                pltpu.make_async_copy(x_ref.at[i], xs.at[i], x_sems.at[i]),
            )
        )
        for copy in copies_in[i]:
            copy.start()
    acc = jnp.zeros((ROWS, QCOLS), F32)
    up = jnp.concatenate([up_ref[:, :QCOLS], up_other_ref[:, :QCOLS]], axis=0)
    for i in range(8):
        at = order_ref[i]
        down = jnp.concatenate([mine_ref[at, :, :WIDTH], other_ref[at, :, :WIDTH]], axis=0)
        copies_in[i][0].wait()
        merged = (ws[i].astype(F32) + tdot(down, up)).astype(BF)
        copies_in[i][1].wait()
        acc = acc + jnp.dot(xs[i], merged, preferred_element_type=F32)
    out_ref[...] = acc.astype(BF)


def attention_kernel(n, qframe_ref, kframe_ref, vis_ref, *refs):
    q_refs = refs[:n]
    kv_ref = refs[n]
    o_refs = refs[n + 1 :]
    lane = lax.broadcasted_iota(jnp.int32, (ROWS, HS), 1)
    row = lax.broadcasted_iota(jnp.int32, (ROWS, 1), 0)

    def heads(b, first, chunks):
        width = chunks * CHUNK
        last = kframe_ref[chunks - 1] * FTOK
        limit = jnp.full((ROWS, 1), vis_ref[first] - last, jnp.int32)
        for f in range(1, FRAMES_DEV):
            limit = jnp.where(row >= f * FTOK, vis_ref[first + f] - last, limit)
        seen = lax.broadcasted_iota(jnp.int32, (ROWS, CHUNK), 1) < limit

        def scores(h):
            cols = slice(h * HS, (h + 1) * HS)
            return lax.dot_general(
                q_refs[b][:, cols],
                kv_ref[:width, cols],
                (((1,), (1,)), ((), ())),
                preferred_element_type=F32,
            )

        s = scores(0)
        stats = jnp.zeros((ROWS, HS), F32)
        for h in range(HEADS_DEV):
            ahead = scores(h + 1) if h + 1 < HEADS_DEV else None
            tail = jnp.where(seen, s[:, width - CHUNK :], NEG)
            s = jnp.concatenate([s[:, : width - CHUNK], tail], axis=1) if chunks > 1 else tail
            top = jnp.max(s, axis=1, keepdims=True)
            p = jnp.exp2((s - top) * EXP_SCALE)
            lanes = p[:, :HS]
            for g in range(1, width // HS):
                lanes = lanes + p[:, g * HS : (g + 1) * HS]
            total = jnp.sum(lanes, axis=1, keepdims=True)
            acc = jnp.dot(
                p.astype(BF),
                kv_ref[:width, QCOLS + h * HS : QCOLS + (h + 1) * HS],
                preferred_element_type=F32,
            )
            has = top > 0.5 * NEG
            o_refs[b][:, h * HS : (h + 1) * HS] = jnp.where(has, acc / total, 0.0).astype(BF)
            level = jnp.where(has, top * EXP_SCALE + jnp.log2(total), NEG)
            high = level.astype(BF).astype(F32)
            mid = (level - high).astype(BF).astype(F32)
            low = level - high - mid
            stats = jnp.where(lane == 3 * h, high, stats)
            stats = jnp.where(lane == 3 * h + 1, mid, stats)
            stats = jnp.where(lane == 3 * h + 2, low, stats)
            s = ahead
        o_refs[b][:, QCOLS:] = stats.astype(BF)

    for b in range(n):
        first = qframe_ref[b]
        end = vis_ref[first + FRAMES_DEV - 1]
        some = jnp.int32(0)
        for j in range(CHUNKS):
            some = some + (kframe_ref[j] * FTOK < end).astype(jnp.int32)

        @pl.when(some == 0)
        def _(b=b):
            o_refs[b][:, :QCOLS] = jnp.zeros((ROWS, QCOLS), BF)
            blank = jnp.where((lane < 3 * HEADS_DEV) & (lane % 3 == 0), NEG, 0.0)
            o_refs[b][:, QCOLS:] = blank.astype(BF)

        for chunks in range(1, CHUNKS + 1):

            @pl.when(some == chunks)
            def _(b=b, first=first, chunks=chunks):
                heads(b, first, chunks)


def attention(queries, qframes, kframes, vis_end, kv):
    n = len(queries)
    return vmem_call(
        functools.partial(attention_kernel, n),
        [jax.ShapeDtypeStruct((ROWS, QCOLS + HS), BF)] * n,
        3,
        n + 1,
        flops=n * 8 * ROWS * QCOLS * CHUNK * CHUNKS,
        nbytes=CHUNKS * CHUNK * 2 * QCOLS * 2,
        mib=60,
    )(jnp.stack(qframes), kframes, vis_end, *queries, kv)


def combine_kernel(*refs):
    parts, out_ref = refs[:4], refs[4]
    stats = [p[:, QCOLS:].astype(F32) for p in parts]
    for h in range(HEADS_DEV):
        levels = []
        for s in stats:
            levels.append(
                s[:, 3 * h : 3 * h + 1] + s[:, 3 * h + 1 : 3 * h + 2] + s[:, 3 * h + 2 : 3 * h + 3]
            )
        top = functools.reduce(jnp.maximum, levels)
        shares = [jnp.exp2(v - top) for v in levels]
        total = shares[0] + shares[1] + shares[2] + shares[3]
        cols = slice(h * HS, (h + 1) * HS)
        acc = jnp.zeros((ROWS, HS), F32)
        for p, w in zip(parts, shares):
            acc = acc + p[:, cols].astype(F32) * w
        out_ref[:, cols] = (acc / total).astype(BF)


def merge_out_kernel(order_ref, w_ref, mine_ref, other_ref, up_ref, up_other_ref, out_ref):
    at = order_ref[pl.program_id(0)]
    up = jnp.concatenate([up_ref[:, QCOLS:], up_other_ref[:, QCOLS:]], axis=0)
    cols = slice(WIDTH, WIDTH + QCOLS)
    down = jnp.concatenate([mine_ref[at, :, cols], other_ref[at, :, cols]], axis=0)
    out_ref[...] = (w_ref[...].astype(F32) + tdot(down, up)).astype(BF)


def merge_out(order, w, mine, other, up, up_other):
    def whole(shape):
        return pl.BlockSpec(shape, lambda i: (0,) * len(shape))

    return pl.pallas_call(
        merge_out_kernel,
        out_shape=jax.ShapeDtypeStruct((8 * QCOLS, WIDTH), BF),
        grid=(8,),
        in_specs=[
            pl.BlockSpec(memory_space=pltpu.SMEM),
            pl.BlockSpec((QCOLS, WIDTH), lambda i: (i, 0)),
            whole(mine.shape),
            whole(other.shape),
            whole(up.shape),
            whole(up_other.shape),
        ],
        out_specs=pl.BlockSpec((QCOLS, WIDTH), lambda i: (i, 0)),
        cost_estimate=pl.CostEstimate(
            flops=2 * 8 * WIDTH * RANK * QCOLS, bytes_accessed=10**7, transcendentals=0
        ),
        compiler_params=pltpu.CompilerParams(vmem_limit_bytes=60 * 1024 * 1024),
    )(order, w, mine, other, up, up_other)


def project_kernel(order_ref, *refs):
    parts, w_ref, out_ref, xs, ws, x_sems, w_sems = refs[:8], *refs[8:]
    half = ROWS // 2
    waits = []
    for i in range(8):
        rows = pl.ds(pl.multiple_of(order_ref[i] * QCOLS, QCOLS), QCOLS)
        mine = [pltpu.make_async_copy(w_ref.at[rows, :], ws.at[i], w_sems.at[i])]
        if i in (2, 6):
            src = slice(0, half) if i == 2 else slice(half, ROWS)
            for k, side in enumerate((2, 6)):
                dst = xs.at[i, k * half : (k + 1) * half, :]
                mine.append(
                    pltpu.make_async_copy(parts[side].at[src, :], dst, x_sems.at[i + 8 * k])
                )
        else:
            mine.append(pltpu.make_async_copy(parts[i], xs.at[i], x_sems.at[i]))
        for copy in mine:
            copy.start()
        waits.append(mine)
    acc = jnp.zeros((ROWS, WIDTH), F32)
    for i in range(8):
        for copy in waits[i]:
            copy.wait()
        acc = acc + jnp.dot(xs[i], ws[i], preferred_element_type=F32)
    out_ref[...] = acc.astype(BF)


def fetch_call(body, out_shape, n_vmem, n_any, x_shape, w_shape, flops):
    return pl.pallas_call(
        body,
        out_shape=out_shape,
        in_specs=[pl.BlockSpec(memory_space=pltpu.SMEM)]
        + [pl.BlockSpec(memory_space=pltpu.VMEM)] * n_vmem
        + [pl.BlockSpec(memory_space=pl.ANY)] * n_any,
        out_specs=pl.BlockSpec(memory_space=pltpu.VMEM),
        scratch_shapes=[
            pltpu.VMEM(x_shape, BF),
            pltpu.VMEM(w_shape, BF),
            pltpu.SemaphoreType.DMA((16,)),
            pltpu.SemaphoreType.DMA((8,)),
        ],
        cost_estimate=pl.CostEstimate(flops=flops, bytes_accessed=10**7, transcendentals=0),
        compiler_params=pltpu.CompilerParams(vmem_limit_bytes=60 * 1024 * 1024),
    )


def cover_kernel(in_ref, out_ref):
    out_ref[...] = in_ref[...]


def cover(seed):
    return pl.pallas_call(
        cover_kernel,
        out_shape=jax.ShapeDtypeStruct(seed.shape, seed.dtype),
        cost_estimate=pl.CostEstimate(flops=3 * 10**10, bytes_accessed=10**8, transcendentals=0),
    )(seed)


def together(*values):
    return lax.optimization_barrier(values)


def after(value, *others):
    return lax.optimization_barrier((value,) + others)[0]


def prep_kernel(scal_ref, down_q_ref, down_o_ref, up_q_ref, up_o_ref, out_ref):
    start = 0
    for i, ref in ((0, down_q_ref), (2, down_o_ref), (1, up_q_ref), (3, up_o_ref)):
        width = ref.shape[1]
        mine = scal_ref[1 + i] == scal_ref[0]
        out_ref[:, start : start + width] = jnp.where(mine, ref[...].astype(F32), 0.0).astype(BF)
        start += width


def prepare(rank, tp, owners, down_q, down_o, up_q, up_o):
    scal = jnp.concatenate([rank[None], owners, tp[None]]).astype(jnp.int32)
    width = 2 * (WIDTH + QCOLS)
    return pl.pallas_call(
        prep_kernel,
        out_shape=jax.ShapeDtypeStruct((RANK, width), BF),
        grid_spec=pltpu.PrefetchScalarGridSpec(
            num_scalar_prefetch=1,
            grid=(1,),
            in_specs=[
                pl.BlockSpec((RANK, WIDTH), lambda i, sc: (0, sc[5])),
                pl.BlockSpec((RANK, QCOLS), lambda i, sc: (0, 0)),
                pl.BlockSpec((RANK, QCOLS), lambda i, sc: (0, 0)),
                pl.BlockSpec((RANK, WIDTH), lambda i, sc: (0, sc[5])),
            ],
            out_specs=pl.BlockSpec((RANK, width), lambda i, sc: (0, 0)),
        ),
        cost_estimate=pl.CostEstimate(flops=3 * 10**10, bytes_accessed=10**8, transcendentals=0),
        compiler_params=pltpu.CompilerParams(vmem_limit_bytes=16 * 1024 * 1024),
    )(scal, down_q, down_o, up_q, up_o)


def copies(piece, axis, n):
    everywhere = jnp.broadcast_to(piece[None], (n,) + piece.shape)
    return lax.all_to_all(everywhere, axis, 0, 0)


def spread(part, axis):
    got = copies(part, axis, SIZES[axis])
    return got[0] + got[1] + got[2] + got[3]


def column_piece(weight, rank, tp):
    piece = lax.dynamic_slice(
        weight, ((rank % 4) * PIECE, (tp ^ (rank // 4)) * WIDTH), (PIECE, WIDTH)
    )
    return piece


def to_columns(piece):
    pairs = []
    for r in range(32):
        for t in range(8):
            pairs.append((r * 8 + t, r * 8 + (t ^ (r // 4))))
    return lax.ppermute(piece, AXES, pairs)


SHIFTS = [(a, d) for a in range(2) for d in range(4)]


def shards(
    tokens,
    norm_gain_vector,
    keys,
    values,
    query_frozen_weight,
    output_frozen_weight,
    query_update_first,
    query_update_second,
    output_update_first,
    output_update_second,
    owners,
    frame_block_number,
):
    zh, y, c = (lax.axis_index(a) for a in CTX)
    tp = lax.axis_index("zl") * 4 + lax.axis_index("x")
    rank = zh * 8 + y * 2 + c

    half = RANK // 2
    half_rows = ROWS // 2
    left = shift(tokens, "x", 1)
    right = shift(tokens, "x", -1)
    other = shift(tokens, "zl", 1)
    factors = prepare(
        rank,
        tp,
        owners,
        query_update_first[0].T,
        output_update_first[0].T,
        query_update_second[0],
        output_update_second[0],
    )
    gain = jnp.pad(norm_gain_vector.reshape(WIDTH // HS, HS), ((0, 16 - WIDTH // HS), (0, 0)))
    gain = copies(gain, TP, 8)
    seed = jnp.zeros((8, HS), F32)
    kv = jnp.concatenate([keys, values], axis=1)
    left, right, other, factors, seed, gain = together(left, right, other, factors, seed, gain)

    columns = column_piece(output_frozen_weight, rank, tp)
    columns = to_columns(after(columns, left))
    other_left = shift(other, "x", 1)
    other_right = shift(other, "x", -1)
    factors = factors + shift(factors, "c", 1)
    part = lax.dynamic_slice_in_dim(factors, c * half, half, 0)
    part = spread(part, "zh")
    seed = cover(seed)
    other_left, other_right, part, seed, columns, kv = together(
        other_left, other_right, part, seed, columns, kv
    )

    kv = lax.all_gather(kv, ("zh", "c"), axis=0, tiled=True)
    far_left = shift(jnp.concatenate([left[:half_rows], other_left[:half_rows]]), "x", 1)
    far_right = shift(jnp.concatenate([right[half_rows:], other_right[half_rows:]]), "x", -1)
    part = spread(part, "y")
    seed = cover(seed)
    far_left, far_right, part, seed, columns = together(
        far_left, far_right, part, seed, columns
    )
    columns = lax.all_gather(columns, CTX, axis=0, tiled=True)

    order = jnp.stack([tp_source(a, d) for a, d in SHIFTS])
    mine = copies(part[:, : WIDTH + QCOLS], TP, 8)
    ups = part[:, WIDTH + QCOLS :]
    ups_other = shift(ups, "c", 1)
    normed = vmem_call(
        norm_kernel,
        jax.ShapeDtypeStruct((8, ROWS, WIDTH), BF),
        1,
        9,
        flops=10**10,
        nbytes=4 * 10**7,
        mib=24,
    )(order, gain, tokens, left, far_left, right, other, other_left, far_right, other_right)
    mine, normed = together(mine, normed)
    theirs = shift(mine, "c", 1)
    queries = fetch_call(
        query_kernel,
        jax.ShapeDtypeStruct((ROWS, QCOLS), BF),
        4,
        2,
        (8, ROWS, WIDTH),
        (8, WIDTH, QCOLS),
        2 * ROWS * 8 * WIDTH * QCOLS + 2 * 8 * WIDTH * RANK * QCOLS,
    )(order, mine, theirs, ups, ups_other, normed, query_frozen_weight)

    order_out = jnp.stack([tp ^ i for i in range(8)])
    out_merged = merge_out(order_out, columns, mine, theirs, ups, ups_other)

    counts = jnp.sum(
        (frame_block_number[None, :] <= frame_block_number[:, None]).astype(jnp.int32), axis=1
    )
    vis_end = counts * FTOK
    kframes = (jnp.arange(CHUNKS, dtype=jnp.int32) * 8 + y * 2) * FRAMES_DEV

    def frames_of(step):
        return (zh * 8 + ((y - step) % 4) * 2 + c) * FRAMES_DEV

    q_left = shift(queries, "y", 1)
    q_right = shift(queries, "y", -1)
    q_far = shift(queries, "y", 2)
    (own,) = attention([queries], [frames_of(0)], kframes, vis_end, kv)
    q_left = after(q_left, own)
    left, right, far = attention(
        [q_left, q_right, q_far],
        [frames_of(1), frames_of(-1), frames_of(2)],
        kframes,
        vis_end,
        kv,
    )
    back_left = shift(left, "y", -1)
    back_right = shift(right, "y", 1)
    back_far = shift(far, "y", 2)

    attended = vmem_call(combine_kernel, jax.ShapeDtypeStruct((ROWS, QCOLS), BF), 0, 4, nbytes=10**6)(
        own, back_left, back_right, back_far
    )
    left = shift(attended, "x", 1)
    right = shift(attended, "x", -1)
    other = shift(attended, "zl", 1)
    other_left = shift(other, "x", 1)
    other_right = shift(other, "x", -1)
    far_left = shift(jnp.concatenate([left[:half_rows], other_left[:half_rows]]), "x", 1)
    far_right = shift(jnp.concatenate([right[half_rows:], other_right[half_rows:]]), "x", -1)
    slots = jnp.stack([tp ^ tp_source(a, d) for a, d in SHIFTS])
    return fetch_call(
        project_kernel,
        jax.ShapeDtypeStruct((ROWS, WIDTH), BF),
        0,
        9,
        (8, ROWS, QCOLS),
        (8, QCOLS, WIDTH),
        2 * ROWS * 8 * WIDTH * QCOLS,
    )(slots, attended, left, far_left, right, other, other_left, far_right, other_right, out_merged)


def solution(mesh):
    fine = Mesh(mesh.devices.reshape([SIZES[a] for a in AXES]), AXES)
    in_specs = (
        P(CTX, TP),
        P(TP),
        P(CTX, TP),
        P(CTX, TP),
        P(None, TP),
        P(TP, None),
        P(CTX, None, None),
        P(CTX, None, TP),
        P(CTX, TP, None),
        P(CTX, None, None),
        P(),
        P(),
    )
    return jax.shard_map(
        shards, mesh=fine, in_specs=in_specs, out_specs=P(CTX, TP), check_vma=False
    )
```

```python
import functools
import math

import jax
import jax.numpy as jnp
from jax import lax
from jax.experimental import pallas as pl
from jax.experimental.pallas import tpu as pltpu
from jax.sharding import Mesh
from jax.sharding import PartitionSpec as P

HS = 128
FTOK = 64
ROWS = 320
FRAMES_DEV = 5
WIDTH = 768
RANK = 64
HEADS_DEV = 3
QCOLS = HEADS_DEV * HS
CHUNK = 2 * ROWS
CHUNKS = 4
NEG = -1e30
PIECE = 96
EPS = 1e-6
AXES = ("zh", "y", "c", "zl", "x")
SIZES = {"zh": 4, "y": 4, "c": 2, "zl": 2, "x": 4}
CTX = ("zh", "y", "c")
TP = ("zl", "x")
EXP_SCALE = (HS ** (-0.5)) * math.log2(math.e)
BF = jnp.bfloat16
F32 = jnp.float32


def shift(v, axis, step):
    n = SIZES[axis]
    return lax.ppermute(v, axis, [(i, (i + step) % n) for i in range(n)])


def tp_source(a, d):
    return (lax.axis_index("zl") ^ a) * 4 + (lax.axis_index("x") - d) % 4


def vmem_call(body, out_shape, n_smem, n_vmem, scratch=(), flops=0, nbytes=0, mib=16, n_any=0):
    return pl.pallas_call(
        body,
        out_shape=out_shape,
        in_specs=[pl.BlockSpec(memory_space=pltpu.SMEM)] * n_smem
        + [pl.BlockSpec(memory_space=pltpu.VMEM)] * n_vmem
        + [pl.BlockSpec(memory_space=pl.ANY)] * n_any,
        scratch_shapes=list(scratch),
        cost_estimate=pl.CostEstimate(flops=flops, bytes_accessed=nbytes, transcendentals=0),
        compiler_params=pltpu.CompilerParams(vmem_limit_bytes=mib * 1024 * 1024),
    )


def tdot(a, b):
    return lax.dot_general(a, b, (((0,), (0,)), ((), ())), preferred_element_type=F32)


def norm_kernel(order_ref, gain_ref, *refs):
    parts, out_ref = refs[:8], refs[8]
    half = ROWS // 2

    def block(i):
        if i in (2, 6):
            rows = slice(0, half) if i == 2 else slice(half, ROWS)
            return jnp.concatenate([parts[2][rows, :], parts[6][rows, :]], axis=0)
        return parts[i][...]

    total = jnp.zeros((ROWS, HS), F32)
    for i in range(8):
        v = block(i).astype(F32)
        v = v * v
        for g in range(WIDTH // HS):
            total = total + v[:, g * HS : (g + 1) * HS]
    total = jnp.sum(total, axis=1, keepdims=True)
    inv = lax.rsqrt(total * (1.0 / (8 * WIDTH)) + EPS)
    for i in range(8):
        at = order_ref[i]
        gain = jnp.concatenate(
            [gain_ref[at, r : r + 1, :].astype(F32) for r in range(WIDTH // HS)], axis=1
        )
        out_ref[i] = (block(i).astype(F32) * inv * gain).astype(BF)


def query_kernel(
    order_ref, mine_ref, other_ref, up_ref, up_other_ref, x_ref, w_ref, out_ref, xs, ws, x_sems, w_sems
):
    copies_in = []
    for i in range(8):
        rows = pl.ds(pl.multiple_of(order_ref[i] * WIDTH, WIDTH), WIDTH)
        copies_in.append(
            (
                pltpu.make_async_copy(w_ref.at[rows, :], ws.at[i], w_sems.at[i]),
                pltpu.make_async_copy(x_ref.at[i], xs.at[i], x_sems.at[i]),
            )
        )
        for copy in copies_in[i]:
            copy.start()
    acc = jnp.zeros((ROWS, QCOLS), F32)
    up = jnp.concatenate([up_ref[:, :QCOLS], up_other_ref[:, :QCOLS]], axis=0)
    for i in range(8):
        at = order_ref[i]
        down = jnp.concatenate([mine_ref[at, :, :WIDTH], other_ref[at, :, :WIDTH]], axis=0)
        copies_in[i][0].wait()
        merged = (ws[i].astype(F32) + tdot(down, up)).astype(BF)
        copies_in[i][1].wait()
        acc = acc + jnp.dot(xs[i], merged, preferred_element_type=F32)
    out_ref[...] = acc.astype(BF)


def attention_kernel(n, qframe_ref, kframe_ref, vis_ref, *refs):
    q_refs = refs[:n]
    kv_ref = refs[n]
    o_refs = refs[n + 1 :]
    lane = lax.broadcasted_iota(jnp.int32, (ROWS, HS), 1)
    row = lax.broadcasted_iota(jnp.int32, (ROWS, HS), 0)

    def heads(b, first, chunks):
        width = chunks * CHUNK
        last = kframe_ref[chunks - 1] * FTOK
        limit = jnp.full((ROWS, HS), vis_ref[first] - last, jnp.int32)
        for f in range(1, FRAMES_DEV):
            limit = jnp.where(row >= f * FTOK, vis_ref[first + f] - last, limit)
        seen = jnp.concatenate([lane + g * HS for g in range(CHUNK // HS)], axis=1)
        seen = seen < jnp.concatenate([limit] * (CHUNK // HS), axis=1)

        def scores(h):
            cols = slice(h * HS, (h + 1) * HS)
            return lax.dot_general(
                q_refs[b][:, cols],
                kv_ref[:width, cols],
                (((1,), (1,)), ((), ())),
                preferred_element_type=F32,
            )

        s = scores(0)
        stats = jnp.zeros((ROWS, HS), F32)
        for h in range(HEADS_DEV):
            ahead = scores(h + 1) if h + 1 < HEADS_DEV else None
            tail = jnp.where(seen, s[:, width - CHUNK :], NEG)
            s = jnp.concatenate([s[:, : width - CHUNK], tail], axis=1) if chunks > 1 else tail
            top = jnp.broadcast_to(jnp.max(s, axis=1, keepdims=True), (ROWS, HS))
            p = jnp.exp2((s - jnp.concatenate([top] * (width // HS), axis=1)) * EXP_SCALE)
            lanes = p[:, :HS]
            for g in range(1, width // HS):
                lanes = lanes + p[:, g * HS : (g + 1) * HS]
            total = jnp.broadcast_to(jnp.sum(lanes, axis=1, keepdims=True), (ROWS, HS))
            acc = jnp.dot(
                p.astype(BF),
                kv_ref[:width, QCOLS + h * HS : QCOLS + (h + 1) * HS],
                preferred_element_type=F32,
            )
            has = top > 0.5 * NEG
            o_refs[b][:, h * HS : (h + 1) * HS] = jnp.where(has, acc / total, 0.0).astype(BF)
            level = jnp.where(has, top * EXP_SCALE + jnp.log2(total), NEG)
            high = level.astype(BF).astype(F32)
            mid = (level - high).astype(BF).astype(F32)
            low = level - high - mid
            stats = jnp.where(lane == 3 * h, high, stats)
            stats = jnp.where(lane == 3 * h + 1, mid, stats)
            stats = jnp.where(lane == 3 * h + 2, low, stats)
            s = ahead
        o_refs[b][:, QCOLS:] = stats.astype(BF)

    for b in range(n):
        first = qframe_ref[b]
        end = vis_ref[first + FRAMES_DEV - 1]
        some = jnp.int32(0)
        for j in range(CHUNKS):
            some = some + (kframe_ref[j] * FTOK < end).astype(jnp.int32)

        @pl.when(some == 0)
        def _(b=b):
            o_refs[b][:, :QCOLS] = jnp.zeros((ROWS, QCOLS), BF)
            blank = jnp.where((lane < 3 * HEADS_DEV) & (lane % 3 == 0), NEG, 0.0)
            o_refs[b][:, QCOLS:] = blank.astype(BF)

        for chunks in range(1, CHUNKS + 1):

            @pl.when(some == chunks)
            def _(b=b, first=first, chunks=chunks):
                heads(b, first, chunks)


def attention(queries, qframes, kframes, vis_end, kv):
    n = len(queries)
    return vmem_call(
        functools.partial(attention_kernel, n),
        [jax.ShapeDtypeStruct((ROWS, QCOLS + HS), BF)] * n,
        3,
        n + 1,
        flops=n * 8 * ROWS * QCOLS * CHUNK * CHUNKS,
        nbytes=CHUNKS * CHUNK * 2 * QCOLS * 2,
        mib=24,
    )(jnp.stack(qframes), kframes, vis_end, *queries, kv)


def combine_kernel(*refs):
    parts, out_ref = refs[:4], refs[4]
    stats = [p[:, QCOLS:].astype(F32) for p in parts]
    for h in range(HEADS_DEV):
        levels = []
        for s in stats:
            levels.append(
                s[:, 3 * h : 3 * h + 1] + s[:, 3 * h + 1 : 3 * h + 2] + s[:, 3 * h + 2 : 3 * h + 3]
            )
        top = functools.reduce(jnp.maximum, levels)
        shares = [jnp.exp2(v - top) for v in levels]
        total = shares[0] + shares[1] + shares[2] + shares[3]
        cols = slice(h * HS, (h + 1) * HS)
        acc = jnp.zeros((ROWS, HS), F32)
        for p, w in zip(parts, shares):
            acc = acc + p[:, cols].astype(F32) * w
        out_ref[:, cols] = (acc / total).astype(BF)


def merge_out_kernel(order_ref, w_ref, mine_ref, other_ref, up_ref, up_other_ref, out_ref):
    at = order_ref[pl.program_id(0)]
    up = jnp.concatenate([up_ref[:, QCOLS:], up_other_ref[:, QCOLS:]], axis=0)
    cols = slice(WIDTH, WIDTH + QCOLS)
    down = jnp.concatenate([mine_ref[at, :, cols], other_ref[at, :, cols]], axis=0)
    out_ref[...] = (w_ref[...].astype(F32) + tdot(down, up)).astype(BF)


def merge_out(order, w, mine, other, up, up_other):
    def whole(shape):
        return pl.BlockSpec(shape, lambda i: (0,) * len(shape))

    return pl.pallas_call(
        merge_out_kernel,
        out_shape=jax.ShapeDtypeStruct((8 * QCOLS, WIDTH), BF),
        grid=(8,),
        in_specs=[
            pl.BlockSpec(memory_space=pltpu.SMEM),
            pl.BlockSpec((QCOLS, WIDTH), lambda i: (i, 0)),
            whole(mine.shape),
            whole(other.shape),
            whole(up.shape),
            whole(up_other.shape),
        ],
        out_specs=pl.BlockSpec((QCOLS, WIDTH), lambda i: (i, 0)),
        cost_estimate=pl.CostEstimate(
            flops=10**10, bytes_accessed=4 * 10**7, transcendentals=0
        ),
        compiler_params=pltpu.CompilerParams(vmem_limit_bytes=16 * 1024 * 1024),
    )(order, w, mine, other, up, up_other)


def project_kernel(order_ref, *refs):
    parts, w_ref, out_ref, xs, ws, x_sems, w_sems = refs[:8], *refs[8:]
    half = ROWS // 2
    waits = []
    for i in range(8):
        rows = pl.ds(pl.multiple_of(order_ref[i] * QCOLS, QCOLS), QCOLS)
        mine = [pltpu.make_async_copy(w_ref.at[rows, :], ws.at[i], w_sems.at[i])]
        if i in (2, 6):
            src = slice(0, half) if i == 2 else slice(half, ROWS)
            for k, side in enumerate((2, 6)):
                dst = xs.at[i, k * half : (k + 1) * half, :]
                mine.append(
                    pltpu.make_async_copy(parts[side].at[src, :], dst, x_sems.at[i + 8 * k])
                )
        else:
            mine.append(pltpu.make_async_copy(parts[i], xs.at[i], x_sems.at[i]))
        for copy in mine:
            copy.start()
        waits.append(mine)
    acc = jnp.zeros((ROWS, WIDTH), F32)
    for i in range(8):
        for copy in waits[i]:
            copy.wait()
        acc = acc + jnp.dot(xs[i], ws[i], preferred_element_type=F32)
    out_ref[...] = acc.astype(BF)


def fetch_call(body, out_shape, n_vmem, n_any, x_shape, w_shape, flops):
    return pl.pallas_call(
        body,
        out_shape=out_shape,
        in_specs=[pl.BlockSpec(memory_space=pltpu.SMEM)]
        + [pl.BlockSpec(memory_space=pltpu.VMEM)] * n_vmem
        + [pl.BlockSpec(memory_space=pl.ANY)] * n_any,
        out_specs=pl.BlockSpec(memory_space=pltpu.VMEM),
        scratch_shapes=[
            pltpu.VMEM(x_shape, BF),
            pltpu.VMEM(w_shape, BF),
            pltpu.SemaphoreType.DMA((16,)),
            pltpu.SemaphoreType.DMA((8,)),
        ],
        cost_estimate=pl.CostEstimate(flops=flops, bytes_accessed=10**7, transcendentals=0),
        compiler_params=pltpu.CompilerParams(vmem_limit_bytes=60 * 1024 * 1024),
    )


def cover_kernel(in_ref, out_ref):
    out_ref[...] = in_ref[...]


def cover(seed):
    return pl.pallas_call(
        cover_kernel,
        out_shape=jax.ShapeDtypeStruct(seed.shape, seed.dtype),
        cost_estimate=pl.CostEstimate(flops=3 * 10**10, bytes_accessed=10**8, transcendentals=0),
    )(seed)


def together(*values):
    return lax.optimization_barrier(values)


def after(value, *others):
    return lax.optimization_barrier((value,) + others)[0]


def prep_kernel(scal_ref, down_q_ref, down_o_ref, up_q_ref, up_o_ref, out_ref):
    start = 0
    for i, ref in ((0, down_q_ref), (2, down_o_ref), (1, up_q_ref), (3, up_o_ref)):
        width = ref.shape[1]
        mine = scal_ref[1 + i] == scal_ref[0]
        out_ref[:, start : start + width] = jnp.where(mine, ref[...].astype(F32), 0.0).astype(BF)
        start += width


def prepare(rank, tp, owners, down_q, down_o, up_q, up_o):
    scal = jnp.concatenate([rank[None], owners, tp[None]]).astype(jnp.int32)
    width = 2 * (WIDTH + QCOLS)
    return pl.pallas_call(
        prep_kernel,
        out_shape=jax.ShapeDtypeStruct((RANK, width), BF),
        grid_spec=pltpu.PrefetchScalarGridSpec(
            num_scalar_prefetch=1,
            grid=(1,),
            in_specs=[
                pl.BlockSpec((RANK, WIDTH), lambda i, sc: (0, sc[5])),
                pl.BlockSpec((RANK, QCOLS), lambda i, sc: (0, 0)),
                pl.BlockSpec((RANK, QCOLS), lambda i, sc: (0, 0)),
                pl.BlockSpec((RANK, WIDTH), lambda i, sc: (0, sc[5])),
            ],
            out_specs=pl.BlockSpec((RANK, width), lambda i, sc: (0, 0)),
        ),
        cost_estimate=pl.CostEstimate(flops=3 * 10**10, bytes_accessed=10**8, transcendentals=0),
        compiler_params=pltpu.CompilerParams(vmem_limit_bytes=16 * 1024 * 1024),
    )(scal, down_q, down_o, up_q, up_o)


def copies(piece, axis, n):
    everywhere = jnp.broadcast_to(piece[None], (n,) + piece.shape)
    return lax.all_to_all(everywhere, axis, 0, 0)


def spread(part, axis):
    got = copies(part, axis, SIZES[axis])
    return got[0] + got[1] + got[2] + got[3]


def column_piece(weight, rank, tp):
    piece = lax.dynamic_slice(
        weight, ((rank % 4) * PIECE, (tp ^ (rank // 4)) * WIDTH), (PIECE, WIDTH)
    )
    return piece


def to_columns(piece):
    pairs = []
    for r in range(32):
        for t in range(8):
            pairs.append((r * 8 + t, r * 8 + (t ^ (r // 4))))
    return lax.ppermute(piece, AXES, pairs)


SHIFTS = [(a, d) for a in range(2) for d in range(4)]


def shards(
    tokens,
    norm_gain_vector,
    keys,
    values,
    query_frozen_weight,
    output_frozen_weight,
    query_update_first,
    query_update_second,
    output_update_first,
    output_update_second,
    owners,
    frame_block_number,
):
    zh, y, c = (lax.axis_index(a) for a in CTX)
    tp = lax.axis_index("zl") * 4 + lax.axis_index("x")
    rank = zh * 8 + y * 2 + c

    half = RANK // 2
    half_rows = ROWS // 2
    left = shift(tokens, "x", 1)
    right = shift(tokens, "x", -1)
    other = shift(tokens, "zl", 1)
    factors = prepare(
        rank,
        tp,
        owners,
        query_update_first[0].T,
        output_update_first[0].T,
        query_update_second[0],
        output_update_second[0],
    )
    factors = factors + shift(factors, "c", 1)
    part = lax.dynamic_slice_in_dim(factors, c * half, half, 0)
    seed = jnp.zeros((8, HS), F32)
    kv = jnp.concatenate([keys, values], axis=1)
    left, right, other, part, seed, kv = together(left, right, other, part, seed, kv)

    kv = lax.all_gather(kv, ("zh", "c"), axis=0, tiled=True)
    other_left = shift(other, "x", 1)
    other_right = shift(other, "x", -1)
    part = spread(part, "zh")
    columns = column_piece(output_frozen_weight, rank, tp)
    columns = to_columns(after(columns, left))
    gain = jnp.pad(norm_gain_vector.reshape(WIDTH // HS, HS), ((0, 16 - WIDTH // HS), (0, 0)))
    gain = copies(after(gain, right), TP, 8)
    seed = cover(seed)
    other_left, other_right, part, seed, columns, gain = together(
        other_left, other_right, part, seed, columns, gain
    )

    far_left = shift(jnp.concatenate([left[:half_rows], other_left[:half_rows]]), "x", 1)
    far_right = shift(jnp.concatenate([right[half_rows:], other_right[half_rows:]]), "x", -1)
    part = spread(part, "y")
    seed = cover(seed)
    far_left, far_right, part, seed, columns = together(
        far_left, far_right, part, seed, columns
    )
    columns = lax.all_gather(columns, CTX, axis=0, tiled=True)

    order = jnp.stack([tp_source(a, d) for a, d in SHIFTS])
    mine = copies(part[:, : WIDTH + QCOLS], TP, 8)
    ups = part[:, WIDTH + QCOLS :]
    ups_other = shift(ups, "c", 1)
    normed = vmem_call(
        norm_kernel,
        jax.ShapeDtypeStruct((8, ROWS, WIDTH), BF),
        1,
        9,
        flops=10**10,
        nbytes=4 * 10**7,
        mib=24,
    )(order, gain, tokens, left, far_left, right, other, other_left, far_right, other_right)
    mine, normed = together(mine, normed)
    theirs = shift(mine, "c", 1)
    queries = fetch_call(
        query_kernel,
        jax.ShapeDtypeStruct((ROWS, QCOLS), BF),
        4,
        2,
        (8, ROWS, WIDTH),
        (8, WIDTH, QCOLS),
        2 * ROWS * 8 * WIDTH * QCOLS + 2 * 8 * WIDTH * RANK * QCOLS,
    )(order, mine, theirs, ups, ups_other, normed, query_frozen_weight)

    order_out = jnp.stack([tp ^ i for i in range(8)])
    out_merged = merge_out(order_out, columns, mine, theirs, ups, ups_other)

    counts = jnp.sum(
        (frame_block_number[None, :] <= frame_block_number[:, None]).astype(jnp.int32), axis=1
    )
    vis_end = counts * FTOK
    kframes = (jnp.arange(CHUNKS, dtype=jnp.int32) * 8 + y * 2) * FRAMES_DEV

    def frames_of(step):
        return (zh * 8 + ((y - step) % 4) * 2 + c) * FRAMES_DEV

    q_left = shift(queries, "y", 1)
    q_right = shift(queries, "y", -1)
    q_far = shift(queries, "y", 2)
    (own,) = attention([queries], [frames_of(0)], kframes, vis_end, kv)
    q_left = after(q_left, own)
    (left,) = attention([q_left], [frames_of(1)], kframes, vis_end, kv)
    back_left = shift(left, "y", -1)
    (right,) = attention([q_right], [frames_of(-1)], kframes, vis_end, kv)
    back_right = shift(right, "y", 1)
    (far,) = attention([q_far], [frames_of(2)], kframes, vis_end, kv)
    back_far = shift(far, "y", 2)

    attended = vmem_call(combine_kernel, jax.ShapeDtypeStruct((ROWS, QCOLS), BF), 0, 4, nbytes=10**6)(
        own, back_left, back_right, back_far
    )
    left = shift(attended, "x", 1)
    right = shift(attended, "x", -1)
    other = shift(attended, "zl", 1)
    other_left = shift(other, "x", 1)
    other_right = shift(other, "x", -1)
    other_left, other_right, out_merged = together(other_left, other_right, out_merged)
    far_left = shift(jnp.concatenate([left[:half_rows], other_left[:half_rows]]), "x", 1)
    far_right = shift(jnp.concatenate([right[half_rows:], other_right[half_rows:]]), "x", -1)
    slots = jnp.stack([tp ^ tp_source(a, d) for a, d in SHIFTS])
    return fetch_call(
        project_kernel,
        jax.ShapeDtypeStruct((ROWS, WIDTH), BF),
        0,
        9,
        (8, ROWS, QCOLS),
        (8, QCOLS, WIDTH),
        2 * ROWS * 8 * WIDTH * QCOLS,
    )(slots, attended, left, far_left, right, other, other_left, far_right, other_right, out_merged)


def solution(mesh):
    fine = Mesh(mesh.devices.reshape([SIZES[a] for a in AXES]), AXES)
    in_specs = (
        P(CTX, TP),
        P(TP),
        P(CTX, TP),
        P(CTX, TP),
        P(None, TP),
        P(TP, None),
        P(CTX, None, None),
        P(CTX, None, TP),
        P(CTX, TP, None),
        P(CTX, None, None),
        P(),
        P(),
    )
    return jax.shard_map(
        shards, mesh=fine, in_specs=in_specs, out_specs=P(CTX, TP), check_vma=False
    )
```

```python
import functools
import math

import jax
import jax.numpy as jnp
from jax import lax
from jax.experimental import pallas as pl
from jax.experimental.pallas import tpu as pltpu
from jax.sharding import Mesh
from jax.sharding import PartitionSpec as P

HS = 128
FTOK = 64
ROWS = 320
FRAMES_DEV = 5
WIDTH = 768
RANK = 64
HEADS_DEV = 3
QCOLS = HEADS_DEV * HS
CHUNK = 2 * ROWS
CHUNKS = 4
NEG = -1e30
PIECE = 96
EPS = 1e-6
AXES = ("zh", "y", "c", "zl", "x")
SIZES = {"zh": 4, "y": 4, "c": 2, "zl": 2, "x": 4}
CTX = ("zh", "y", "c")
TP = ("zl", "x")
EXP_SCALE = (HS ** (-0.5)) * math.log2(math.e)
BF = jnp.bfloat16
F32 = jnp.float32


def shift(v, axis, step):
    n = SIZES[axis]
    return lax.ppermute(v, axis, [(i, (i + step) % n) for i in range(n)])


def tp_source(a, d):
    return (lax.axis_index("zl") ^ a) * 4 + (lax.axis_index("x") - d) % 4


def vmem_call(body, out_shape, n_smem, n_vmem, scratch=(), flops=0, nbytes=0, mib=16, n_any=0):
    return pl.pallas_call(
        body,
        out_shape=out_shape,
        in_specs=[pl.BlockSpec(memory_space=pltpu.SMEM)] * n_smem
        + [pl.BlockSpec(memory_space=pltpu.VMEM)] * n_vmem
        + [pl.BlockSpec(memory_space=pl.ANY)] * n_any,
        scratch_shapes=list(scratch),
        cost_estimate=pl.CostEstimate(flops=flops, bytes_accessed=nbytes, transcendentals=0),
        compiler_params=pltpu.CompilerParams(vmem_limit_bytes=mib * 1024 * 1024),
    )


def tdot(a, b):
    return lax.dot_general(a, b, (((0,), (0,)), ((), ())), preferred_element_type=F32)


def norm_kernel(order_ref, gain_ref, *refs):
    parts, out_ref = refs[:8], refs[8]
    half = ROWS // 2

    def block(i):
        if i in (2, 6):
            rows = slice(0, half) if i == 2 else slice(half, ROWS)
            return jnp.concatenate([parts[2][rows, :], parts[6][rows, :]], axis=0)
        return parts[i][...]

    total = jnp.zeros((ROWS, HS), F32)
    for i in range(8):
        v = block(i).astype(F32)
        v = v * v
        for g in range(WIDTH // HS):
            total = total + v[:, g * HS : (g + 1) * HS]
    total = jnp.sum(total, axis=1, keepdims=True)
    inv = lax.rsqrt(total * (1.0 / (8 * WIDTH)) + EPS)
    for i in range(8):
        at = order_ref[i]
        gain = jnp.concatenate(
            [gain_ref[at, r : r + 1, :].astype(F32) for r in range(WIDTH // HS)], axis=1
        )
        out_ref[i] = (block(i).astype(F32) * inv * gain).astype(BF)


def query_kernel(
    order_ref, mine_ref, other_ref, up_ref, up_other_ref, x_ref, w_ref, out_ref, xs, ws, x_sems, w_sems
):
    copies_in = []
    for i in range(8):
        rows = pl.ds(pl.multiple_of(order_ref[i] * WIDTH, WIDTH), WIDTH)
        copies_in.append(
            (
                pltpu.make_async_copy(w_ref.at[rows, :], ws.at[i], w_sems.at[i]),
                pltpu.make_async_copy(x_ref.at[i], xs.at[i], x_sems.at[i]),
            )
        )
        for copy in copies_in[i]:
            copy.start()
    acc = jnp.zeros((ROWS, QCOLS), F32)
    up = jnp.concatenate([up_ref[:, :QCOLS], up_other_ref[:, :QCOLS]], axis=0)
    for i in range(8):
        at = order_ref[i]
        down = jnp.concatenate([mine_ref[at, :, :WIDTH], other_ref[at, :, :WIDTH]], axis=0)
        copies_in[i][0].wait()
        merged = (ws[i].astype(F32) + tdot(down, up)).astype(BF)
        copies_in[i][1].wait()
        acc = acc + jnp.dot(xs[i], merged, preferred_element_type=F32)
    out_ref[...] = acc.astype(BF)


def attention_kernel(n, qframe_ref, kframe_ref, vis_ref, *refs):
    q_refs = refs[:n]
    kv_ref = refs[n]
    o_refs = refs[n + 1 :]
    lane = lax.broadcasted_iota(jnp.int32, (ROWS, HS), 1)
    row = lax.broadcasted_iota(jnp.int32, (ROWS, HS), 0)

    def heads(b, first, chunks):
        width = chunks * CHUNK
        last = kframe_ref[chunks - 1] * FTOK
        limit = jnp.full((ROWS, HS), vis_ref[first] - last, jnp.int32)
        for f in range(1, FRAMES_DEV):
            limit = jnp.where(row >= f * FTOK, vis_ref[first + f] - last, limit)
        seen = jnp.concatenate([lane + g * HS for g in range(CHUNK // HS)], axis=1)
        seen = seen < jnp.concatenate([limit] * (CHUNK // HS), axis=1)

        def scores(h):
            cols = slice(h * HS, (h + 1) * HS)
            return lax.dot_general(
                q_refs[b][:, cols],
                kv_ref[:width, cols],
                (((1,), (1,)), ((), ())),
                preferred_element_type=F32,
            )

        s = scores(0)
        stats = jnp.zeros((ROWS, HS), F32)
        for h in range(HEADS_DEV):
            ahead = scores(h + 1) if h + 1 < HEADS_DEV else None
            tail = jnp.where(seen, s[:, width - CHUNK :], NEG)
            s = jnp.concatenate([s[:, : width - CHUNK], tail], axis=1) if chunks > 1 else tail
            top = jnp.broadcast_to(jnp.max(s, axis=1, keepdims=True), (ROWS, HS))
            p = jnp.exp2((s - jnp.concatenate([top] * (width // HS), axis=1)) * EXP_SCALE)
            lanes = p[:, :HS]
            for g in range(1, width // HS):
                lanes = lanes + p[:, g * HS : (g + 1) * HS]
            total = jnp.broadcast_to(jnp.sum(lanes, axis=1, keepdims=True), (ROWS, HS))
            acc = jnp.dot(
                p.astype(BF),
                kv_ref[:width, QCOLS + h * HS : QCOLS + (h + 1) * HS],
                preferred_element_type=F32,
            )
            has = top > 0.5 * NEG
            o_refs[b][:, h * HS : (h + 1) * HS] = jnp.where(has, acc / total, 0.0).astype(BF)
            level = jnp.where(has, top * EXP_SCALE + jnp.log2(total), NEG)
            high = level.astype(BF).astype(F32)
            mid = (level - high).astype(BF).astype(F32)
            low = level - high - mid
            stats = jnp.where(lane == 3 * h, high, stats)
            stats = jnp.where(lane == 3 * h + 1, mid, stats)
            stats = jnp.where(lane == 3 * h + 2, low, stats)
            s = ahead
        o_refs[b][:, QCOLS:] = stats.astype(BF)

    for b in range(n):
        first = qframe_ref[b]
        end = vis_ref[first + FRAMES_DEV - 1]
        some = jnp.int32(0)
        for j in range(CHUNKS):
            some = some + (kframe_ref[j] * FTOK < end).astype(jnp.int32)

        @pl.when(some == 0)
        def _(b=b):
            o_refs[b][:, :QCOLS] = jnp.zeros((ROWS, QCOLS), BF)
            blank = jnp.where((lane < 3 * HEADS_DEV) & (lane % 3 == 0), NEG, 0.0)
            o_refs[b][:, QCOLS:] = blank.astype(BF)

        for chunks in range(1, CHUNKS + 1):

            @pl.when(some == chunks)
            def _(b=b, first=first, chunks=chunks):
                heads(b, first, chunks)


def attention(queries, qframes, kframes, vis_end, kv):
    n = len(queries)
    return vmem_call(
        functools.partial(attention_kernel, n),
        [jax.ShapeDtypeStruct((ROWS, QCOLS + HS), BF)] * n,
        3,
        n + 1,
        flops=n * 8 * ROWS * QCOLS * CHUNK * CHUNKS,
        nbytes=CHUNKS * CHUNK * 2 * QCOLS * 2,
        mib=24,
    )(jnp.stack(qframes), kframes, vis_end, *queries, kv)


def combine_kernel(*refs):
    parts, out_ref = refs[:4], refs[4]
    stats = [p[:, QCOLS:].astype(F32) for p in parts]
    for h in range(HEADS_DEV):
        levels = []
        for s in stats:
            levels.append(
                s[:, 3 * h : 3 * h + 1] + s[:, 3 * h + 1 : 3 * h + 2] + s[:, 3 * h + 2 : 3 * h + 3]
            )
        top = functools.reduce(jnp.maximum, levels)
        shares = [jnp.exp2(v - top) for v in levels]
        total = shares[0] + shares[1] + shares[2] + shares[3]
        cols = slice(h * HS, (h + 1) * HS)
        acc = jnp.zeros((ROWS, HS), F32)
        for p, w in zip(parts, shares):
            acc = acc + p[:, cols].astype(F32) * w
        out_ref[:, cols] = (acc / total).astype(BF)


def project_kernel(order_ref, *refs):
    mine_ref, other_ref, up_ref, up_other_ref = refs[:4]
    parts, w_ref, out_ref, xs, ws, x_sems, w_sems = refs[4:12], *refs[12:]
    half = ROWS // 2
    waits = []
    for i in range(8):
        rows = pl.ds(pl.multiple_of(order_ref[8 + i] * QCOLS, QCOLS), QCOLS)
        mine = [pltpu.make_async_copy(w_ref.at[rows, :], ws.at[i], w_sems.at[i])]
        if i in (2, 6):
            src = slice(0, half) if i == 2 else slice(half, ROWS)
            for k, side in enumerate((2, 6)):
                dst = xs.at[i, k * half : (k + 1) * half, :]
                mine.append(
                    pltpu.make_async_copy(parts[side].at[src, :], dst, x_sems.at[i + 8 * k])
                )
        else:
            mine.append(pltpu.make_async_copy(parts[i], xs.at[i], x_sems.at[i]))
        for copy in mine:
            copy.start()
        waits.append(mine)
    acc = jnp.zeros((ROWS, WIDTH), F32)
    up = jnp.concatenate([up_ref[:, QCOLS:], up_other_ref[:, QCOLS:]], axis=0)
    cols = slice(WIDTH, WIDTH + QCOLS)
    for i in range(8):
        at = order_ref[i]
        down = jnp.concatenate([mine_ref[at, :, cols], other_ref[at, :, cols]], axis=0)
        for copy in waits[i]:
            copy.wait()
        merged = (ws[i].astype(F32) + tdot(down, up)).astype(BF)
        acc = acc + jnp.dot(xs[i], merged, preferred_element_type=F32)
    out_ref[...] = acc.astype(BF)


def fetch_call(body, out_shape, n_vmem, n_any, x_shape, w_shape, flops):
    return pl.pallas_call(
        body,
        out_shape=out_shape,
        in_specs=[pl.BlockSpec(memory_space=pltpu.SMEM)]
        + [pl.BlockSpec(memory_space=pltpu.VMEM)] * n_vmem
        + [pl.BlockSpec(memory_space=pl.ANY)] * n_any,
        out_specs=pl.BlockSpec(memory_space=pltpu.VMEM),
        scratch_shapes=[
            pltpu.VMEM(x_shape, BF),
            pltpu.VMEM(w_shape, BF),
            pltpu.SemaphoreType.DMA((16,)),
            pltpu.SemaphoreType.DMA((8,)),
        ],
        cost_estimate=pl.CostEstimate(flops=flops, bytes_accessed=10**7, transcendentals=0),
        compiler_params=pltpu.CompilerParams(vmem_limit_bytes=60 * 1024 * 1024),
    )


def cover_kernel(in_ref, out_ref):
    out_ref[...] = in_ref[...]


def cover(seed):
    return pl.pallas_call(
        cover_kernel,
        out_shape=jax.ShapeDtypeStruct(seed.shape, seed.dtype),
        cost_estimate=pl.CostEstimate(flops=3 * 10**10, bytes_accessed=10**8, transcendentals=0),
    )(seed)


def together(*values):
    return lax.optimization_barrier(values)


def after(value, *others):
    return lax.optimization_barrier((value,) + others)[0]


def prep_kernel(scal_ref, down_q_ref, down_o_ref, up_q_ref, up_o_ref, out_ref):
    start = 0
    for i, ref in ((0, down_q_ref), (2, down_o_ref), (1, up_q_ref), (3, up_o_ref)):
        width = ref.shape[1]
        mine = scal_ref[1 + i] == scal_ref[0]
        out_ref[:, start : start + width] = jnp.where(mine, ref[...].astype(F32), 0.0).astype(BF)
        start += width


def prepare(rank, tp, owners, down_q, down_o, up_q, up_o):
    scal = jnp.concatenate([rank[None], owners, tp[None]]).astype(jnp.int32)
    width = 2 * (WIDTH + QCOLS)
    return pl.pallas_call(
        prep_kernel,
        out_shape=jax.ShapeDtypeStruct((RANK, width), BF),
        grid_spec=pltpu.PrefetchScalarGridSpec(
            num_scalar_prefetch=1,
            grid=(1,),
            in_specs=[
                pl.BlockSpec((RANK, WIDTH), lambda i, sc: (0, sc[5])),
                pl.BlockSpec((RANK, QCOLS), lambda i, sc: (0, 0)),
                pl.BlockSpec((RANK, QCOLS), lambda i, sc: (0, 0)),
                pl.BlockSpec((RANK, WIDTH), lambda i, sc: (0, sc[5])),
            ],
            out_specs=pl.BlockSpec((RANK, width), lambda i, sc: (0, 0)),
        ),
        cost_estimate=pl.CostEstimate(flops=3 * 10**10, bytes_accessed=10**8, transcendentals=0),
        compiler_params=pltpu.CompilerParams(vmem_limit_bytes=16 * 1024 * 1024),
    )(scal, down_q, down_o, up_q, up_o)


def copies(piece, axis, n):
    everywhere = jnp.broadcast_to(piece[None], (n,) + piece.shape)
    return lax.all_to_all(everywhere, axis, 0, 0)


def spread(part, axis):
    got = copies(part, axis, SIZES[axis])
    return got[0] + got[1] + got[2] + got[3]


def column_piece(weight, rank, tp):
    piece = lax.dynamic_slice(
        weight, ((rank % 4) * PIECE, (tp ^ (rank // 4)) * WIDTH), (PIECE, WIDTH)
    )
    return piece


def to_columns(piece):
    pairs = []
    for r in range(32):
        for t in range(8):
            pairs.append((r * 8 + t, r * 8 + (t ^ (r // 4))))
    return lax.ppermute(piece, AXES, pairs)


SHIFTS = [(a, d) for a in range(2) for d in range(4)]


def shards(
    tokens,
    norm_gain_vector,
    keys,
    values,
    query_frozen_weight,
    output_frozen_weight,
    query_update_first,
    query_update_second,
    output_update_first,
    output_update_second,
    owners,
    frame_block_number,
):
    zh, y, c = (lax.axis_index(a) for a in CTX)
    tp = lax.axis_index("zl") * 4 + lax.axis_index("x")
    rank = zh * 8 + y * 2 + c

    half = RANK // 2
    half_rows = ROWS // 2
    left = shift(tokens, "x", 1)
    right = shift(tokens, "x", -1)
    other = shift(tokens, "zl", 1)
    factors = prepare(
        rank,
        tp,
        owners,
        query_update_first[0].T,
        output_update_first[0].T,
        query_update_second[0],
        output_update_second[0],
    )
    factors = factors + shift(factors, "c", 1)
    part = lax.dynamic_slice_in_dim(factors, c * half, half, 0)
    seed = jnp.zeros((8, HS), F32)
    kv = jnp.concatenate([keys, values], axis=1)
    gain = jnp.pad(norm_gain_vector.reshape(WIDTH // HS, HS), ((0, 16 - WIDTH // HS), (0, 0)))
    gain = copies(gain, TP, 8)
    left, right, other, part, seed, kv, gain = together(
        left, right, other, part, seed, kv, gain
    )

    kv = lax.all_gather(kv, ("zh", "c"), axis=0, tiled=True)
    other_left = shift(other, "x", 1)
    other_right = shift(other, "x", -1)
    part = spread(part, "zh")
    seed = cover(seed)
    other_left, other_right, part, seed = together(other_left, other_right, part, seed)

    far_left = shift(jnp.concatenate([left[:half_rows], other_left[:half_rows]]), "x", 1)
    far_right = shift(jnp.concatenate([right[half_rows:], other_right[half_rows:]]), "x", -1)
    part = spread(part, "y")
    seed = cover(seed)
    far_left, far_right, part, seed = together(far_left, far_right, part, seed)
    columns = column_piece(output_frozen_weight, rank, tp)
    columns = to_columns(after(columns, far_left))

    order = jnp.stack([tp_source(a, d) for a, d in SHIFTS])
    mine = copies(part[:, : WIDTH + QCOLS], TP, 8)
    ups = part[:, WIDTH + QCOLS :]
    ups_other = shift(ups, "c", 1)
    normed = vmem_call(
        norm_kernel,
        jax.ShapeDtypeStruct((8, ROWS, WIDTH), BF),
        1,
        9,
        flops=10**10,
        nbytes=4 * 10**7,
        mib=24,
    )(order, gain, tokens, left, far_left, right, other, other_left, far_right, other_right)
    mine, normed, columns = together(mine, normed, columns)
    columns = lax.all_gather(columns, CTX, axis=0, tiled=True)
    theirs = shift(mine, "c", 1)
    queries = fetch_call(
        query_kernel,
        jax.ShapeDtypeStruct((ROWS, QCOLS), BF),
        4,
        2,
        (8, ROWS, WIDTH),
        (8, WIDTH, QCOLS),
        2 * ROWS * 8 * WIDTH * QCOLS + 2 * 8 * WIDTH * RANK * QCOLS,
    )(order, mine, theirs, ups, ups_other, normed, query_frozen_weight)

    counts = jnp.sum(
        (frame_block_number[None, :] <= frame_block_number[:, None]).astype(jnp.int32), axis=1
    )
    vis_end = counts * FTOK
    kframes = (jnp.arange(CHUNKS, dtype=jnp.int32) * 8 + y * 2) * FRAMES_DEV

    def frames_of(step):
        return (zh * 8 + ((y - step) % 4) * 2 + c) * FRAMES_DEV

    q_left = shift(queries, "y", 1)
    q_right = shift(queries, "y", -1)
    q_far = shift(queries, "y", 2)
    (own,) = attention([queries], [frames_of(0)], kframes, vis_end, kv)
    q_left = after(q_left, own)
    (left,) = attention([q_left], [frames_of(1)], kframes, vis_end, kv)
    back_left = shift(left, "y", -1)
    (right,) = attention([q_right], [frames_of(-1)], kframes, vis_end, kv)
    back_right = shift(right, "y", 1)
    (far,) = attention([q_far], [frames_of(2)], kframes, vis_end, kv)
    back_far = shift(far, "y", 2)

    attended = vmem_call(combine_kernel, jax.ShapeDtypeStruct((ROWS, QCOLS), BF), 0, 4, nbytes=10**6)(
        own, back_left, back_right, back_far
    )
    left = shift(attended, "x", 1)
    right = shift(attended, "x", -1)
    other = shift(attended, "zl", 1)
    other_left = shift(other, "x", 1)
    other_right = shift(other, "x", -1)
    far_left = shift(jnp.concatenate([left[:half_rows], other_left[:half_rows]]), "x", 1)
    far_right = shift(jnp.concatenate([right[half_rows:], other_right[half_rows:]]), "x", -1)
    slots = jnp.concatenate([order, tp ^ order])
    return fetch_call(
        project_kernel,
        jax.ShapeDtypeStruct((ROWS, WIDTH), BF),
        4,
        9,
        (8, ROWS, QCOLS),
        (8, QCOLS, WIDTH),
        2 * ROWS * 8 * WIDTH * QCOLS,
    )(
        slots,
        mine,
        theirs,
        ups,
        ups_other,
        attended,
        left,
        far_left,
        right,
        other,
        other_left,
        far_right,
        other_right,
        columns,
    )


def solution(mesh):
    fine = Mesh(mesh.devices.reshape([SIZES[a] for a in AXES]), AXES)
    in_specs = (
        P(CTX, TP),
        P(TP),
        P(CTX, TP),
        P(CTX, TP),
        P(None, TP),
        P(TP, None),
        P(CTX, None, None),
        P(CTX, None, TP),
        P(CTX, TP, None),
        P(CTX, None, None),
        P(),
        P(),
    )
    return jax.shard_map(
        shards, mesh=fine, in_specs=in_specs, out_specs=P(CTX, TP), check_vma=False
    )
```

```python
import functools
import math

import jax
import jax.numpy as jnp
from jax import lax
from jax.experimental import pallas as pl
from jax.experimental.pallas import tpu as pltpu
from jax.sharding import Mesh
from jax.sharding import PartitionSpec as P

HS = 128
FTOK = 64
ROWS = 320
FRAMES_DEV = 5
WIDTH = 768
RANK = 64
HEADS_DEV = 3
QCOLS = HEADS_DEV * HS
CHUNK = 2 * ROWS
CHUNKS = 4
NEG = -1e30
PIECE = 96
EPS = 1e-6
AXES = ("zh", "y", "c", "zl", "x")
SIZES = {"zh": 4, "y": 4, "c": 2, "zl": 2, "x": 4}
CTX = ("zh", "y", "c")
TP = ("zl", "x")
EXP_SCALE = (HS ** (-0.5)) * math.log2(math.e)
BF = jnp.bfloat16
F32 = jnp.float32


def shift(v, axis, step):
    n = SIZES[axis]
    return lax.ppermute(v, axis, [(i, (i + step) % n) for i in range(n)])


def tp_source(a, d):
    return (lax.axis_index("zl") ^ a) * 4 + (lax.axis_index("x") - d) % 4


def vmem_call(body, out_shape, n_smem, n_vmem, scratch=(), flops=0, nbytes=0, mib=16, n_any=0):
    return pl.pallas_call(
        body,
        out_shape=out_shape,
        in_specs=[pl.BlockSpec(memory_space=pltpu.SMEM)] * n_smem
        + [pl.BlockSpec(memory_space=pltpu.VMEM)] * n_vmem
        + [pl.BlockSpec(memory_space=pl.ANY)] * n_any,
        scratch_shapes=list(scratch),
        cost_estimate=pl.CostEstimate(flops=flops, bytes_accessed=nbytes, transcendentals=0),
        compiler_params=pltpu.CompilerParams(vmem_limit_bytes=mib * 1024 * 1024),
    )


def tdot(a, b):
    return lax.dot_general(a, b, (((0,), (0,)), ((), ())), preferred_element_type=F32)


def norm_kernel(order_ref, gain_ref, *refs):
    parts, out_ref = refs[:8], refs[8]
    half = ROWS // 2

    def block(i):
        if i in (2, 6):
            rows = slice(0, half) if i == 2 else slice(half, ROWS)
            return jnp.concatenate([parts[2][rows, :], parts[6][rows, :]], axis=0)
        return parts[i][...]

    total = jnp.zeros((ROWS, HS), F32)
    for i in range(8):
        v = block(i).astype(F32)
        v = v * v
        for g in range(WIDTH // HS):
            total = total + v[:, g * HS : (g + 1) * HS]
    total = jnp.sum(total, axis=1, keepdims=True)
    inv = lax.rsqrt(total * (1.0 / (8 * WIDTH)) + EPS)
    for i in range(8):
        at = order_ref[i]
        gain = jnp.concatenate(
            [gain_ref[at, r : r + 1, :].astype(F32) for r in range(WIDTH // HS)], axis=1
        )
        out_ref[i] = (block(i).astype(F32) * inv * gain).astype(BF)


def query_kernel(
    order_ref, mine_ref, other_ref, up_ref, up_other_ref, x_ref, w_ref, out_ref, xs, ws, x_sems, w_sems
):
    copies_in = []
    for i in range(8):
        rows = pl.ds(pl.multiple_of(order_ref[i] * WIDTH, WIDTH), WIDTH)
        copies_in.append(
            (
                pltpu.make_async_copy(w_ref.at[rows, :], ws.at[i], w_sems.at[i]),
                pltpu.make_async_copy(x_ref.at[i], xs.at[i], x_sems.at[i]),
            )
        )
        for copy in copies_in[i]:
            copy.start()
    acc = jnp.zeros((ROWS, QCOLS), F32)
    up = jnp.concatenate([up_ref[:, :QCOLS], up_other_ref[:, :QCOLS]], axis=0)
    for i in range(8):
        at = order_ref[i]
        down = jnp.concatenate([mine_ref[at, :, :WIDTH], other_ref[at, :, :WIDTH]], axis=0)
        copies_in[i][0].wait()
        merged = (ws[i].astype(F32) + tdot(down, up)).astype(BF)
        copies_in[i][1].wait()
        acc = acc + jnp.dot(xs[i], merged, preferred_element_type=F32)
    out_ref[...] = acc.astype(BF)


def attention_kernel(n, qframe_ref, kframe_ref, vis_ref, *refs):
    q_refs = refs[:n]
    kv_ref = refs[n]
    o_refs = refs[n + 1 :]
    lane = lax.broadcasted_iota(jnp.int32, (ROWS, HS), 1)
    row = lax.broadcasted_iota(jnp.int32, (ROWS, HS), 0)

    def heads(b, first, chunks):
        width = chunks * CHUNK
        last = kframe_ref[chunks - 1] * FTOK
        limit = jnp.full((ROWS, HS), vis_ref[first] - last, jnp.int32)
        for f in range(1, FRAMES_DEV):
            limit = jnp.where(row >= f * FTOK, vis_ref[first + f] - last, limit)
        seen = jnp.concatenate([lane + g * HS for g in range(CHUNK // HS)], axis=1)
        seen = seen < jnp.concatenate([limit] * (CHUNK // HS), axis=1)

        def scores(h):
            cols = slice(h * HS, (h + 1) * HS)
            return lax.dot_general(
                q_refs[b][:, cols],
                kv_ref[:width, cols],
                (((1,), (1,)), ((), ())),
                preferred_element_type=F32,
            )

        s = scores(0)
        stats = jnp.zeros((ROWS, HS), F32)
        for h in range(HEADS_DEV):
            ahead = scores(h + 1) if h + 1 < HEADS_DEV else None
            tail = jnp.where(seen, s[:, width - CHUNK :], NEG)
            s = jnp.concatenate([s[:, : width - CHUNK], tail], axis=1) if chunks > 1 else tail
            top = jnp.broadcast_to(jnp.max(s, axis=1, keepdims=True), (ROWS, HS))
            p = jnp.exp2((s - jnp.concatenate([top] * (width // HS), axis=1)) * EXP_SCALE)
            lanes = p[:, :HS]
            for g in range(1, width // HS):
                lanes = lanes + p[:, g * HS : (g + 1) * HS]
            total = jnp.broadcast_to(jnp.sum(lanes, axis=1, keepdims=True), (ROWS, HS))
            acc = jnp.dot(
                p.astype(BF),
                kv_ref[:width, QCOLS + h * HS : QCOLS + (h + 1) * HS],
                preferred_element_type=F32,
            )
            has = top > 0.5 * NEG
            o_refs[b][:, h * HS : (h + 1) * HS] = jnp.where(has, acc / total, 0.0).astype(BF)
            level = jnp.where(has, top * EXP_SCALE + jnp.log2(total), NEG)
            high = level.astype(BF).astype(F32)
            mid = (level - high).astype(BF).astype(F32)
            low = level - high - mid
            stats = jnp.where(lane == 3 * h, high, stats)
            stats = jnp.where(lane == 3 * h + 1, mid, stats)
            stats = jnp.where(lane == 3 * h + 2, low, stats)
            s = ahead
        o_refs[b][:, QCOLS:] = stats.astype(BF)

    for b in range(n):
        first = qframe_ref[b]
        end = vis_ref[first + FRAMES_DEV - 1]
        some = jnp.int32(0)
        for j in range(CHUNKS):
            some = some + (kframe_ref[j] * FTOK < end).astype(jnp.int32)

        @pl.when(some == 0)
        def _(b=b):
            o_refs[b][:, :QCOLS] = jnp.zeros((ROWS, QCOLS), BF)
            blank = jnp.where((lane < 3 * HEADS_DEV) & (lane % 3 == 0), NEG, 0.0)
            o_refs[b][:, QCOLS:] = blank.astype(BF)

        for chunks in range(1, CHUNKS + 1):

            @pl.when(some == chunks)
            def _(b=b, first=first, chunks=chunks):
                heads(b, first, chunks)


def attention(queries, qframes, kframes, vis_end, kv):
    n = len(queries)
    return vmem_call(
        functools.partial(attention_kernel, n),
        [jax.ShapeDtypeStruct((ROWS, QCOLS + HS), BF)] * n,
        3,
        n + 1,
        flops=n * 8 * ROWS * QCOLS * CHUNK * CHUNKS,
        nbytes=CHUNKS * CHUNK * 2 * QCOLS * 2,
        mib=24,
    )(jnp.stack(qframes), kframes, vis_end, *queries, kv)


def combine_kernel(*refs):
    parts, out_ref = refs[:4], refs[4]
    stats = [p[:, QCOLS:].astype(F32) for p in parts]
    for h in range(HEADS_DEV):
        levels = []
        for s in stats:
            levels.append(
                s[:, 3 * h : 3 * h + 1] + s[:, 3 * h + 1 : 3 * h + 2] + s[:, 3 * h + 2 : 3 * h + 3]
            )
        top = functools.reduce(jnp.maximum, levels)
        shares = [jnp.exp2(v - top) for v in levels]
        total = shares[0] + shares[1] + shares[2] + shares[3]
        cols = slice(h * HS, (h + 1) * HS)
        acc = jnp.zeros((ROWS, HS), F32)
        for p, w in zip(parts, shares):
            acc = acc + p[:, cols].astype(F32) * w
        out_ref[:, cols] = (acc / total).astype(BF)


def project_kernel(order_ref, *refs):
    mine_ref, other_ref, up_ref, up_other_ref = refs[:4]
    parts, w_ref, out_ref, xs, ws, x_sems, w_sems = refs[4:12], *refs[12:]
    half = ROWS // 2
    waits = []
    for i in range(8):
        rows = pl.ds(pl.multiple_of(order_ref[8 + i] * QCOLS, QCOLS), QCOLS)
        mine = [pltpu.make_async_copy(w_ref.at[rows, :], ws.at[i], w_sems.at[i])]
        if i in (2, 6):
            src = slice(0, half) if i == 2 else slice(half, ROWS)
            for k, side in enumerate((2, 6)):
                dst = xs.at[i, k * half : (k + 1) * half, :]
                mine.append(
                    pltpu.make_async_copy(parts[side].at[src, :], dst, x_sems.at[i + 8 * k])
                )
        else:
            mine.append(pltpu.make_async_copy(parts[i], xs.at[i], x_sems.at[i]))
        for copy in mine:
            copy.start()
        waits.append(mine)
    acc = jnp.zeros((ROWS, WIDTH), F32)
    up = jnp.concatenate([up_ref[:, QCOLS:], up_other_ref[:, QCOLS:]], axis=0)
    cols = slice(WIDTH, WIDTH + QCOLS)
    for i in range(8):
        at = order_ref[i]
        down = jnp.concatenate([mine_ref[at, :, cols], other_ref[at, :, cols]], axis=0)
        for copy in waits[i]:
            copy.wait()
        merged = (ws[i].astype(F32) + tdot(down, up)).astype(BF)
        acc = acc + jnp.dot(xs[i], merged, preferred_element_type=F32)
    out_ref[...] = acc.astype(BF)


def fetch_call(body, out_shape, n_vmem, n_any, x_shape, w_shape, flops):
    return pl.pallas_call(
        body,
        out_shape=out_shape,
        in_specs=[pl.BlockSpec(memory_space=pltpu.SMEM)]
        + [pl.BlockSpec(memory_space=pltpu.VMEM)] * n_vmem
        + [pl.BlockSpec(memory_space=pl.ANY)] * n_any,
        out_specs=pl.BlockSpec(memory_space=pltpu.VMEM),
        scratch_shapes=[
            pltpu.VMEM(x_shape, BF),
            pltpu.VMEM(w_shape, BF),
            pltpu.SemaphoreType.DMA((16,)),
            pltpu.SemaphoreType.DMA((8,)),
        ],
        cost_estimate=pl.CostEstimate(flops=flops, bytes_accessed=10**7, transcendentals=0),
        compiler_params=pltpu.CompilerParams(vmem_limit_bytes=60 * 1024 * 1024),
    )


def cover_kernel(in_ref, out_ref):
    out_ref[...] = in_ref[...]


def cover(seed):
    return pl.pallas_call(
        cover_kernel,
        out_shape=jax.ShapeDtypeStruct(seed.shape, seed.dtype),
        cost_estimate=pl.CostEstimate(flops=3 * 10**10, bytes_accessed=10**8, transcendentals=0),
    )(seed)


def together(*values):
    return lax.optimization_barrier(values)


def after(value, *others):
    return lax.optimization_barrier((value,) + others)[0]


def prep_kernel(scal_ref, down_q_ref, down_o_ref, up_q_ref, up_o_ref, out_ref):
    start = 0
    for i, ref in ((0, down_q_ref), (2, down_o_ref), (1, up_q_ref), (3, up_o_ref)):
        width = ref.shape[1]
        mine = scal_ref[1 + i] == scal_ref[0]
        out_ref[:, start : start + width] = jnp.where(mine, ref[...].astype(F32), 0.0).astype(BF)
        start += width


def prepare(rank, tp, owners, down_q, down_o, up_q, up_o):
    scal = jnp.concatenate([rank[None], owners, tp[None]]).astype(jnp.int32)
    width = 2 * (WIDTH + QCOLS)
    return pl.pallas_call(
        prep_kernel,
        out_shape=jax.ShapeDtypeStruct((RANK, width), BF),
        grid_spec=pltpu.PrefetchScalarGridSpec(
            num_scalar_prefetch=1,
            grid=(1,),
            in_specs=[
                pl.BlockSpec((RANK, WIDTH), lambda i, sc: (0, sc[5])),
                pl.BlockSpec((RANK, QCOLS), lambda i, sc: (0, 0)),
                pl.BlockSpec((RANK, QCOLS), lambda i, sc: (0, 0)),
                pl.BlockSpec((RANK, WIDTH), lambda i, sc: (0, sc[5])),
            ],
            out_specs=pl.BlockSpec((RANK, width), lambda i, sc: (0, 0)),
        ),
        cost_estimate=pl.CostEstimate(flops=3 * 10**10, bytes_accessed=10**8, transcendentals=0),
        compiler_params=pltpu.CompilerParams(vmem_limit_bytes=60 * 1024 * 1024),
    )(scal, down_q, down_o, up_q, up_o)


def copies(piece, axis, n):
    everywhere = jnp.broadcast_to(piece[None], (n,) + piece.shape)
    return lax.all_to_all(everywhere, axis, 0, 0)


def spread(part, axis):
    got = copies(part, axis, SIZES[axis])
    return got[0] + got[1] + got[2] + got[3]


def column_piece(weight, rank, tp):
    piece = lax.dynamic_slice(
        weight, ((rank % 4) * PIECE, (tp ^ (rank // 4)) * WIDTH), (PIECE, WIDTH)
    )
    return piece


def to_columns(piece):
    pairs = []
    for r in range(32):
        for t in range(8):
            pairs.append((r * 8 + t, r * 8 + (t ^ (r // 4))))
    return lax.ppermute(piece, AXES, pairs)


SHIFTS = [(a, d) for a in range(2) for d in range(4)]


def shards(
    tokens,
    norm_gain_vector,
    keys,
    values,
    query_frozen_weight,
    output_frozen_weight,
    query_update_first,
    query_update_second,
    output_update_first,
    output_update_second,
    owners,
    frame_block_number,
):
    zh, y, c = (lax.axis_index(a) for a in CTX)
    tp = lax.axis_index("zl") * 4 + lax.axis_index("x")
    rank = zh * 8 + y * 2 + c

    half = RANK // 2
    half_rows = ROWS // 2
    left = shift(tokens, "x", 1)
    right = shift(tokens, "x", -1)
    other = shift(tokens, "zl", 1)
    factors = prepare(
        rank,
        tp,
        owners,
        query_update_first[0].T,
        output_update_first[0].T,
        query_update_second[0],
        output_update_second[0],
    )
    factors = factors + shift(factors, "c", 1)
    part = lax.dynamic_slice_in_dim(factors, c * half, half, 0)
    seed = jnp.zeros((8, HS), F32)
    kv = jnp.concatenate([keys, values], axis=1)
    gain = jnp.pad(norm_gain_vector.reshape(WIDTH // HS, HS), ((0, 16 - WIDTH // HS), (0, 0)))
    gain = copies(gain, TP, 8)
    left, right, other, part, seed, kv, gain = together(
        left, right, other, part, seed, kv, gain
    )

    kv = lax.all_gather(kv, ("zh", "c"), axis=0, tiled=True)
    other_left = shift(other, "x", 1)
    other_right = shift(other, "x", -1)
    part = spread(part, "zh")
    seed = cover(seed)
    other_left, other_right, part, seed = together(other_left, other_right, part, seed)

    far_left = shift(jnp.concatenate([left[:half_rows], other_left[:half_rows]]), "x", 1)
    far_right = shift(jnp.concatenate([right[half_rows:], other_right[half_rows:]]), "x", -1)
    part = spread(part, "y")
    seed = cover(seed)
    far_left, far_right, part, seed = together(far_left, far_right, part, seed)
    columns = column_piece(output_frozen_weight, rank, tp)
    columns = to_columns(after(columns, far_left))

    order = jnp.stack([tp_source(a, d) for a, d in SHIFTS])
    mine = copies(part[:, : WIDTH + QCOLS], TP, 8)
    ups = part[:, WIDTH + QCOLS :]
    ups_other = shift(ups, "c", 1)
    normed = vmem_call(
        norm_kernel,
        jax.ShapeDtypeStruct((8, ROWS, WIDTH), BF),
        1,
        9,
        flops=10**10,
        nbytes=4 * 10**7,
        mib=24,
    )(order, gain, tokens, left, far_left, right, other, other_left, far_right, other_right)
    mine, normed, columns = together(mine, normed, columns)
    columns = lax.all_gather(columns, CTX, axis=0, tiled=True)
    theirs = shift(mine, "c", 1)
    queries = fetch_call(
        query_kernel,
        jax.ShapeDtypeStruct((ROWS, QCOLS), BF),
        4,
        2,
        (8, ROWS, WIDTH),
        (8, WIDTH, QCOLS),
        2 * ROWS * 8 * WIDTH * QCOLS + 2 * 8 * WIDTH * RANK * QCOLS,
    )(order, mine, theirs, ups, ups_other, normed, query_frozen_weight)

    counts = jnp.sum(
        (frame_block_number[None, :] <= frame_block_number[:, None]).astype(jnp.int32), axis=1
    )
    vis_end = counts * FTOK
    kframes = (jnp.arange(CHUNKS, dtype=jnp.int32) * 8 + y * 2) * FRAMES_DEV

    def frames_of(step):
        return (zh * 8 + ((y - step) % 4) * 2 + c) * FRAMES_DEV

    q_left = shift(queries, "y", 1)
    q_right = shift(queries, "y", -1)
    q_far = shift(queries, "y", 2)
    (own,) = attention([queries], [frames_of(0)], kframes, vis_end, kv)
    q_left, q_right, q_far, own = together(q_left, q_right, q_far, own)
    (left,) = attention([q_left], [frames_of(1)], kframes, vis_end, kv)
    back_left = shift(left, "y", -1)
    (right,) = attention([q_right], [frames_of(-1)], kframes, vis_end, kv)
    back_right = shift(right, "y", 1)
    (far,) = attention([q_far], [frames_of(2)], kframes, vis_end, kv)
    back_far = shift(far, "y", 2)

    attended = vmem_call(combine_kernel, jax.ShapeDtypeStruct((ROWS, QCOLS), BF), 0, 4, nbytes=10**6)(
        own, back_left, back_right, back_far
    )
    left = shift(attended, "x", 1)
    right = shift(attended, "x", -1)
    other = shift(attended, "zl", 1)
    other_left = shift(other, "x", 1)
    other_right = shift(other, "x", -1)
    far_left = shift(jnp.concatenate([left[:half_rows], other_left[:half_rows]]), "x", 1)
    far_right = shift(jnp.concatenate([right[half_rows:], other_right[half_rows:]]), "x", -1)
    slots = jnp.concatenate([order, tp ^ order])
    return fetch_call(
        project_kernel,
        jax.ShapeDtypeStruct((ROWS, WIDTH), BF),
        4,
        9,
        (8, ROWS, QCOLS),
        (8, QCOLS, WIDTH),
        2 * ROWS * 8 * WIDTH * QCOLS,
    )(
        slots,
        mine,
        theirs,
        ups,
        ups_other,
        attended,
        left,
        far_left,
        right,
        other,
        other_left,
        far_right,
        other_right,
        columns,
    )


def solution(mesh):
    fine = Mesh(mesh.devices.reshape([SIZES[a] for a in AXES]), AXES)
    in_specs = (
        P(CTX, TP),
        P(TP),
        P(CTX, TP),
        P(CTX, TP),
        P(None, TP),
        P(TP, None),
        P(CTX, None, None),
        P(CTX, None, TP),
        P(CTX, TP, None),
        P(CTX, None, None),
        P(),
        P(),
    )
    return jax.shard_map(
        shards, mesh=fine, in_specs=in_specs, out_specs=P(CTX, TP), check_vma=False
    )
```

```python
import functools
import math

import jax
import jax.numpy as jnp
from jax import lax
from jax.experimental import pallas as pl
from jax.experimental.pallas import tpu as pltpu
from jax.sharding import Mesh
from jax.sharding import PartitionSpec as P

HS = 128
FTOK = 64
ROWS = 320
FRAMES_DEV = 5
WIDTH = 768
RANK = 64
HEADS_DEV = 3
QCOLS = HEADS_DEV * HS
CHUNK = 2 * ROWS
CHUNKS = 4
NEG = -1e30
PIECE = 96
EPS = 1e-6
AXES = ("zh", "y", "c", "zl", "x")
SIZES = {"zh": 4, "y": 4, "c": 2, "zl": 2, "x": 4}
CTX = ("zh", "y", "c")
TP = ("zl", "x")
EXP_SCALE = (HS ** (-0.5)) * math.log2(math.e)
BF = jnp.bfloat16
F32 = jnp.float32


def shift(v, axis, step):
    n = SIZES[axis]
    return lax.ppermute(v, axis, [(i, (i + step) % n) for i in range(n)])


def tp_source(a, d):
    return (lax.axis_index("zl") ^ a) * 4 + (lax.axis_index("x") - d) % 4


def vmem_call(body, out_shape, n_smem, n_vmem, scratch=(), flops=0, nbytes=0, mib=16, n_any=0):
    return pl.pallas_call(
        body,
        out_shape=out_shape,
        in_specs=[pl.BlockSpec(memory_space=pltpu.SMEM)] * n_smem
        + [pl.BlockSpec(memory_space=pltpu.VMEM)] * n_vmem
        + [pl.BlockSpec(memory_space=pl.ANY)] * n_any,
        scratch_shapes=list(scratch),
        cost_estimate=pl.CostEstimate(flops=flops, bytes_accessed=nbytes, transcendentals=0),
        compiler_params=pltpu.CompilerParams(vmem_limit_bytes=mib * 1024 * 1024),
    )


def tdot(a, b):
    return lax.dot_general(a, b, (((0,), (0,)), ((), ())), preferred_element_type=F32)


def norm_kernel(order_ref, gain_ref, *refs):
    parts, out_ref = refs[:8], refs[8]
    half = ROWS // 2

    def block(i):
        if i in (2, 6):
            rows = slice(0, half) if i == 2 else slice(half, ROWS)
            return jnp.concatenate([parts[2][rows, :], parts[6][rows, :]], axis=0)
        return parts[i][...]

    total = jnp.zeros((ROWS, HS), F32)
    for i in range(8):
        v = block(i).astype(F32)
        v = v * v
        for g in range(WIDTH // HS):
            total = total + v[:, g * HS : (g + 1) * HS]
    total = jnp.sum(total, axis=1, keepdims=True)
    inv = lax.rsqrt(total * (1.0 / (8 * WIDTH)) + EPS)
    for i in range(8):
        at = order_ref[i]
        gain = jnp.concatenate(
            [gain_ref[at, r : r + 1, :].astype(F32) for r in range(WIDTH // HS)], axis=1
        )
        out_ref[i] = (block(i).astype(F32) * inv * gain).astype(BF)


def query_kernel(
    order_ref, mine_ref, other_ref, up_ref, up_other_ref, x_ref, w_ref, out_ref, xs, ws, x_sems, w_sems
):
    copies_in = []
    for i in range(8):
        rows = pl.ds(pl.multiple_of(order_ref[i] * WIDTH, WIDTH), WIDTH)
        copies_in.append(
            (
                pltpu.make_async_copy(w_ref.at[rows, :], ws.at[i], w_sems.at[i]),
                pltpu.make_async_copy(x_ref.at[i], xs.at[i], x_sems.at[i]),
            )
        )
        for copy in copies_in[i]:
            copy.start()
    acc = jnp.zeros((ROWS, QCOLS), F32)
    up = jnp.concatenate([up_ref[:, :QCOLS], up_other_ref[:, :QCOLS]], axis=0)
    for i in range(8):
        at = order_ref[i]
        down = jnp.concatenate([mine_ref[at, :, :WIDTH], other_ref[at, :, :WIDTH]], axis=0)
        copies_in[i][0].wait()
        merged = (ws[i].astype(F32) + tdot(down, up)).astype(BF)
        copies_in[i][1].wait()
        acc = acc + jnp.dot(xs[i], merged, preferred_element_type=F32)
    out_ref[...] = acc.astype(BF)


def attention_kernel(n, qframe_ref, kframe_ref, vis_ref, *refs):
    q_refs = refs[:n]
    kv_ref = refs[n]
    o_refs = refs[n + 1 :]
    lane = lax.broadcasted_iota(jnp.int32, (ROWS, HS), 1)
    row = lax.broadcasted_iota(jnp.int32, (ROWS, HS), 0)

    def heads(b, first, chunks):
        width = chunks * CHUNK
        last = kframe_ref[chunks - 1] * FTOK
        limit = jnp.full((ROWS, HS), vis_ref[first] - last, jnp.int32)
        for f in range(1, FRAMES_DEV):
            limit = jnp.where(row >= f * FTOK, vis_ref[first + f] - last, limit)
        seen = jnp.concatenate([lane + g * HS for g in range(CHUNK // HS)], axis=1)
        seen = seen < jnp.concatenate([limit] * (CHUNK // HS), axis=1)

        def scores(h):
            cols = slice(h * HS, (h + 1) * HS)
            return lax.dot_general(
                q_refs[b][:, cols],
                kv_ref[:width, cols],
                (((1,), (1,)), ((), ())),
                preferred_element_type=F32,
            )

        s = scores(0)
        stats = jnp.zeros((ROWS, HS), F32)
        for h in range(HEADS_DEV):
            ahead = scores(h + 1) if h + 1 < HEADS_DEV else None
            tail = jnp.where(seen, s[:, width - CHUNK :], NEG)
            s = jnp.concatenate([s[:, : width - CHUNK], tail], axis=1) if chunks > 1 else tail
            top = jnp.broadcast_to(jnp.max(s, axis=1, keepdims=True), (ROWS, HS))
            p = jnp.exp2((s - jnp.concatenate([top] * (width // HS), axis=1)) * EXP_SCALE)
            lanes = p[:, :HS]
            for g in range(1, width // HS):
                lanes = lanes + p[:, g * HS : (g + 1) * HS]
            total = jnp.broadcast_to(jnp.sum(lanes, axis=1, keepdims=True), (ROWS, HS))
            acc = jnp.dot(
                p.astype(BF),
                kv_ref[:width, QCOLS + h * HS : QCOLS + (h + 1) * HS],
                preferred_element_type=F32,
            )
            has = top > 0.5 * NEG
            o_refs[b][:, h * HS : (h + 1) * HS] = jnp.where(has, acc / total, 0.0).astype(BF)
            level = jnp.where(has, top * EXP_SCALE + jnp.log2(total), NEG)
            high = level.astype(BF).astype(F32)
            mid = (level - high).astype(BF).astype(F32)
            low = level - high - mid
            stats = jnp.where(lane == 3 * h, high, stats)
            stats = jnp.where(lane == 3 * h + 1, mid, stats)
            stats = jnp.where(lane == 3 * h + 2, low, stats)
            s = ahead
        o_refs[b][:, QCOLS:] = stats.astype(BF)

    for b in range(n):
        first = qframe_ref[b]
        end = vis_ref[first + FRAMES_DEV - 1]
        some = jnp.int32(0)
        for j in range(CHUNKS):
            some = some + (kframe_ref[j] * FTOK < end).astype(jnp.int32)

        @pl.when(some == 0)
        def _(b=b):
            o_refs[b][:, :QCOLS] = jnp.zeros((ROWS, QCOLS), BF)
            blank = jnp.where((lane < 3 * HEADS_DEV) & (lane % 3 == 0), NEG, 0.0)
            o_refs[b][:, QCOLS:] = blank.astype(BF)

        for chunks in range(1, CHUNKS + 1):

            @pl.when(some == chunks)
            def _(b=b, first=first, chunks=chunks):
                heads(b, first, chunks)


def attention(queries, qframes, kframes, vis_end, kv):
    n = len(queries)
    return vmem_call(
        functools.partial(attention_kernel, n),
        [jax.ShapeDtypeStruct((ROWS, QCOLS + HS), BF)] * n,
        3,
        n + 1,
        flops=n * 8 * ROWS * QCOLS * CHUNK * CHUNKS,
        nbytes=CHUNKS * CHUNK * 2 * QCOLS * 2,
        mib=24,
    )(jnp.stack(qframes), kframes, vis_end, *queries, kv)


def combine_kernel(*refs):
    parts, out_ref = refs[:4], refs[4]
    stats = [p[:, QCOLS:].astype(F32) for p in parts]
    for h in range(HEADS_DEV):
        levels = []
        for s in stats:
            levels.append(
                s[:, 3 * h : 3 * h + 1] + s[:, 3 * h + 1 : 3 * h + 2] + s[:, 3 * h + 2 : 3 * h + 3]
            )
        top = functools.reduce(jnp.maximum, levels)
        shares = [jnp.exp2(v - top) for v in levels]
        total = shares[0] + shares[1] + shares[2] + shares[3]
        cols = slice(h * HS, (h + 1) * HS)
        acc = jnp.zeros((ROWS, HS), F32)
        for p, w in zip(parts, shares):
            acc = acc + p[:, cols].astype(F32) * w
        out_ref[:, cols] = (acc / total).astype(BF)


def project_kernel(order_ref, *refs):
    mine_ref, other_ref, up_ref, up_other_ref = refs[:4]
    parts, w_ref, out_ref, xs, ws, x_sems, w_sems = refs[4:12], *refs[12:]
    half = ROWS // 2
    waits = []
    for i in range(8):
        rows = pl.ds(pl.multiple_of(order_ref[8 + i] * QCOLS, QCOLS), QCOLS)
        mine = [pltpu.make_async_copy(w_ref.at[rows, :], ws.at[i], w_sems.at[i])]
        if i in (2, 6):
            src = slice(0, half) if i == 2 else slice(half, ROWS)
            for k, side in enumerate((2, 6)):
                dst = xs.at[i, k * half : (k + 1) * half, :]
                mine.append(
                    pltpu.make_async_copy(parts[side].at[src, :], dst, x_sems.at[i + 8 * k])
                )
        else:
            mine.append(pltpu.make_async_copy(parts[i], xs.at[i], x_sems.at[i]))
        for copy in mine:
            copy.start()
        waits.append(mine)
    acc = jnp.zeros((ROWS, WIDTH), F32)
    up = jnp.concatenate([up_ref[:, QCOLS:], up_other_ref[:, QCOLS:]], axis=0)
    cols = slice(WIDTH, WIDTH + QCOLS)
    for i in range(8):
        at = order_ref[i]
        down = jnp.concatenate([mine_ref[at, :, cols], other_ref[at, :, cols]], axis=0)
        for copy in waits[i]:
            copy.wait()
        merged = (ws[i].astype(F32) + tdot(down, up)).astype(BF)
        acc = acc + jnp.dot(xs[i], merged, preferred_element_type=F32)
    out_ref[...] = acc.astype(BF)


def fetch_call(body, out_shape, n_vmem, n_any, x_shape, w_shape, flops):
    return pl.pallas_call(
        body,
        out_shape=out_shape,
        in_specs=[pl.BlockSpec(memory_space=pltpu.SMEM)]
        + [pl.BlockSpec(memory_space=pltpu.VMEM)] * n_vmem
        + [pl.BlockSpec(memory_space=pl.ANY)] * n_any,
        out_specs=pl.BlockSpec(memory_space=pltpu.VMEM),
        scratch_shapes=[
            pltpu.VMEM(x_shape, BF),
            pltpu.VMEM(w_shape, BF),
            pltpu.SemaphoreType.DMA((16,)),
            pltpu.SemaphoreType.DMA((8,)),
        ],
        cost_estimate=pl.CostEstimate(flops=flops, bytes_accessed=10**7, transcendentals=0),
        compiler_params=pltpu.CompilerParams(vmem_limit_bytes=60 * 1024 * 1024),
    )


def cover_kernel(in_ref, out_ref):
    out_ref[...] = in_ref[...]


def cover(seed):
    return pl.pallas_call(
        cover_kernel,
        out_shape=jax.ShapeDtypeStruct(seed.shape, seed.dtype),
        cost_estimate=pl.CostEstimate(flops=3 * 10**10, bytes_accessed=10**8, transcendentals=0),
    )(seed)


def together(*values):
    return lax.optimization_barrier(values)


def after(value, *others):
    return lax.optimization_barrier((value,) + others)[0]


def prep_kernel(scal_ref, down_q_ref, down_o_ref, up_q_ref, up_o_ref, out_ref):
    start = 0
    for i, ref in ((0, down_q_ref), (2, down_o_ref), (1, up_q_ref), (3, up_o_ref)):
        width = ref.shape[1]
        mine = scal_ref[1 + i] == scal_ref[0]
        out_ref[:, start : start + width] = jnp.where(mine, ref[...].astype(F32), 0.0).astype(BF)
        start += width


def prepare(rank, tp, owners, down_q, down_o, up_q, up_o):
    scal = jnp.concatenate([rank[None], owners, tp[None]]).astype(jnp.int32)
    width = 2 * (WIDTH + QCOLS)
    return pl.pallas_call(
        prep_kernel,
        out_shape=jax.ShapeDtypeStruct((RANK, width), BF),
        grid_spec=pltpu.PrefetchScalarGridSpec(
            num_scalar_prefetch=1,
            grid=(1,),
            in_specs=[
                pl.BlockSpec((RANK, WIDTH), lambda i, sc: (0, sc[5])),
                pl.BlockSpec((RANK, QCOLS), lambda i, sc: (0, 0)),
                pl.BlockSpec((RANK, QCOLS), lambda i, sc: (0, 0)),
                pl.BlockSpec((RANK, WIDTH), lambda i, sc: (0, sc[5])),
            ],
            out_specs=pl.BlockSpec((RANK, width), lambda i, sc: (0, 0)),
        ),
        cost_estimate=pl.CostEstimate(flops=3 * 10**10, bytes_accessed=10**8, transcendentals=0),
        compiler_params=pltpu.CompilerParams(vmem_limit_bytes=60 * 1024 * 1024),
    )(scal, down_q, down_o, up_q, up_o)


def copies(piece, axis, n):
    everywhere = jnp.broadcast_to(piece[None], (n,) + piece.shape)
    return lax.all_to_all(everywhere, axis, 0, 0)


def spread(part, axis):
    got = copies(part, axis, SIZES[axis])
    return got[0] + got[1] + got[2] + got[3]


def column_piece(weight, rank, tp):
    piece = lax.dynamic_slice(
        weight, ((rank % 4) * PIECE, (tp ^ (rank // 4)) * WIDTH), (PIECE, WIDTH)
    )
    return piece


def to_columns(piece):
    pairs = []
    for r in range(32):
        for t in range(8):
            pairs.append((r * 8 + t, r * 8 + (t ^ (r // 4))))
    return lax.ppermute(piece, AXES, pairs)


SHIFTS = [(a, d) for a in range(2) for d in range(4)]


def shards(
    tokens,
    norm_gain_vector,
    keys,
    values,
    query_frozen_weight,
    output_frozen_weight,
    query_update_first,
    query_update_second,
    output_update_first,
    output_update_second,
    owners,
    frame_block_number,
):
    zh, y, c = (lax.axis_index(a) for a in CTX)
    tp = lax.axis_index("zl") * 4 + lax.axis_index("x")
    rank = zh * 8 + y * 2 + c

    half = RANK // 2
    half_rows = ROWS // 2
    left = shift(tokens, "x", 1)
    right = shift(tokens, "x", -1)
    other = shift(tokens, "zl", 1)
    factors = prepare(
        rank,
        tp,
        owners,
        query_update_first[0].T,
        output_update_first[0].T,
        query_update_second[0],
        output_update_second[0],
    )
    factors = factors + shift(factors, "c", 1)
    part = lax.dynamic_slice_in_dim(factors, c * half, half, 0)
    seed = jnp.zeros((8, HS), F32)
    kv = jnp.concatenate([keys, values], axis=1)
    gain = jnp.pad(norm_gain_vector.reshape(WIDTH // HS, HS), ((0, 16 - WIDTH // HS), (0, 0)))
    gain = copies(gain, TP, 8)
    left, right, other, part, seed, kv = together(left, right, other, part, seed, kv)

    kv = lax.all_gather(kv, ("zh", "c"), axis=0, tiled=True)
    other_left = shift(other, "x", 1)
    other_right = shift(other, "x", -1)
    part = spread(part, "zh")
    columns = column_piece(output_frozen_weight, rank, tp)
    seed = cover(seed)
    other_left, other_right, part, seed, columns, gain = together(
        other_left, other_right, part, seed, columns, gain
    )

    far_left = shift(jnp.concatenate([left[:half_rows], other_left[:half_rows]]), "x", 1)
    far_right = shift(jnp.concatenate([right[half_rows:], other_right[half_rows:]]), "x", -1)
    part = spread(part, "y")
    seed = cover(seed)
    far_left, far_right, part, seed, columns = together(
        far_left, far_right, part, seed, columns
    )
    columns = to_columns(columns)

    order = jnp.stack([tp_source(a, d) for a, d in SHIFTS])
    mine = copies(part[:, : WIDTH + QCOLS], TP, 8)
    ups = part[:, WIDTH + QCOLS :]
    ups_other = shift(ups, "c", 1)
    normed = vmem_call(
        norm_kernel,
        jax.ShapeDtypeStruct((8, ROWS, WIDTH), BF),
        1,
        9,
        flops=10**10,
        nbytes=4 * 10**7,
        mib=24,
    )(order, gain, tokens, left, far_left, right, other, other_left, far_right, other_right)
    mine, normed, columns = together(mine, normed, columns)
    columns = lax.all_gather(columns, CTX, axis=0, tiled=True)
    theirs = shift(mine, "c", 1)
    queries = fetch_call(
        query_kernel,
        jax.ShapeDtypeStruct((ROWS, QCOLS), BF),
        4,
        2,
        (8, ROWS, WIDTH),
        (8, WIDTH, QCOLS),
        2 * ROWS * 8 * WIDTH * QCOLS + 2 * 8 * WIDTH * RANK * QCOLS,
    )(order, mine, theirs, ups, ups_other, normed, query_frozen_weight)

    counts = jnp.sum(
        (frame_block_number[None, :] <= frame_block_number[:, None]).astype(jnp.int32), axis=1
    )
    vis_end = counts * FTOK
    kframes = (jnp.arange(CHUNKS, dtype=jnp.int32) * 8 + y * 2) * FRAMES_DEV

    def frames_of(step):
        return (zh * 8 + ((y - step) % 4) * 2 + c) * FRAMES_DEV

    q_left = shift(queries, "y", 1)
    q_right = shift(queries, "y", -1)
    q_far = shift(queries, "y", 2)
    (own,) = attention([queries], [frames_of(0)], kframes, vis_end, kv)
    q_left, q_right, q_far, own = together(q_left, q_right, q_far, own)
    (left,) = attention([q_left], [frames_of(1)], kframes, vis_end, kv)
    back_left = shift(left, "y", -1)
    (right,) = attention([q_right], [frames_of(-1)], kframes, vis_end, kv)
    back_right = shift(right, "y", 1)
    (far,) = attention([q_far], [frames_of(2)], kframes, vis_end, kv)
    back_far = shift(far, "y", 2)

    attended = vmem_call(combine_kernel, jax.ShapeDtypeStruct((ROWS, QCOLS), BF), 0, 4, nbytes=10**6)(
        own, back_left, back_right, back_far
    )
    left = shift(attended, "x", 1)
    right = shift(attended, "x", -1)
    other = shift(attended, "zl", 1)
    other_left = shift(other, "x", 1)
    other_right = shift(other, "x", -1)
    far_left = shift(jnp.concatenate([left[:half_rows], other_left[:half_rows]]), "x", 1)
    far_right = shift(jnp.concatenate([right[half_rows:], other_right[half_rows:]]), "x", -1)
    slots = jnp.concatenate([order, tp ^ order])
    return fetch_call(
        project_kernel,
        jax.ShapeDtypeStruct((ROWS, WIDTH), BF),
        4,
        9,
        (8, ROWS, QCOLS),
        (8, QCOLS, WIDTH),
        2 * ROWS * 8 * WIDTH * QCOLS,
    )(
        slots,
        mine,
        theirs,
        ups,
        ups_other,
        attended,
        left,
        far_left,
        right,
        other,
        other_left,
        far_right,
        other_right,
        columns,
    )


def solution(mesh):
    fine = Mesh(mesh.devices.reshape([SIZES[a] for a in AXES]), AXES)
    in_specs = (
        P(CTX, TP),
        P(TP),
        P(CTX, TP),
        P(CTX, TP),
        P(None, TP),
        P(TP, None),
        P(CTX, None, None),
        P(CTX, None, TP),
        P(CTX, TP, None),
        P(CTX, None, None),
        P(),
        P(),
    )
    return jax.shard_map(
        shards, mesh=fine, in_specs=in_specs, out_specs=P(CTX, TP), check_vma=False
    )
```

```python
import functools
import math

import jax
import jax.numpy as jnp
from jax import lax
from jax.experimental import pallas as pl
from jax.experimental.pallas import tpu as pltpu
from jax.sharding import Mesh
from jax.sharding import PartitionSpec as P

HS = 128
FTOK = 64
ROWS = 320
FRAMES_DEV = 5
WIDTH = 768
RANK = 64
HEADS_DEV = 3
QCOLS = HEADS_DEV * HS
CHUNK = 2 * ROWS
CHUNKS = 4
NEG = -1e30
PIECE = 96
EPS = 1e-6
AXES = ("zh", "y", "c", "zl", "x")
SIZES = {"zh": 4, "y": 4, "c": 2, "zl": 2, "x": 4}
CTX = ("zh", "y", "c")
TP = ("zl", "x")
EXP_SCALE = (HS ** (-0.5)) * math.log2(math.e)
BF = jnp.bfloat16
F32 = jnp.float32


def shift(v, axis, step):
    n = SIZES[axis]
    return lax.ppermute(v, axis, [(i, (i + step) % n) for i in range(n)])


def tp_source(a, d):
    return (lax.axis_index("zl") ^ a) * 4 + (lax.axis_index("x") - d) % 4


def vmem_call(body, out_shape, n_smem, n_vmem, scratch=(), flops=0, nbytes=0, mib=16, n_any=0):
    return pl.pallas_call(
        body,
        out_shape=out_shape,
        in_specs=[pl.BlockSpec(memory_space=pltpu.SMEM)] * n_smem
        + [pl.BlockSpec(memory_space=pltpu.VMEM)] * n_vmem
        + [pl.BlockSpec(memory_space=pl.ANY)] * n_any,
        scratch_shapes=list(scratch),
        cost_estimate=pl.CostEstimate(flops=flops, bytes_accessed=nbytes, transcendentals=0),
        compiler_params=pltpu.CompilerParams(vmem_limit_bytes=mib * 1024 * 1024),
    )


def tdot(a, b):
    return lax.dot_general(a, b, (((0,), (0,)), ((), ())), preferred_element_type=F32)


def norm_kernel(order_ref, gain_ref, *refs):
    parts, out_ref = refs[:8], refs[8]
    half = ROWS // 2

    def block(i):
        if i in (2, 6):
            rows = slice(0, half) if i == 2 else slice(half, ROWS)
            return jnp.concatenate([parts[2][rows, :], parts[6][rows, :]], axis=0)
        return parts[i][...]

    total = jnp.zeros((ROWS, HS), F32)
    for i in range(8):
        v = block(i).astype(F32)
        v = v * v
        for g in range(WIDTH // HS):
            total = total + v[:, g * HS : (g + 1) * HS]
    total = jnp.sum(total, axis=1, keepdims=True)
    inv = lax.rsqrt(total * (1.0 / (8 * WIDTH)) + EPS)
    for i in range(8):
        at = order_ref[i]
        gain = jnp.concatenate(
            [gain_ref[at, r : r + 1, :].astype(F32) for r in range(WIDTH // HS)], axis=1
        )
        out_ref[i] = (block(i).astype(F32) * inv * gain).astype(BF)


def query_kernel(
    order_ref, mine_ref, other_ref, up_ref, up_other_ref, x_ref, w_ref, out_ref, xs, ws, x_sems, w_sems
):
    copies_in = []
    for i in range(8):
        rows = pl.ds(pl.multiple_of(order_ref[i] * WIDTH, WIDTH), WIDTH)
        copies_in.append(
            (
                pltpu.make_async_copy(w_ref.at[rows, :], ws.at[i], w_sems.at[i]),
                pltpu.make_async_copy(x_ref.at[i], xs.at[i], x_sems.at[i]),
            )
        )
        for copy in copies_in[i]:
            copy.start()
    acc = jnp.zeros((ROWS, QCOLS), F32)
    up = jnp.concatenate([up_ref[:, :QCOLS], up_other_ref[:, :QCOLS]], axis=0)
    for i in range(8):
        at = order_ref[i]
        down = jnp.concatenate([mine_ref[at, :, :WIDTH], other_ref[at, :, :WIDTH]], axis=0)
        copies_in[i][0].wait()
        merged = (ws[i].astype(F32) + tdot(down, up)).astype(BF)
        copies_in[i][1].wait()
        acc = acc + jnp.dot(xs[i], merged, preferred_element_type=F32)
    out_ref[...] = acc.astype(BF)


def attention_kernel(n, qframe_ref, kframe_ref, vis_ref, *refs):
    q_refs = refs[:n]
    kv_ref = refs[n]
    o_refs = refs[n + 1 :]
    lane = lax.broadcasted_iota(jnp.int32, (ROWS, HS), 1)
    row = lax.broadcasted_iota(jnp.int32, (ROWS, HS), 0)

    def heads(b, first, chunks):
        width = chunks * CHUNK
        last = kframe_ref[chunks - 1] * FTOK
        limit = jnp.full((ROWS, HS), vis_ref[first] - last, jnp.int32)
        for f in range(1, FRAMES_DEV):
            limit = jnp.where(row >= f * FTOK, vis_ref[first + f] - last, limit)
        seen = jnp.concatenate([lane + g * HS for g in range(CHUNK // HS)], axis=1)
        seen = seen < jnp.concatenate([limit] * (CHUNK // HS), axis=1)

        def scores(h):
            cols = slice(h * HS, (h + 1) * HS)
            return lax.dot_general(
                q_refs[b][:, cols],
                kv_ref[:width, cols],
                (((1,), (1,)), ((), ())),
                preferred_element_type=F32,
            )

        s = scores(0)
        stats = jnp.zeros((ROWS, HS), F32)
        for h in range(HEADS_DEV):
            ahead = scores(h + 1) if h + 1 < HEADS_DEV else None
            tail = jnp.where(seen, s[:, width - CHUNK :], NEG)
            s = jnp.concatenate([s[:, : width - CHUNK], tail], axis=1) if chunks > 1 else tail
            top = jnp.broadcast_to(jnp.max(s, axis=1, keepdims=True), (ROWS, HS))
            p = jnp.exp2((s - jnp.concatenate([top] * (width // HS), axis=1)) * EXP_SCALE)
            lanes = p[:, :HS]
            for g in range(1, width // HS):
                lanes = lanes + p[:, g * HS : (g + 1) * HS]
            total = jnp.broadcast_to(jnp.sum(lanes, axis=1, keepdims=True), (ROWS, HS))
            acc = jnp.dot(
                p.astype(BF),
                kv_ref[:width, QCOLS + h * HS : QCOLS + (h + 1) * HS],
                preferred_element_type=F32,
            )
            has = top > 0.5 * NEG
            o_refs[b][:, h * HS : (h + 1) * HS] = jnp.where(has, acc / total, 0.0).astype(BF)
            level = jnp.where(has, top * EXP_SCALE + jnp.log2(total), NEG)
            high = level.astype(BF).astype(F32)
            mid = (level - high).astype(BF).astype(F32)
            low = level - high - mid
            stats = jnp.where(lane == 3 * h, high, stats)
            stats = jnp.where(lane == 3 * h + 1, mid, stats)
            stats = jnp.where(lane == 3 * h + 2, low, stats)
            s = ahead
        o_refs[b][:, QCOLS:] = stats.astype(BF)

    for b in range(n):
        first = qframe_ref[b]
        end = vis_ref[first + FRAMES_DEV - 1]
        some = jnp.int32(0)
        for j in range(CHUNKS):
            some = some + (kframe_ref[j] * FTOK < end).astype(jnp.int32)

        @pl.when(some == 0)
        def _(b=b):
            o_refs[b][:, :QCOLS] = jnp.zeros((ROWS, QCOLS), BF)
            blank = jnp.where((lane < 3 * HEADS_DEV) & (lane % 3 == 0), NEG, 0.0)
            o_refs[b][:, QCOLS:] = blank.astype(BF)

        for chunks in range(1, CHUNKS + 1):

            @pl.when(some == chunks)
            def _(b=b, first=first, chunks=chunks):
                heads(b, first, chunks)


def attention(queries, qframes, kframes, vis_end, kv):
    n = len(queries)
    return vmem_call(
        functools.partial(attention_kernel, n),
        [jax.ShapeDtypeStruct((ROWS, QCOLS + HS), BF)] * n,
        3,
        n + 1,
        flops=n * 8 * ROWS * QCOLS * CHUNK * CHUNKS,
        nbytes=CHUNKS * CHUNK * 2 * QCOLS * 2,
        mib=24,
    )(jnp.stack(qframes), kframes, vis_end, *queries, kv)


def combine_kernel(*refs):
    parts, out_ref = refs[:4], refs[4]
    stats = [p[:, QCOLS:].astype(F32) for p in parts]
    for h in range(HEADS_DEV):
        levels = []
        for s in stats:
            levels.append(
                s[:, 3 * h : 3 * h + 1] + s[:, 3 * h + 1 : 3 * h + 2] + s[:, 3 * h + 2 : 3 * h + 3]
            )
        top = functools.reduce(jnp.maximum, levels)
        shares = [jnp.exp2(v - top) for v in levels]
        total = shares[0] + shares[1] + shares[2] + shares[3]
        cols = slice(h * HS, (h + 1) * HS)
        acc = jnp.zeros((ROWS, HS), F32)
        for p, w in zip(parts, shares):
            acc = acc + p[:, cols].astype(F32) * w
        out_ref[:, cols] = (acc / total).astype(BF)


def project_kernel(order_ref, *refs):
    mine_ref, other_ref, up_ref, up_other_ref = refs[:4]
    parts, w_ref, out_ref, xs, ws, x_sems, w_sems = refs[4:12], *refs[12:]
    half = ROWS // 2
    waits = []
    for i in range(8):
        rows = pl.ds(pl.multiple_of(order_ref[8 + i] * QCOLS, QCOLS), QCOLS)
        mine = [pltpu.make_async_copy(w_ref.at[rows, :], ws.at[i], w_sems.at[i])]
        if i in (2, 6):
            src = slice(0, half) if i == 2 else slice(half, ROWS)
            for k, side in enumerate((2, 6)):
                dst = xs.at[i, k * half : (k + 1) * half, :]
                mine.append(
                    pltpu.make_async_copy(parts[side].at[src, :], dst, x_sems.at[i + 8 * k])
                )
        else:
            mine.append(pltpu.make_async_copy(parts[i], xs.at[i], x_sems.at[i]))
        for copy in mine:
            copy.start()
        waits.append(mine)
    acc = jnp.zeros((ROWS, WIDTH), F32)
    up = jnp.concatenate([up_ref[:, QCOLS:], up_other_ref[:, QCOLS:]], axis=0)
    cols = slice(WIDTH, WIDTH + QCOLS)
    for i in range(8):
        at = order_ref[i]
        down = jnp.concatenate([mine_ref[at, :, cols], other_ref[at, :, cols]], axis=0)
        for copy in waits[i]:
            copy.wait()
        merged = (ws[i].astype(F32) + tdot(down, up)).astype(BF)
        acc = acc + jnp.dot(xs[i], merged, preferred_element_type=F32)
    out_ref[...] = acc.astype(BF)


def fetch_call(body, out_shape, n_vmem, n_any, x_shape, w_shape, flops):
    return pl.pallas_call(
        body,
        out_shape=out_shape,
        in_specs=[pl.BlockSpec(memory_space=pltpu.SMEM)]
        + [pl.BlockSpec(memory_space=pltpu.VMEM)] * n_vmem
        + [pl.BlockSpec(memory_space=pl.ANY)] * n_any,
        out_specs=pl.BlockSpec(memory_space=pltpu.VMEM),
        scratch_shapes=[
            pltpu.VMEM(x_shape, BF),
            pltpu.VMEM(w_shape, BF),
            pltpu.SemaphoreType.DMA((16,)),
            pltpu.SemaphoreType.DMA((8,)),
        ],
        cost_estimate=pl.CostEstimate(flops=flops, bytes_accessed=10**7, transcendentals=0),
        compiler_params=pltpu.CompilerParams(vmem_limit_bytes=60 * 1024 * 1024),
    )


def cover_kernel(in_ref, out_ref):
    out_ref[...] = in_ref[...]


def cover(seed):
    return pl.pallas_call(
        cover_kernel,
        out_shape=jax.ShapeDtypeStruct(seed.shape, seed.dtype),
        cost_estimate=pl.CostEstimate(flops=3 * 10**10, bytes_accessed=10**8, transcendentals=0),
    )(seed)


def together(*values):
    return lax.optimization_barrier(values)


def after(value, *others):
    return lax.optimization_barrier((value,) + others)[0]


def prep_kernel(scal_ref, down_q_ref, down_o_ref, up_q_ref, up_o_ref, out_ref):
    start = 0
    for i, ref in ((0, down_q_ref), (2, down_o_ref), (1, up_q_ref), (3, up_o_ref)):
        width = ref.shape[1]
        mine = scal_ref[1 + i] == scal_ref[0]
        out_ref[:, start : start + width] = jnp.where(mine, ref[...].astype(F32), 0.0).astype(BF)
        start += width


def prepare(rank, tp, owners, down_q, down_o, up_q, up_o):
    scal = jnp.concatenate([rank[None], owners, tp[None]]).astype(jnp.int32)
    width = 2 * (WIDTH + QCOLS)
    return pl.pallas_call(
        prep_kernel,
        out_shape=jax.ShapeDtypeStruct((RANK, width), BF),
        grid_spec=pltpu.PrefetchScalarGridSpec(
            num_scalar_prefetch=1,
            grid=(1,),
            in_specs=[
                pl.BlockSpec((RANK, WIDTH), lambda i, sc: (0, sc[5])),
                pl.BlockSpec((RANK, QCOLS), lambda i, sc: (0, 0)),
                pl.BlockSpec((RANK, QCOLS), lambda i, sc: (0, 0)),
                pl.BlockSpec((RANK, WIDTH), lambda i, sc: (0, sc[5])),
            ],
            out_specs=pl.BlockSpec((RANK, width), lambda i, sc: (0, 0)),
        ),
        cost_estimate=pl.CostEstimate(flops=3 * 10**10, bytes_accessed=10**8, transcendentals=0),
        compiler_params=pltpu.CompilerParams(vmem_limit_bytes=60 * 1024 * 1024),
    )(scal, down_q, down_o, up_q, up_o)


def copies(piece, axis, n):
    everywhere = jnp.broadcast_to(piece[None], (n,) + piece.shape)
    return lax.all_to_all(everywhere, axis, 0, 0)


def many(piece, n):
    return jnp.broadcast_to(piece[None], (n,) + piece.shape)


def spread(pieces, axis):
    got = lax.all_to_all(pieces, axis, 0, 0)
    return got[0] + got[1] + got[2] + got[3]


def column_piece(weight, rank, tp):
    piece = lax.dynamic_slice(
        weight, ((rank % 4) * PIECE, (tp ^ (rank // 4)) * WIDTH), (PIECE, WIDTH)
    )
    return piece


def to_columns(piece):
    pairs = []
    for r in range(32):
        for t in range(8):
            pairs.append((r * 8 + t, r * 8 + (t ^ (r // 4))))
    return lax.ppermute(piece, AXES, pairs)


SHIFTS = [(a, d) for a in range(2) for d in range(4)]


def shards(
    tokens,
    norm_gain_vector,
    keys,
    values,
    query_frozen_weight,
    output_frozen_weight,
    query_update_first,
    query_update_second,
    output_update_first,
    output_update_second,
    owners,
    frame_block_number,
):
    zh, y, c = (lax.axis_index(a) for a in CTX)
    tp = lax.axis_index("zl") * 4 + lax.axis_index("x")
    rank = zh * 8 + y * 2 + c

    half = RANK // 2
    half_rows = ROWS // 2
    left = shift(tokens, "x", 1)
    right = shift(tokens, "x", -1)
    other = shift(tokens, "zl", 1)
    factors = prepare(
        rank,
        tp,
        owners,
        query_update_first[0].T,
        output_update_first[0].T,
        query_update_second[0],
        output_update_second[0],
    )
    factors = factors + shift(factors, "c", 1)
    part = many(lax.dynamic_slice_in_dim(factors, c * half, half, 0), 4)
    seed = jnp.zeros((8, HS), F32)
    kv = jnp.concatenate([keys, values], axis=1)
    gain = jnp.pad(norm_gain_vector.reshape(WIDTH // HS, HS), ((0, 16 - WIDTH // HS), (0, 0)))
    gain = copies(gain, TP, 8)
    left, right, other, part, seed, kv, gain = together(
        left, right, other, part, seed, kv, gain
    )

    kv = lax.all_gather(kv, ("zh", "c"), axis=0, tiled=True)
    other_left = shift(other, "x", 1)
    other_right = shift(other, "x", -1)
    part = many(spread(part, "zh"), 4)
    columns = column_piece(output_frozen_weight, rank, tp)
    seed = cover(seed)
    other_left, other_right, part, seed, columns = together(
        other_left, other_right, part, seed, columns
    )

    far_left = shift(jnp.concatenate([left[:half_rows], other_left[:half_rows]]), "x", 1)
    far_right = shift(jnp.concatenate([right[half_rows:], other_right[half_rows:]]), "x", -1)
    part = spread(part, "y")
    downs = many(part[:, : WIDTH + QCOLS], 8)
    ups = part[:, WIDTH + QCOLS :]
    seed = cover(seed)
    far_left, far_right, downs, ups, seed, columns = together(
        far_left, far_right, downs, ups, seed, columns
    )
    columns = to_columns(columns)

    order = jnp.stack([tp_source(a, d) for a, d in SHIFTS])
    mine = lax.all_to_all(downs, TP, 0, 0)
    ups_other = shift(ups, "c", 1)
    normed = vmem_call(
        norm_kernel,
        jax.ShapeDtypeStruct((8, ROWS, WIDTH), BF),
        1,
        9,
        flops=10**10,
        nbytes=4 * 10**7,
        mib=24,
    )(order, gain, tokens, left, far_left, right, other, other_left, far_right, other_right)
    mine, normed, columns = together(mine, normed, columns)
    columns = lax.all_gather(columns, CTX, axis=0, tiled=True)
    theirs = shift(mine, "c", 1)
    queries = fetch_call(
        query_kernel,
        jax.ShapeDtypeStruct((ROWS, QCOLS), BF),
        4,
        2,
        (8, ROWS, WIDTH),
        (8, WIDTH, QCOLS),
        2 * ROWS * 8 * WIDTH * QCOLS + 2 * 8 * WIDTH * RANK * QCOLS,
    )(order, mine, theirs, ups, ups_other, normed, query_frozen_weight)

    counts = jnp.sum(
        (frame_block_number[None, :] <= frame_block_number[:, None]).astype(jnp.int32), axis=1
    )
    vis_end = counts * FTOK
    kframes = (jnp.arange(CHUNKS, dtype=jnp.int32) * 8 + y * 2) * FRAMES_DEV

    def frames_of(step):
        return (zh * 8 + ((y - step) % 4) * 2 + c) * FRAMES_DEV

    q_left = shift(queries, "y", 1)
    q_right = shift(queries, "y", -1)
    q_far = shift(queries, "y", 2)
    (own,) = attention([queries], [frames_of(0)], kframes, vis_end, kv)
    q_left, q_right, q_far, own = together(q_left, q_right, q_far, own)
    (left,) = attention([q_left], [frames_of(1)], kframes, vis_end, kv)
    back_left = shift(left, "y", -1)
    (right,) = attention([q_right], [frames_of(-1)], kframes, vis_end, kv)
    back_right = shift(right, "y", 1)
    (far,) = attention([q_far], [frames_of(2)], kframes, vis_end, kv)
    back_far = shift(far, "y", 2)

    attended = vmem_call(combine_kernel, jax.ShapeDtypeStruct((ROWS, QCOLS), BF), 0, 4, nbytes=10**6)(
        own, back_left, back_right, back_far
    )
    left = shift(attended, "x", 1)
    right = shift(attended, "x", -1)
    other = shift(attended, "zl", 1)
    other_left = shift(other, "x", 1)
    other_right = shift(other, "x", -1)
    far_left = shift(jnp.concatenate([left[:half_rows], other_left[:half_rows]]), "x", 1)
    far_right = shift(jnp.concatenate([right[half_rows:], other_right[half_rows:]]), "x", -1)
    slots = jnp.concatenate([order, tp ^ order])
    return fetch_call(
        project_kernel,
        jax.ShapeDtypeStruct((ROWS, WIDTH), BF),
        4,
        9,
        (8, ROWS, QCOLS),
        (8, QCOLS, WIDTH),
        2 * ROWS * 8 * WIDTH * QCOLS,
    )(
        slots,
        mine,
        theirs,
        ups,
        ups_other,
        attended,
        left,
        far_left,
        right,
        other,
        other_left,
        far_right,
        other_right,
        columns,
    )


def solution(mesh):
    fine = Mesh(mesh.devices.reshape([SIZES[a] for a in AXES]), AXES)
    in_specs = (
        P(CTX, TP),
        P(TP),
        P(CTX, TP),
        P(CTX, TP),
        P(None, TP),
        P(TP, None),
        P(CTX, None, None),
        P(CTX, None, TP),
        P(CTX, TP, None),
        P(CTX, None, None),
        P(),
        P(),
    )
    return jax.shard_map(
        shards, mesh=fine, in_specs=in_specs, out_specs=P(CTX, TP), check_vma=False
    )
```

```python
import functools
import math

import jax
import jax.numpy as jnp
from jax import lax
from jax.experimental import pallas as pl
from jax.experimental.pallas import tpu as pltpu
from jax.sharding import Mesh
from jax.sharding import PartitionSpec as P

HS = 128
FTOK = 64
ROWS = 320
FRAMES_DEV = 5
WIDTH = 768
RANK = 64
HEADS_DEV = 3
QCOLS = HEADS_DEV * HS
CHUNK = 2 * ROWS
CHUNKS = 4
NEG = -1e30
PIECE = 96
EPS = 1e-6
AXES = ("zh", "y", "c", "zl", "x")
SIZES = {"zh": 4, "y": 4, "c": 2, "zl": 2, "x": 4}
CTX = ("zh", "y", "c")
TP = ("zl", "x")
EXP_SCALE = (HS ** (-0.5)) * math.log2(math.e)
BF = jnp.bfloat16
F32 = jnp.float32


def shift(v, axis, step):
    n = SIZES[axis]
    return lax.ppermute(v, axis, [(i, (i + step) % n) for i in range(n)])


def tp_source(a, d):
    return (lax.axis_index("zl") ^ a) * 4 + (lax.axis_index("x") - d) % 4


def vmem_call(body, out_shape, n_smem, n_vmem, scratch=(), flops=0, nbytes=0, mib=16, n_any=0):
    return pl.pallas_call(
        body,
        out_shape=out_shape,
        in_specs=[pl.BlockSpec(memory_space=pltpu.SMEM)] * n_smem
        + [pl.BlockSpec(memory_space=pltpu.VMEM)] * n_vmem
        + [pl.BlockSpec(memory_space=pl.ANY)] * n_any,
        scratch_shapes=list(scratch),
        cost_estimate=pl.CostEstimate(flops=flops, bytes_accessed=nbytes, transcendentals=0),
        compiler_params=pltpu.CompilerParams(vmem_limit_bytes=mib * 1024 * 1024),
    )


def tdot(a, b):
    return lax.dot_general(a, b, (((0,), (0,)), ((), ())), preferred_element_type=F32)


def norm_kernel(order_ref, gain_ref, *refs):
    parts, out_ref = refs[:8], refs[8]
    half = ROWS // 2

    def block(i):
        if i in (2, 6):
            rows = slice(0, half) if i == 2 else slice(half, ROWS)
            return jnp.concatenate([parts[2][rows, :], parts[6][rows, :]], axis=0)
        return parts[i][...]

    total = jnp.zeros((ROWS, HS), F32)
    for i in range(8):
        v = block(i).astype(F32)
        v = v * v
        for g in range(WIDTH // HS):
            total = total + v[:, g * HS : (g + 1) * HS]
    total = jnp.sum(total, axis=1, keepdims=True)
    inv = lax.rsqrt(total * (1.0 / (8 * WIDTH)) + EPS)
    for i in range(8):
        at = order_ref[i]
        gain = jnp.concatenate(
            [gain_ref[at, r : r + 1, :].astype(F32) for r in range(WIDTH // HS)], axis=1
        )
        out_ref[i] = (block(i).astype(F32) * inv * gain).astype(BF)


def query_kernel(
    order_ref, mine_ref, other_ref, up_ref, up_other_ref, x_ref, w_ref, out_ref, xs, ws, x_sems, w_sems
):
    copies_in = []
    for i in range(8):
        rows = pl.ds(pl.multiple_of(order_ref[i] * WIDTH, WIDTH), WIDTH)
        copies_in.append(
            (
                pltpu.make_async_copy(w_ref.at[rows, :], ws.at[i], w_sems.at[i]),
                pltpu.make_async_copy(x_ref.at[i], xs.at[i], x_sems.at[i]),
            )
        )
        for copy in copies_in[i]:
            copy.start()
    acc = jnp.zeros((ROWS, QCOLS), F32)
    up = jnp.concatenate([up_ref[:, :QCOLS], up_other_ref[:, :QCOLS]], axis=0)
    for i in range(8):
        at = order_ref[i]
        down = jnp.concatenate([mine_ref[at, :, :WIDTH], other_ref[at, :, :WIDTH]], axis=0)
        copies_in[i][0].wait()
        merged = (ws[i].astype(F32) + tdot(down, up)).astype(BF)
        copies_in[i][1].wait()
        acc = acc + jnp.dot(xs[i], merged, preferred_element_type=F32)
    out_ref[...] = acc.astype(BF)


def attention_kernel(n, qframe_ref, kframe_ref, vis_ref, *refs):
    q_refs = refs[:n]
    kv_ref = refs[n]
    o_refs = refs[n + 1 :]
    lane = lax.broadcasted_iota(jnp.int32, (ROWS, HS), 1)
    row = lax.broadcasted_iota(jnp.int32, (ROWS, HS), 0)

    def heads(b, first, chunks):
        width = chunks * CHUNK
        last = kframe_ref[chunks - 1] * FTOK
        limit = jnp.full((ROWS, HS), vis_ref[first] - last, jnp.int32)
        for f in range(1, FRAMES_DEV):
            limit = jnp.where(row >= f * FTOK, vis_ref[first + f] - last, limit)
        seen = jnp.concatenate([lane + g * HS for g in range(CHUNK // HS)], axis=1)
        seen = seen < jnp.concatenate([limit] * (CHUNK // HS), axis=1)

        def scores(h):
            cols = slice(h * HS, (h + 1) * HS)
            return lax.dot_general(
                q_refs[b][:, cols],
                kv_ref[:width, cols],
                (((1,), (1,)), ((), ())),
                preferred_element_type=F32,
            )

        s = scores(0)
        stats = jnp.zeros((ROWS, HS), F32)
        for h in range(HEADS_DEV):
            ahead = scores(h + 1) if h + 1 < HEADS_DEV else None
            tail = jnp.where(seen, s[:, width - CHUNK :], NEG)
            s = jnp.concatenate([s[:, : width - CHUNK], tail], axis=1) if chunks > 1 else tail
            top = jnp.broadcast_to(jnp.max(s, axis=1, keepdims=True), (ROWS, HS))
            p = jnp.exp2((s - jnp.concatenate([top] * (width // HS), axis=1)) * EXP_SCALE)
            lanes = p[:, :HS]
            for g in range(1, width // HS):
                lanes = lanes + p[:, g * HS : (g + 1) * HS]
            total = jnp.broadcast_to(jnp.sum(lanes, axis=1, keepdims=True), (ROWS, HS))
            acc = jnp.dot(
                p.astype(BF),
                kv_ref[:width, QCOLS + h * HS : QCOLS + (h + 1) * HS],
                preferred_element_type=F32,
            )
            has = top > 0.5 * NEG
            o_refs[b][:, h * HS : (h + 1) * HS] = jnp.where(has, acc / total, 0.0).astype(BF)
            level = jnp.where(has, top * EXP_SCALE + jnp.log2(total), NEG)
            high = level.astype(BF).astype(F32)
            mid = (level - high).astype(BF).astype(F32)
            low = level - high - mid
            stats = jnp.where(lane == 3 * h, high, stats)
            stats = jnp.where(lane == 3 * h + 1, mid, stats)
            stats = jnp.where(lane == 3 * h + 2, low, stats)
            s = ahead
        o_refs[b][:, QCOLS:] = stats.astype(BF)

    for b in range(n):
        first = qframe_ref[b]
        end = vis_ref[first + FRAMES_DEV - 1]
        some = jnp.int32(0)
        for j in range(CHUNKS):
            some = some + (kframe_ref[j] * FTOK < end).astype(jnp.int32)

        @pl.when(some == 0)
        def _(b=b):
            o_refs[b][:, :QCOLS] = jnp.zeros((ROWS, QCOLS), BF)
            blank = jnp.where((lane < 3 * HEADS_DEV) & (lane % 3 == 0), NEG, 0.0)
            o_refs[b][:, QCOLS:] = blank.astype(BF)

        for chunks in range(1, CHUNKS + 1):

            @pl.when(some == chunks)
            def _(b=b, first=first, chunks=chunks):
                heads(b, first, chunks)


def attention(queries, qframes, kframes, vis_end, kv):
    n = len(queries)
    return vmem_call(
        functools.partial(attention_kernel, n),
        [jax.ShapeDtypeStruct((ROWS, QCOLS + HS), BF)] * n,
        3,
        n + 1,
        flops=n * 8 * ROWS * QCOLS * CHUNK * CHUNKS,
        nbytes=CHUNKS * CHUNK * 2 * QCOLS * 2,
        mib=24,
    )(jnp.stack(qframes), kframes, vis_end, *queries, kv)


def combine_kernel(*refs):
    parts, out_ref = refs[:4], refs[4]
    stats = [p[:, QCOLS:].astype(F32) for p in parts]
    for h in range(HEADS_DEV):
        levels = []
        for s in stats:
            levels.append(
                s[:, 3 * h : 3 * h + 1] + s[:, 3 * h + 1 : 3 * h + 2] + s[:, 3 * h + 2 : 3 * h + 3]
            )
        top = functools.reduce(jnp.maximum, levels)
        shares = [jnp.exp2(v - top) for v in levels]
        total = shares[0] + shares[1] + shares[2] + shares[3]
        cols = slice(h * HS, (h + 1) * HS)
        acc = jnp.zeros((ROWS, HS), F32)
        for p, w in zip(parts, shares):
            acc = acc + p[:, cols].astype(F32) * w
        out_ref[:, cols] = (acc / total).astype(BF)


def project_kernel(order_ref, *refs):
    mine_ref, other_ref, up_ref, up_other_ref = refs[:4]
    parts, w_ref, out_ref, xs, ws, x_sems, w_sems = refs[4:12], *refs[12:]
    half = ROWS // 2
    waits = []
    for i in range(8):
        rows = pl.ds(pl.multiple_of(order_ref[8 + i] * QCOLS, QCOLS), QCOLS)
        mine = [pltpu.make_async_copy(w_ref.at[rows, :], ws.at[i], w_sems.at[i])]
        if i in (2, 6):
            src = slice(0, half) if i == 2 else slice(half, ROWS)
            for k, side in enumerate((2, 6)):
                dst = xs.at[i, k * half : (k + 1) * half, :]
                mine.append(
                    pltpu.make_async_copy(parts[side].at[src, :], dst, x_sems.at[i + 8 * k])
                )
        else:
            mine.append(pltpu.make_async_copy(parts[i], xs.at[i], x_sems.at[i]))
        for copy in mine:
            copy.start()
        waits.append(mine)
    acc = jnp.zeros((ROWS, WIDTH), F32)
    up = jnp.concatenate([up_ref[:, QCOLS:], up_other_ref[:, QCOLS:]], axis=0)
    cols = slice(WIDTH, WIDTH + QCOLS)
    for i in range(8):
        at = order_ref[i]
        down = jnp.concatenate([mine_ref[at, :, cols], other_ref[at, :, cols]], axis=0)
        for copy in waits[i]:
            copy.wait()
        merged = (ws[i].astype(F32) + tdot(down, up)).astype(BF)
        acc = acc + jnp.dot(xs[i], merged, preferred_element_type=F32)
    out_ref[...] = acc.astype(BF)


def fetch_call(body, out_shape, n_vmem, n_any, x_shape, w_shape, flops):
    return pl.pallas_call(
        body,
        out_shape=out_shape,
        in_specs=[pl.BlockSpec(memory_space=pltpu.SMEM)]
        + [pl.BlockSpec(memory_space=pltpu.VMEM)] * n_vmem
        + [pl.BlockSpec(memory_space=pl.ANY)] * n_any,
        out_specs=pl.BlockSpec(memory_space=pltpu.VMEM),
        scratch_shapes=[
            pltpu.VMEM(x_shape, BF),
            pltpu.VMEM(w_shape, BF),
            pltpu.SemaphoreType.DMA((16,)),
            pltpu.SemaphoreType.DMA((8,)),
        ],
        cost_estimate=pl.CostEstimate(flops=flops, bytes_accessed=10**7, transcendentals=0),
        compiler_params=pltpu.CompilerParams(vmem_limit_bytes=60 * 1024 * 1024),
    )


def cover_kernel(in_ref, out_ref):
    out_ref[...] = in_ref[...]


def cover(seed):
    return pl.pallas_call(
        cover_kernel,
        out_shape=jax.ShapeDtypeStruct(seed.shape, seed.dtype),
        cost_estimate=pl.CostEstimate(flops=3 * 10**10, bytes_accessed=10**8, transcendentals=0),
    )(seed)


def together(*values):
    return lax.optimization_barrier(values)


def after(value, *others):
    return lax.optimization_barrier((value,) + others)[0]


def prep_kernel(scal_ref, down_q_ref, down_o_ref, up_q_ref, up_o_ref, out_ref):
    start = 0
    for i, ref in ((0, down_q_ref), (2, down_o_ref), (1, up_q_ref), (3, up_o_ref)):
        width = ref.shape[1]
        mine = scal_ref[1 + i] == scal_ref[0]
        out_ref[:, start : start + width] = jnp.where(mine, ref[...].astype(F32), 0.0).astype(BF)
        start += width


def prepare(rank, tp, owners, down_q, down_o, up_q, up_o):
    scal = jnp.concatenate([rank[None], owners, tp[None]]).astype(jnp.int32)
    width = 2 * (WIDTH + QCOLS)
    return pl.pallas_call(
        prep_kernel,
        out_shape=jax.ShapeDtypeStruct((RANK, width), BF),
        grid_spec=pltpu.PrefetchScalarGridSpec(
            num_scalar_prefetch=1,
            grid=(1,),
            in_specs=[
                pl.BlockSpec((RANK, WIDTH), lambda i, sc: (0, sc[5])),
                pl.BlockSpec((RANK, QCOLS), lambda i, sc: (0, 0)),
                pl.BlockSpec((RANK, QCOLS), lambda i, sc: (0, 0)),
                pl.BlockSpec((RANK, WIDTH), lambda i, sc: (0, sc[5])),
            ],
            out_specs=pl.BlockSpec((RANK, width), lambda i, sc: (0, 0)),
        ),
        cost_estimate=pl.CostEstimate(flops=3 * 10**10, bytes_accessed=10**8, transcendentals=0),
        compiler_params=pltpu.CompilerParams(vmem_limit_bytes=60 * 1024 * 1024),
    )(scal, down_q, down_o, up_q, up_o)


def copies(piece, axis, n):
    everywhere = jnp.broadcast_to(piece[None], (n,) + piece.shape)
    return lax.all_to_all(everywhere, axis, 0, 0)


def spread(part, axis):
    got = copies(part, axis, SIZES[axis])
    return got[0] + got[1] + got[2] + got[3]


def column_piece(weight, rank, tp):
    piece = lax.dynamic_slice(
        weight, ((rank % 4) * PIECE, (tp ^ (rank // 4)) * WIDTH), (PIECE, WIDTH)
    )
    return piece


def to_columns(piece):
    pairs = []
    for r in range(32):
        for t in range(8):
            pairs.append((r * 8 + t, r * 8 + (t ^ (r // 4))))
    return lax.ppermute(piece, AXES, pairs)


SHIFTS = [(a, d) for a in range(2) for d in range(4)]


def shards(
    tokens,
    norm_gain_vector,
    keys,
    values,
    query_frozen_weight,
    output_frozen_weight,
    query_update_first,
    query_update_second,
    output_update_first,
    output_update_second,
    owners,
    frame_block_number,
):
    zh, y, c = (lax.axis_index(a) for a in CTX)
    tp = lax.axis_index("zl") * 4 + lax.axis_index("x")
    rank = zh * 8 + y * 2 + c

    half = RANK // 2
    half_rows = ROWS // 2
    left = shift(tokens, "x", 1)
    right = shift(tokens, "x", -1)
    other = shift(tokens, "zl", 1)
    factors = prepare(
        rank,
        tp,
        owners,
        query_update_first[0].T,
        output_update_first[0].T,
        query_update_second[0],
        output_update_second[0],
    )
    factors = factors + shift(factors, "c", 1)
    part = lax.dynamic_slice_in_dim(factors, c * half, half, 0)
    seed = jnp.zeros((8, HS), F32)
    kv = jnp.concatenate([keys, values], axis=1)
    gain = jnp.pad(norm_gain_vector.reshape(WIDTH // HS, HS), ((0, 16 - WIDTH // HS), (0, 0)))
    gain = copies(gain, TP, 8)
    left, right, other, part, seed, kv, gain = together(
        left, right, other, part, seed, kv, gain
    )

    kv = lax.all_gather(kv, ("zh", "c"), axis=0, tiled=True)
    other_left = shift(other, "x", 1)
    other_right = shift(other, "x", -1)
    part = spread(part, "zh")
    columns = column_piece(output_frozen_weight, rank, tp)
    seed = cover(seed)
    other_left, other_right, part, seed, columns = together(
        other_left, other_right, part, seed, columns
    )

    far_left = shift(jnp.concatenate([left[:half_rows], other_left[:half_rows]]), "x", 1)
    far_right = shift(jnp.concatenate([right[half_rows:], other_right[half_rows:]]), "x", -1)
    part = spread(part, "y")
    seed = cover(seed)
    far_left, far_right, part, seed = together(far_left, far_right, part, seed)
    columns = to_columns(after(columns, far_left))

    order = jnp.stack([tp_source(a, d) for a, d in SHIFTS])
    mine = copies(part[:, : WIDTH + QCOLS], TP, 8)
    ups = part[:, WIDTH + QCOLS :]
    ups_other = shift(ups, "c", 1)
    normed = vmem_call(
        norm_kernel,
        jax.ShapeDtypeStruct((8, ROWS, WIDTH), BF),
        1,
        9,
        flops=10**10,
        nbytes=4 * 10**7,
        mib=24,
    )(order, gain, tokens, left, far_left, right, other, other_left, far_right, other_right)
    mine, normed, columns = together(mine, normed, columns)
    columns = lax.all_gather(columns, CTX, axis=0, tiled=True)
    theirs = shift(mine, "c", 1)
    queries = fetch_call(
        query_kernel,
        jax.ShapeDtypeStruct((ROWS, QCOLS), BF),
        4,
        2,
        (8, ROWS, WIDTH),
        (8, WIDTH, QCOLS),
        2 * ROWS * 8 * WIDTH * QCOLS + 2 * 8 * WIDTH * RANK * QCOLS,
    )(order, mine, theirs, ups, ups_other, normed, query_frozen_weight)

    counts = jnp.sum(
        (frame_block_number[None, :] <= frame_block_number[:, None]).astype(jnp.int32), axis=1
    )
    vis_end = counts * FTOK
    kframes = (jnp.arange(CHUNKS, dtype=jnp.int32) * 8 + y * 2) * FRAMES_DEV

    def frames_of(step):
        return (zh * 8 + ((y - step) % 4) * 2 + c) * FRAMES_DEV

    q_left = shift(queries, "y", 1)
    q_right = shift(queries, "y", -1)
    q_far = shift(queries, "y", 2)
    (own,) = attention([queries], [frames_of(0)], kframes, vis_end, kv)
    q_left, q_right, q_far, own = together(q_left, q_right, q_far, own)
    (left,) = attention([q_left], [frames_of(1)], kframes, vis_end, kv)
    back_left = shift(left, "y", -1)
    (right,) = attention([q_right], [frames_of(-1)], kframes, vis_end, kv)
    back_right = shift(right, "y", 1)
    (far,) = attention([q_far], [frames_of(2)], kframes, vis_end, kv)
    back_far = shift(far, "y", 2)

    attended = vmem_call(combine_kernel, jax.ShapeDtypeStruct((ROWS, QCOLS), BF), 0, 4, nbytes=10**6)(
        own, back_left, back_right, back_far
    )
    left = shift(attended, "x", 1)
    right = shift(attended, "x", -1)
    other = shift(attended, "zl", 1)
    other_left = shift(other, "x", 1)
    other_right = shift(other, "x", -1)
    far_left = shift(jnp.concatenate([left[:half_rows], other_left[:half_rows]]), "x", 1)
    far_right = shift(jnp.concatenate([right[half_rows:], other_right[half_rows:]]), "x", -1)
    slots = jnp.concatenate([order, tp ^ order])
    return fetch_call(
        project_kernel,
        jax.ShapeDtypeStruct((ROWS, WIDTH), BF),
        4,
        9,
        (8, ROWS, QCOLS),
        (8, QCOLS, WIDTH),
        2 * ROWS * 8 * WIDTH * QCOLS,
    )(
        slots,
        mine,
        theirs,
        ups,
        ups_other,
        attended,
        left,
        far_left,
        right,
        other,
        other_left,
        far_right,
        other_right,
        columns,
    )


def solution(mesh):
    fine = Mesh(mesh.devices.reshape([SIZES[a] for a in AXES]), AXES)
    in_specs = (
        P(CTX, TP),
        P(TP),
        P(CTX, TP),
        P(CTX, TP),
        P(None, TP),
        P(TP, None),
        P(CTX, None, None),
        P(CTX, None, TP),
        P(CTX, TP, None),
        P(CTX, None, None),
        P(),
        P(),
    )
    return jax.shard_map(
        shards, mesh=fine, in_specs=in_specs, out_specs=P(CTX, TP), check_vma=False
    )
```
